32 devices in a mesh: groups: 2 (over y), blk: 4 (over z), split: 2 (over x), sub: 2 (over core).
Axes of the slice: x: 2, y: 2, z: 4, core: 2. Of those that a mesh axis runs over, the one named last changes fastest.
Arguments:
- attention_output_rows: bfloat16 [1024, 8192], P(('groups', 'blk'), 'split'), parts along dimension 0, may hold values from -6 to 6
- residual: bfloat16 [1024, 8192], P(('groups', 'split'), ('blk', 'sub')), parts along dimension 0, may hold values from -6 to 6
- output_projection_weight: bfloat16 [8192, 8192], P('split', ('blk', 'sub')), may hold values from -0.0625 to 0.0625
- down_adapter_bank: bfloat16 [4, 64, 8192], P('blk', None, 'split'), may hold values from -0.0625 to 0.0625
- up_adapter_bank: bfloat16 [4, 64, 8192], P('split', None, ('blk', 'sub')), may hold values from -0.75 to 0.75
- rollout_row_tenant: int32 [1024], P('groups'), parts along dimension 0, may hold values from 0 to 3, as said below
- tenant_bank_entry: int32 [4], replicated, may hold values from 0 to 3, each once
- tenant_live_rank: int32 [4], replicated, may hold values from 16 to 64, as said below
Outputs:
- layer_out: bfloat16 [1024, 8192], P(('groups', 'split'), ('blk', 'sub')), parts along dimension 0
The draws below stay inside these ranges and needn't reach their ends.
There are 2 independent parts, one for each index of `groups`. The reference program is written for one: setup_inputs(seed, part) draws one part's arguments, and reference() takes and returns one part's arrays. A program takes and returns all parts, laid end to end along the dimension named above; an argument that names none is the same for every part. Nothing has to cross between parts.
Inputs may be any that keep to these rules, and one draw needn't show every extreme that they name: `rollout_row_tenant`: every tenant owns at least one row of every part. `tenant_live_rank`: some tenant has the full rank 64.
All inputs are finite; a program needn't handle non-finite values.
Results may differ from the reference program's by a relative error of at most 0.0038.
Values may be sent and summed in bfloat16 or wider, within the bound.
No kernel may reach another device: no remote copies, remote signals or barrier semaphores. Data moves between devices by JAX's collectives and lax.ppermute only.
A program may use at most 64 MiB of HBM per device.

```python
import jax
import jax.numpy as jnp

MODEL_WIDTH = 8192
PADDED_RANK = 64
TOKENS = 512
TENANT_TOTAL = 4


def draw_rollout_row_tenant(key, part):
    first_key, second_key, order_key, mix_key = jax.random.split(jax.random.fold_in(key, 11), 4)
    first = jax.random.randint(first_key, (TOKENS,), 0, TENANT_TOTAL)
    second = jax.random.randint(second_key, (TOKENS,), 0, TENANT_TOTAL)
    skewed = jnp.minimum(first, second)
    order = jax.random.permutation(order_key, TENANT_TOTAL)
    tenant_ids = order[skewed].astype(jnp.int32)
    tenant_ids = tenant_ids.at[:TENANT_TOTAL].set(jnp.arange(TENANT_TOTAL, dtype=jnp.int32))
    return jax.random.permutation(mix_key, tenant_ids).astype(jnp.int32)


def draw_tenant_live_rank(key, part):
    value_key, place_key = jax.random.split(jax.random.fold_in(key, 23), 2)
    ranks = jax.random.randint(value_key, (TENANT_TOTAL,), PADDED_RANK // 4, PADDED_RANK + 1)
    position = jax.random.randint(place_key, (), 0, TENANT_TOTAL)
    return ranks.at[position].set(PADDED_RANK).astype(jnp.int32)


def levels(own_key, extent, shards, smallest, largest):
    loudness = 1.0
    for dim, blocks in shards:
        heights = jax.random.uniform(jax.random.fold_in(jax.random.fold_in(own_key, 6), dim), (blocks,), jnp.float32, smallest / len(shards), largest / len(shards))
        loudness = loudness * jnp.repeat(jnp.exp(heights), extent[dim] // blocks).reshape((-1,) + (1,) * (len(extent) - 1 - dim))
    return loudness


def noise(key, dims, width, reach, pieces=(), held_as=jnp.bfloat16):
    values = width * jax.random.normal(key, dims, jnp.float32)
    if pieces:
        values = values * levels(key, dims, pieces, -0.22, 0.18)
    return jnp.clip(values, -reach, reach).astype(held_as)


def setup_inputs(seed: int = 0, part: int = 0) -> dict:
    keys = jax.random.split(jax.random.key(seed), 9)
    part_keys = jax.random.split(jax.random.fold_in(keys[8], part), 9)
    return {
        "attention_output_rows": noise(part_keys[0], (TOKENS, MODEL_WIDTH), 1.0, 6.0, ((0, 4), (1, 2))),
        "residual": noise(part_keys[1], (TOKENS, MODEL_WIDTH), 1.0, 6.0, ((0, 2), (1, 8))),
        "output_projection_weight": noise(keys[2], (MODEL_WIDTH, MODEL_WIDTH), MODEL_WIDTH ** -0.5, 0.0625, ((0, 2), (1, 8))),
        "down_adapter_bank": noise(keys[3], (TENANT_TOTAL, PADDED_RANK, MODEL_WIDTH), MODEL_WIDTH ** -0.5, 0.0625, ((0, 4), (2, 2))),
        "up_adapter_bank": noise(keys[4], (TENANT_TOTAL, PADDED_RANK, MODEL_WIDTH), PADDED_RANK ** -0.5, 0.75, ((0, 2), (2, 8))),
        "rollout_row_tenant": draw_rollout_row_tenant(jax.random.fold_in(jax.random.fold_in(keys[8], part), 71), part),
        "tenant_bank_entry": jax.random.permutation(keys[6], TENANT_TOTAL).astype(jnp.int32),
        "tenant_live_rank": draw_tenant_live_rank(jax.random.fold_in(keys[8], 71), part),
    }


def reference(attention_output_rows, residual, output_projection_weight, down_adapter_bank, up_adapter_bank, rollout_row_tenant, tenant_bank_entry, tenant_live_rank):
    frozen_output_term = jnp.dot(attention_output_rows, output_projection_weight, preferred_element_type=jnp.float32)
    slot_row = tenant_bank_entry[rollout_row_tenant]
    rank_row = tenant_live_rank[rollout_row_tenant]
    reduced_rank_rows = jnp.dot(attention_output_rows, down_adapter_bank.reshape(TENANT_TOTAL * PADDED_RANK, MODEL_WIDTH).T, preferred_element_type=jnp.float32)
    low_rank = jnp.take_along_axis(reduced_rank_rows.reshape(TOKENS, TENANT_TOTAL, PADDED_RANK), slot_row[:, None, None], axis=1)[:, 0, :]
    kept_mask = jnp.arange(PADDED_RANK)[None, :] < rank_row[:, None]
    scaling = PADDED_RANK / rank_row.astype(jnp.float32)
    low_scaled = jnp.where(kept_mask, low_rank * scaling[:, None], 0.0).astype(jnp.bfloat16)
    slot_hot = slot_row[:, None] == jnp.arange(TENANT_TOTAL)[None, :]
    rank_expanded_rows = jnp.where(slot_hot[:, :, None], low_scaled[:, None, :], jnp.zeros((), jnp.bfloat16)).reshape(TOKENS, TENANT_TOTAL * PADDED_RANK)
    adapter_output_term = jnp.dot(rank_expanded_rows, up_adapter_bank.reshape(TENANT_TOTAL * PADDED_RANK, MODEL_WIDTH), preferred_element_type=jnp.float32)
    return (residual.astype(jnp.float32) + frozen_output_term + adapter_output_term).astype(jnp.bfloat16)
```

```python
import jax
import jax.numpy as jnp
from jax import lax
from jax.sharding import PartitionSpec as P

F32 = jnp.float32
BF16 = jnp.bfloat16


def low_rank_weights(low, slot, live, slots, rank_width):
    kept = jnp.arange(rank_width, dtype=jnp.int32)[None, :] < live[:, None]
    scaling = rank_width / live.astype(F32)
    scaled = jnp.where(kept, low * scaling[:, None], jnp.zeros((), F32)).astype(BF16)
    hot = slot[:, None] == jnp.arange(slots, dtype=jnp.int32)[None, :]
    spread = jnp.where(hot[:, :, None], scaled[:, None, :], jnp.zeros((), BF16))
    return spread.reshape(low.shape[0], slots * rank_width)


def tables(tenant, entry, live):
    ids = jnp.arange(entry.shape[0], dtype=jnp.int32)
    hot = (tenant[:, None] == ids[None, :]).astype(jnp.int32)
    return jnp.sum(hot * entry[None, :], axis=1), jnp.sum(hot * live[None, :], axis=1)


def general(rows, residual, weight, down, up, tenant, entry, live):
    own = residual.shape[0]
    cols = weight.shape[1]
    width = down.shape[1]
    slots = entry.shape[0]
    slot_all, live_all = tables(tenant, entry, live)
    part = rows.shape[0] // lax.axis_size("sub")
    mine = lax.dynamic_slice_in_dim(rows, lax.axis_index("sub") * part, part, 0)
    halves = lax.all_gather(lax.all_gather(mine, "blk", axis=0), "sub", axis=1)
    full = halves.reshape(-1, rows.shape[1])
    base = jnp.dot(full, weight, preferred_element_type=F32)
    low = lax.dot_general(
        full, down.reshape(-1, down.shape[2]), (((1,), (1,)), ((), ())), preferred_element_type=F32
    )
    held = down.shape[0]
    places = lax.axis_index("blk") * held + jnp.arange(held, dtype=jnp.int32)
    here = slot_all[:, None] == places[None, :]
    low = jnp.sum(
        jnp.where(here[:, :, None], low.reshape(-1, held, width), jnp.zeros((), F32)), axis=1
    )
    low = lax.psum(lax.psum_scatter(low, "split", scatter_dimension=0, tiled=True), "blk")
    base = lax.psum_scatter(base, "split", scatter_dimension=0, tiled=True)
    start = lax.axis_index("split") * own
    spread = low_rank_weights(
        low,
        lax.dynamic_slice_in_dim(slot_all, start, own, 0),
        lax.dynamic_slice_in_dim(live_all, start, own, 0),
        slots,
        width,
    )
    ups = lax.all_gather(up, "split", axis=0, tiled=True).reshape(slots * width, cols)
    lora = jnp.dot(spread, ups, preferred_element_type=F32)
    return (residual.astype(F32) + base + lora).astype(BF16)


def line(rows, residual, weight, down, up, tenant, entry, live):
    z, x, c = lax.axis_index("blk"), lax.axis_index("split"), lax.axis_index("sub")
    own = residual.shape[0]
    cols = weight.shape[1]
    width = down.shape[1]
    slots = entry.shape[0]
    slot_all, live_all = tables(tenant, entry, live)
    start = x * own

    up_other = lax.ppermute(up, "split", [(0, 1), (1, 0)])
    ups = jnp.where(x == 0, jnp.concatenate([up, up_other]), jnp.concatenate([up_other, up]))
    ups = ups.reshape(slots * width, cols)

    half = rows.shape[0] // 2
    mine = lax.dynamic_slice_in_dim(rows, c * half, half, 0)
    end = (z == 0) | (z == 3)

    pieces = 2
    step = half // pieces
    near, third, fourth = [], [], []
    for p in range(pieces):
        piece = mine[p * step : (p + 1) * step]
        a = lax.ppermute(piece, "blk", [(0, 1), (1, 0), (2, 3), (3, 2)])
        b = lax.ppermute(piece, "blk", [(1, 2), (2, 1)])
        e = lax.ppermute(
            jnp.where(end, piece, b), "blk", [(0, 2), (3, 1), (1, 0), (2, 3)]
        )
        f = lax.ppermute(e, "blk", [(1, 0), (2, 3)])
        near.append(a)
        third.append(jnp.where(end, e, b))
        fourth.append(jnp.where(end, f, e))

    def both(piece):
        other = lax.ppermute(piece, "sub", [(0, 1), (1, 0)])
        return jnp.where(c == 0, jnp.concatenate([piece, other]), jnp.concatenate([other, piece]))

    def whole(parts):
        pairs = [both(part) for part in parts]
        return jnp.concatenate(
            [pair[:step] for pair in pairs] + [pair[step:] for pair in pairs]
        )

    down_map = down[0]

    def products(block):
        base = jnp.dot(block, weight, preferred_element_type=F32)
        low = lax.dot_general(block, down_map, (((1,), (1,)), ((), ())), preferred_element_type=F32)
        return base, low

    blocks = [rows, whole(near), whole(third), whole(fourth)]
    results = [products(block) for block in blocks]
    low_z = z >= 2
    odd = (z % 2) == 1

    def ordered(first, second, swap):
        return jnp.where(swap, jnp.concatenate([second, first]), jnp.concatenate([first, second]))

    early = ordered(results[0][0], results[1][0], odd)
    late = ordered(results[2][0], results[3][0], low_z)
    home = (z // 2) == x
    to_home = [(2 * k + 1 - k // 2, 2 * k + k // 2) for k in range(4)]
    to_away = [(b, a) for a, b in to_home]
    got_early = lax.ppermute(early.astype(BF16), ("blk", "split"), to_home)
    got_late = lax.ppermute(late.astype(BF16), ("blk", "split"), to_away)
    base = jnp.where(home, early, late) + jnp.where(home, got_early, got_late).astype(F32)

    low_early = ordered(results[0][1], results[1][1], odd)
    low_late = ordered(results[2][1], results[3][1], low_z)
    low_keep = jnp.where(home, low_early, low_late)
    low_send = jnp.where(home, low_late, low_early)
    low = low_keep + lax.ppermute(low_send, "split", [(0, 1), (1, 0)])
    slot = lax.dynamic_slice_in_dim(slot_all, start, own, 0)
    low = jnp.where((slot == z)[:, None], low, jnp.zeros((), F32))
    low = low + lax.ppermute(low, "blk", [(0, 1), (1, 0), (2, 3), (3, 2)])
    low = low + lax.ppermute(low, "blk", [(0, 2), (2, 0), (1, 3), (3, 1)])
    spread = low_rank_weights(
        low, slot, lax.dynamic_slice_in_dim(live_all, start, own, 0), slots, width
    )
    lora = jnp.dot(spread, ups, preferred_element_type=F32)
    return (residual.astype(F32) + base + lora).astype(BF16)


def shards(rows, residual, weight, down, up, tenant, entry, live):
    sizes = [lax.axis_size(name) for name in ("blk", "split", "sub")]
    plan = line if sizes == [4, 2, 2] and down.shape[0] == 1 else general
    return plan(rows, residual, weight, down, up, tenant, entry, live)


def solution(mesh):
    in_specs = (
        P(("groups", "blk"), "split"),
        P(("groups", "split"), ("blk", "sub")),
        P("split", ("blk", "sub")),
        P("blk", None, "split"),
        P("split", None, ("blk", "sub")),
        P("groups"),
        P(),
        P(),
    )
    out_specs = P(("groups", "split"), ("blk", "sub"))
    return jax.shard_map(shards, mesh=mesh, in_specs=in_specs, out_specs=out_specs, check_vma=False)
```

```python
import jax
import jax.numpy as jnp
from jax import lax
from jax.experimental import pallas as pl
from jax.experimental.pallas import tpu as pltpu
from jax.sharding import PartitionSpec as P

F32 = jnp.float32
BF16 = jnp.bfloat16


def low_rank_weights(low, slot, live, slots, rank_width):
    kept = jnp.arange(rank_width, dtype=jnp.int32)[None, :] < live[:, None]
    scaling = rank_width / live.astype(F32)
    scaled = jnp.where(kept, low * scaling[:, None], jnp.zeros((), F32)).astype(BF16)
    hot = slot[:, None] == jnp.arange(slots, dtype=jnp.int32)[None, :]
    spread = jnp.where(hot[:, :, None], scaled[:, None, :], jnp.zeros((), BF16))
    return spread.reshape(low.shape[0], slots * rank_width)


def tables(tenant, entry, live):
    ids = jnp.arange(entry.shape[0], dtype=jnp.int32)
    hot = (tenant[:, None] == ids[None, :]).astype(jnp.int32)
    return jnp.sum(hot * entry[None, :], axis=1), jnp.sum(hot * live[None, :], axis=1)


def general(rows, residual, weight, down, up, tenant, entry, live):
    own = residual.shape[0]
    cols = weight.shape[1]
    width = down.shape[1]
    slots = entry.shape[0]
    slot_all, live_all = tables(tenant, entry, live)
    part = rows.shape[0] // lax.axis_size("sub")
    mine = lax.dynamic_slice_in_dim(rows, lax.axis_index("sub") * part, part, 0)
    halves = lax.all_gather(lax.all_gather(mine, "blk", axis=0), "sub", axis=1)
    full = halves.reshape(-1, rows.shape[1])
    base = jnp.dot(full, weight, preferred_element_type=F32)
    low = lax.dot_general(
        full, down.reshape(-1, down.shape[2]), (((1,), (1,)), ((), ())), preferred_element_type=F32
    )
    held = down.shape[0]
    places = lax.axis_index("blk") * held + jnp.arange(held, dtype=jnp.int32)
    here = slot_all[:, None] == places[None, :]
    low = jnp.sum(
        jnp.where(here[:, :, None], low.reshape(-1, held, width), jnp.zeros((), F32)), axis=1
    )
    low = lax.psum(lax.psum_scatter(low, "split", scatter_dimension=0, tiled=True), "blk")
    base = lax.psum_scatter(base, "split", scatter_dimension=0, tiled=True)
    start = lax.axis_index("split") * own
    spread = low_rank_weights(
        low,
        lax.dynamic_slice_in_dim(slot_all, start, own, 0),
        lax.dynamic_slice_in_dim(live_all, start, own, 0),
        slots,
        width,
    )
    ups = lax.all_gather(up, "split", axis=0, tiled=True).reshape(slots * width, cols)
    lora = jnp.dot(spread, ups, preferred_element_type=F32)
    return (residual.astype(F32) + base + lora).astype(BF16)


def place_kernel(index_ref, sums_ref, got_ref, *refs):
    refs[-1][...] = (sums_ref[...] + got_ref[...].astype(F32)).astype(refs[-1].dtype)


def place(index, sums, got, step, rows, held=None):
    cols = sums.shape[1]
    piece = pl.BlockSpec((step, cols), lambda i, index: (i, 0))
    operands, in_specs, aliases = [index, sums, got], [piece, piece], {}
    if held is not None:
        operands.append(held)
        in_specs.append(pl.BlockSpec(memory_space=pl.ANY))
        aliases = {3: 0}
    return pl.pallas_call(
        place_kernel,
        out_shape=jax.ShapeDtypeStruct((rows, cols), BF16),
        grid_spec=pltpu.PrefetchScalarGridSpec(
            num_scalar_prefetch=1,
            grid=(sums.shape[0] // step,),
            in_specs=in_specs,
            out_specs=pl.BlockSpec((step, cols), lambda i, index: (index[i], 0)),
        ),
        input_output_aliases=aliases,
    )(*operands)


SWAP = [(0, 1), (1, 0)]
NEIGHBOURS = [(0, 1), (1, 0), (2, 3), (3, 2)]
MIDDLE = [(0, 0), (1, 2), (2, 1), (3, 3)]
ONWARD = [(0, 2), (3, 1), (1, 0), (2, 3)]
INWARD = [(0, 1), (3, 2)]


def line(rows, residual, weight, down, up, tenant, entry, live):
    z, x, c = lax.axis_index("blk"), lax.axis_index("split"), lax.axis_index("sub")
    block_rows, width = rows.shape[0], down.shape[1]
    own, cols = residual.shape
    slots = entry.shape[0]
    slot_all, live_all = tables(tenant, entry, live)
    end = (z == 0) | (z == 3)
    home = (z // 2) == x
    pieces = 2
    step = block_rows // pieces
    half = step // 2

    b, near, third, fourth = [], [], [], []
    mine = [
        lax.dynamic_slice_in_dim(rows, p * step + c * half, half, 0) for p in range(pieces)
    ]
    for piece in mine:
        a = lax.ppermute(piece, "blk", NEIGHBOURS)
        b = lax.ppermute(piece, "blk", MIDDLE)
        e = lax.ppermute(b, "blk", ONWARD)
        f = lax.ppermute(e, "blk", NEIGHBOURS)
        near.append(a)
        third.append(jnp.where(end, e, b))
        fourth.append(jnp.where(end, f, e))

    def both(piece):
        other = lax.ppermute(piece, "sub", SWAP)
        return jnp.where(c == 0, jnp.concatenate([piece, other]), jnp.concatenate([other, piece]))

    near, third, fourth = ([both(piece) for piece in part] for part in (near, third, fourth))
    near, third = jnp.concatenate(near), jnp.concatenate(third)

    down_map = down[0]
    maps = jnp.concatenate([down_map, lax.ppermute(down_map, "blk", INWARD)])
    first_id = jnp.where(end, -1, z)
    second_id = jnp.where(end, -1, jnp.where(z == 1, 0, 3))

    def low_rank(block, place):
        slot = lax.dynamic_slice_in_dim(slot_all, place, block.shape[0], 0)[:, None]
        low = lax.dot_general(block, maps, (((1,), (1,)), ((), ())), preferred_element_type=F32)
        zero = jnp.zeros((), F32)
        return jnp.where(slot == first_id, low[:, :width], zero) + jnp.where(
            slot == second_id, low[:, width:], zero
        )

    near_id = z + 1 - 2 * (z % 2)
    third_id = jnp.where(z < 2, 2, 1)
    fourth_id = jnp.where(z < 2, 3, 0)
    low_near = jnp.concatenate(
        [low_rank(rows, z * block_rows), low_rank(near, near_id * block_rows)]
    )
    low_far = jnp.concatenate(
        [low_rank(third, third_id * block_rows)]
        + [low_rank(fourth[p], fourth_id * block_rows + p * step) for p in range(pieces)]
    )
    low = jnp.where(home, low_near, low_far) + lax.ppermute(
        jnp.where(home, low_far, low_near), "split", SWAP
    )
    low = low + lax.ppermute(low, "blk", MIDDLE)
    low = jnp.where(x == 0, jnp.concatenate([low[block_rows:], low[:block_rows]]), low)
    start = x * own
    slot = lax.dynamic_slice_in_dim(slot_all, start, own, 0)
    rank = lax.dynamic_slice_in_dim(live_all, start, own, 0)
    kept = jnp.arange(width, dtype=jnp.int32)[None, :] < rank[:, None]
    scaling = width / rank.astype(F32)
    scaled = jnp.where(kept, low * scaling[:, None], jnp.zeros((), F32)).astype(BF16)
    scaled = jnp.where(end, lax.ppermute(scaled, "blk", NEIGHBOURS), scaled)
    hot = slot[:, None] == jnp.arange(slots, dtype=jnp.int32)[None, :]
    spread = jnp.where(hot[:, :, None], scaled[:, None, :], jnp.zeros((), BF16))
    spread = spread.reshape(own, slots * width)
    up_other = lax.ppermute(up, "split", SWAP)
    ups = jnp.where(x == 0, jnp.concatenate([up, up_other]), jnp.concatenate([up_other, up]))
    lora = jnp.dot(spread, ups.reshape(slots * width, cols), preferred_element_type=F32)
    rest = residual.astype(F32) + lora

    def product(block):
        return jnp.dot(block, weight, preferred_element_type=F32)

    def exchange(near_sum, far_sum):
        got = lax.ppermute(jnp.where(home, far_sum, near_sum).astype(BF16), "split", SWAP)
        return jnp.where(home, near_sum, far_sum), got

    near_sum = product(near)
    first, first_got = exchange(product(rows), product(third))
    first_place = jnp.where(home, z % 2, z // 2)
    out = None
    kept_sums, gots, places = [first], [first_got], []
    for p in range(pieces):
        kept_sum, got = exchange(near_sum[p * step : (p + 1) * step], product(fourth[p]))
        kept_sums.append(kept_sum)
        gots.append(got)
    places = [first_place * pieces + p for p in range(pieces)] + [
        (1 - first_place) * pieces + p for p in range(pieces)
    ]

    def total(kept_sum, at):
        return kept_sum + lax.dynamic_slice_in_dim(rest, at * step, kept_sum.shape[0], 0)

    early = jnp.concatenate(
        [total(first, first_place * pieces)]
        + [total(kept_sums[p], places[pieces + p - 1]) for p in range(1, pieces)]
    )
    out = place(
        jnp.stack(places[:-1]).astype(jnp.int32),
        early,
        jnp.concatenate(gots[:-1]),
        step,
        own,
    )
    return place(
        jnp.stack(places[-1:]).astype(jnp.int32),
        total(kept_sums[-1], places[-1]),
        gots[-1],
        step,
        own,
        out,
    )


def shards(rows, residual, weight, down, up, tenant, entry, live):
    sizes = [lax.axis_size(name) for name in ("blk", "split", "sub")]
    plan = line if sizes == [4, 2, 2] and down.shape[0] == 1 else general
    return plan(rows, residual, weight, down, up, tenant, entry, live)


def solution(mesh):
    in_specs = (
        P(("groups", "blk"), "split"),
        P(("groups", "split"), ("blk", "sub")),
        P("split", ("blk", "sub")),
        P("blk", None, "split"),
        P("split", None, ("blk", "sub")),
        P("groups"),
        P(),
        P(),
    )
    out_specs = P(("groups", "split"), ("blk", "sub"))
    return jax.shard_map(shards, mesh=mesh, in_specs=in_specs, out_specs=out_specs, check_vma=False)
```

```python
import functools

import jax
import jax.numpy as jnp
from jax import lax
from jax.experimental import pallas as pl
from jax.experimental.pallas import tpu as pltpu
from jax.sharding import PartitionSpec as P

F32 = jnp.float32
BF16 = jnp.bfloat16


def low_rank_weights(low, slot, live, slots, rank_width):
    kept = jnp.arange(rank_width, dtype=jnp.int32)[None, :] < live[:, None]
    scaling = rank_width / live.astype(F32)
    scaled = jnp.where(kept, low * scaling[:, None], jnp.zeros((), F32)).astype(BF16)
    hot = slot[:, None] == jnp.arange(slots, dtype=jnp.int32)[None, :]
    spread = jnp.where(hot[:, :, None], scaled[:, None, :], jnp.zeros((), BF16))
    return spread.reshape(low.shape[0], slots * rank_width)


def tables(tenant, entry, live):
    ids = jnp.arange(entry.shape[0], dtype=jnp.int32)
    hot = (tenant[:, None] == ids[None, :]).astype(jnp.int32)
    return jnp.sum(hot * entry[None, :], axis=1), jnp.sum(hot * live[None, :], axis=1)


def general(rows, residual, weight, down, up, tenant, entry, live):
    own = residual.shape[0]
    cols = weight.shape[1]
    width = down.shape[1]
    slots = entry.shape[0]
    slot_all, live_all = tables(tenant, entry, live)
    part = rows.shape[0] // lax.axis_size("sub")
    mine = lax.dynamic_slice_in_dim(rows, lax.axis_index("sub") * part, part, 0)
    halves = lax.all_gather(lax.all_gather(mine, "blk", axis=0), "sub", axis=1)
    full = halves.reshape(-1, rows.shape[1])
    base = jnp.dot(full, weight, preferred_element_type=F32)
    low = lax.dot_general(
        full, down.reshape(-1, down.shape[2]), (((1,), (1,)), ((), ())), preferred_element_type=F32
    )
    held = down.shape[0]
    places = lax.axis_index("blk") * held + jnp.arange(held, dtype=jnp.int32)
    here = slot_all[:, None] == places[None, :]
    low = jnp.sum(
        jnp.where(here[:, :, None], low.reshape(-1, held, width), jnp.zeros((), F32)), axis=1
    )
    low = lax.psum(lax.psum_scatter(low, "split", scatter_dimension=0, tiled=True), "blk")
    base = lax.psum_scatter(base, "split", scatter_dimension=0, tiled=True)
    start = lax.axis_index("split") * own
    spread = low_rank_weights(
        low,
        lax.dynamic_slice_in_dim(slot_all, start, own, 0),
        lax.dynamic_slice_in_dim(live_all, start, own, 0),
        slots,
        width,
    )
    ups = lax.all_gather(up, "split", axis=0, tiled=True).reshape(slots * width, cols)
    lora = jnp.dot(spread, ups, preferred_element_type=F32)
    return (residual.astype(F32) + base + lora).astype(BF16)


SWAP = [(0, 1), (1, 0)]
NEAR = [(0, 1), (1, 0), (2, 3), (3, 2)]
FAR = [(0, 2), (2, 0), (1, 3), (3, 1)]
VMEM = pl.BlockSpec(memory_space=pltpu.VMEM)
SMEM = pl.BlockSpec(memory_space=pltpu.SMEM)
COST = pl.CostEstimate(flops=0, bytes_accessed=0, transcendentals=0)
PARAMS = pltpu.CompilerParams(vmem_limit_bytes=16 * 1024 * 1024)


def products(rows, weight_ref, store):
    cols = weight_ref.shape[1]
    tile = 256 if cols % 256 == 0 else cols
    for j in range(0, cols, tile):
        store(j, tile, jnp.dot(rows, weight_ref[:, j : j + tile], preferred_element_type=F32))


def low_product(rows, down_ref):
    return lax.dot_general(
        rows, down_ref[...], (((1,), (1,)), ((), ())), preferred_element_type=F32
    )


def row_pieces(flags_ref, refs):
    c = flags_ref[1]
    ordered = []
    for mine, other in zip(refs[::2], refs[1::2]):
        mine, other = mine[...], other[...]
        ordered += [jnp.where(c == 0, mine, other), jnp.where(c == 0, other, mine)]
    return jnp.concatenate(ordered)


def own_kernel(rows_ref, weight_ref, down_ref, sum_ref, low_ref):
    rows = rows_ref[...]

    def store(j, tile, value):
        sum_ref[:, j : j + tile] = value

    products(rows, weight_ref, store)
    low_ref[...] = low_product(rows, down_ref)


def mix_kernel(plan, flags_ref, weight_ref, down_ref, *refs):
    taken = 0
    groups = []
    for count, begin in plan:
        groups.append((row_pieces(flags_ref, refs[taken : taken + count]), begin))
        taken += count
    refs = list(refs[taken:])
    helds = [refs.pop(0) if begin is not None else None for _, begin in groups]
    home = flags_ref[0] == 1
    low_ref = refs.pop()
    rows = jnp.concatenate([group for group, _ in groups])
    low_ref[...] = low_product(rows, down_ref)
    has_parts = any(begin is not None for _, begin in groups)
    send_ref = refs.pop() if has_parts else None
    keep_ref = refs.pop() if has_parts else None
    sum_ref = refs.pop() if refs else None

    def store(j, tile, value):
        at, sent, summed = 0, 0, 0
        for (group, begin), held_ref in zip(groups, helds):
            count = group.shape[0]
            part = value[at : at + count]
            if begin is None:
                sum_ref[summed : summed + count, j : j + tile] = part
                summed += count
            else:
                held = held_ref[begin : begin + count, j : j + tile]
                keep_ref[sent : sent + count, j : j + tile] = jnp.where(home, held, part)
                send_ref[sent : sent + count, j : j + tile] = jnp.where(home, part, held).astype(
                    BF16
                )
                sent += count
            at += count

    products(rows, weight_ref, store)


def call(kernel, outs, in_specs, operands):
    return pl.pallas_call(
        kernel,
        out_shape=[jax.ShapeDtypeStruct(shape, dtype) for shape, dtype in outs],
        in_specs=in_specs,
        out_specs=[VMEM] * len(outs),
        compiler_params=PARAMS,
        cost_estimate=COST,
    )(*operands)


def final_kernel(flags_ref, residual_ref, spread_ref, ups_ref, *refs):
    *parts, out_ref, rest_ref = refs
    rest_ref[...] = residual_ref[...].astype(F32) + jnp.dot(
        spread_ref[...], ups_ref[...], preferred_element_type=F32
    )
    step = out_ref.shape[0] // 4
    place = flags_ref[2] * (2 * step)
    at = 0
    for keep, got in zip(parts[::2], parts[1::2]):
        for begin in range(0, keep.shape[0], step):
            first = place if at < 2 else 2 * step - place
            rows = pl.ds(pl.multiple_of(first + (at % 2) * step, step), step)
            here = slice(begin, begin + step)
            out_ref[rows, :] = (
                rest_ref[rows, :] + keep[here, :] + got[here, :].astype(F32)
            ).astype(BF16)
            at += 1


def line(rows, residual, weight, down, up, tenant, entry, live):
    z, x, c = lax.axis_index("blk"), lax.axis_index("split"), lax.axis_index("sub")
    block_rows, feats = rows.shape
    width = down.shape[1]
    own, cols = residual.shape
    slots = entry.shape[0]
    slot_all, live_all = tables(tenant, entry, live)
    home = (z // 2) == x
    flags = jnp.stack([home.astype(jnp.int32), c, z % 2])
    unit = 16
    step = block_rows // 2
    half = step // 2
    down_map = down[0]
    barrier = lax.optimization_barrier

    def swapped(piece):
        parts = []
        for at in range(0, piece.shape[0], unit):
            part = piece[at : at + unit]
            parts += [part, lax.ppermute(part, "sub", SWAP)]
        return parts

    def mixed(plan, groups, helds):
        counts = [sum(part.shape[0] for part in group) for group in groups]
        sums = sum(n for n, begin in zip(counts, plan) if begin is None)
        parts = sum(n for n, begin in zip(counts, plan) if begin is not None)
        outs = [((sums, cols), F32)] if sums else []
        outs += [((parts, cols), F32), ((parts, cols), BF16)] if parts else []
        outs.append(((sums + parts, width), F32))
        flat = [part for group in groups for part in group]
        return call(
            functools.partial(mix_kernel, [(len(g), b) for g, b in zip(groups, plan)]),
            outs,
            [SMEM] + [VMEM] * (2 + len(flat) + len(helds)),
            [flags, weight, down_map] + flat + helds,
        )

    def over_x(value):
        return lax.ppermute(value, "split", SWAP)

    mine = lax.dynamic_index_in_dim(
        rows.reshape(block_rows // (2 * unit), 2, unit, feats), c, 1, False
    ).reshape(2, half, feats)
    mine = [mine[0], mine[1]]
    far = [lax.ppermute(piece, "blk", FAR) for piece in mine]
    near = [lax.ppermute(piece, "blk", NEAR) for piece in mine]
    up_other = over_x(up)
    own_sum, own_low = call(
        own_kernel,
        [((block_rows, cols), F32), ((block_rows, width), F32)],
        [VMEM] * 3,
        [rows, weight, down_map],
    )
    far[0], own_sum, own_low, up_other = barrier((far[0], own_sum, own_low, up_other))

    last = [lax.ppermute(far[0], "blk", NEAR)]
    keep_a, send_a, low_a = mixed([0], [swapped(far[0])], [own_sum])
    near_sum, near_low = mixed([None], [swapped(near[0]) + swapped(near[1])], [])
    got_a = over_x(send_a)
    far[1], last[0], got_a, keep_a, near_sum, own_sum = barrier(
        (far[1], last[0], got_a, keep_a, near_sum, own_sum)
    )

    last.append(lax.ppermute(far[1], "blk", NEAR))
    keep_b, send_b, low_b = mixed(
        [step, 0], [swapped(far[1]), swapped(last[0])], [own_sum, near_sum]
    )
    got_b = over_x(send_b)
    last[1], send_b, keep_b, near_sum = barrier((last[1], send_b, keep_b, near_sum))

    keep_c, send_c, low_c = mixed([step], [swapped(last[1])], [near_sum])
    got_c = over_x(send_c)

    odd = z % 2 == 1
    far_low = jnp.concatenate([low_a, low_b[:step]])
    last_low = jnp.concatenate([low_b[step:], low_c])
    near_half = jnp.where(
        odd, jnp.concatenate([near_low, own_low]), jnp.concatenate([own_low, near_low])
    )
    far_half = jnp.where(
        odd, jnp.concatenate([last_low, far_low]), jnp.concatenate([far_low, last_low])
    )
    start = x * own
    slot = lax.dynamic_slice_in_dim(slot_all, start, own, 0)
    rank = lax.dynamic_slice_in_dim(live_all, start, own, 0)
    low = jnp.where(home, near_half, far_half) + over_x(jnp.where(home, far_half, near_half))
    low = jnp.where((slot == z)[:, None], low, jnp.zeros((), F32))
    low, got_b = barrier((low, got_b))
    low = low + lax.ppermute(low, "blk", NEAR)
    low, got_c = barrier((low, got_c))
    low = low + lax.ppermute(low, "blk", FAR)
    spread = low_rank_weights(low, slot, rank, slots, width)
    ups = jnp.where(x == 0, jnp.concatenate([up, up_other]), jnp.concatenate([up_other, up]))
    parts = [keep_a, got_a, keep_b, got_b, keep_c, got_c]
    return pl.pallas_call(
        final_kernel,
        out_shape=jax.ShapeDtypeStruct(residual.shape, BF16),
        in_specs=[SMEM] + [VMEM] * (3 + len(parts)),
        out_specs=VMEM,
        scratch_shapes=[pltpu.VMEM(residual.shape, F32)],
        compiler_params=PARAMS,
        cost_estimate=COST,
    )(flags, residual, spread, ups.reshape(slots * width, cols), *parts)


def shards(rows, residual, weight, down, up, tenant, entry, live):
    sizes = [lax.axis_size(name) for name in ("blk", "split", "sub")]
    plan = line if sizes == [4, 2, 2] and down.shape[0] == 1 else general
    return plan(rows, residual, weight, down, up, tenant, entry, live)


def solution(mesh):
    in_specs = (
        P(("groups", "blk"), "split"),
        P(("groups", "split"), ("blk", "sub")),
        P("split", ("blk", "sub")),
        P("blk", None, "split"),
        P("split", None, ("blk", "sub")),
        P("groups"),
        P(),
        P(),
    )
    out_specs = P(("groups", "split"), ("blk", "sub"))
    return jax.shard_map(shards, mesh=mesh, in_specs=in_specs, out_specs=out_specs, check_vma=False)
```

```python
import functools

import jax
import jax.numpy as jnp
from jax import lax
from jax.experimental import pallas as pl
from jax.experimental.pallas import tpu as pltpu
from jax.sharding import PartitionSpec as P

F32 = jnp.float32
BF16 = jnp.bfloat16


def low_rank_weights(low, slot, live, slots, rank_width):
    kept = jnp.arange(rank_width, dtype=jnp.int32)[None, :] < live[:, None]
    scaling = rank_width / live.astype(F32)
    scaled = jnp.where(kept, low * scaling[:, None], jnp.zeros((), F32)).astype(BF16)
    hot = slot[:, None] == jnp.arange(slots, dtype=jnp.int32)[None, :]
    spread = jnp.where(hot[:, :, None], scaled[:, None, :], jnp.zeros((), BF16))
    return spread.reshape(low.shape[0], slots * rank_width)


def tables(tenant, entry, live):
    ids = jnp.arange(entry.shape[0], dtype=jnp.int32)
    hot = (tenant[:, None] == ids[None, :]).astype(jnp.int32)
    return jnp.sum(hot * entry[None, :], axis=1), jnp.sum(hot * live[None, :], axis=1)


def general(rows, residual, weight, down, up, tenant, entry, live):
    own = residual.shape[0]
    cols = weight.shape[1]
    width = down.shape[1]
    slots = entry.shape[0]
    slot_all, live_all = tables(tenant, entry, live)
    part = rows.shape[0] // lax.axis_size("sub")
    mine = lax.dynamic_slice_in_dim(rows, lax.axis_index("sub") * part, part, 0)
    halves = lax.all_gather(lax.all_gather(mine, "blk", axis=0), "sub", axis=1)
    full = halves.reshape(-1, rows.shape[1])
    base = jnp.dot(full, weight, preferred_element_type=F32)
    low = lax.dot_general(
        full, down.reshape(-1, down.shape[2]), (((1,), (1,)), ((), ())), preferred_element_type=F32
    )
    held = down.shape[0]
    places = lax.axis_index("blk") * held + jnp.arange(held, dtype=jnp.int32)
    here = slot_all[:, None] == places[None, :]
    low = jnp.sum(
        jnp.where(here[:, :, None], low.reshape(-1, held, width), jnp.zeros((), F32)), axis=1
    )
    low = lax.psum(lax.psum_scatter(low, "split", scatter_dimension=0, tiled=True), "blk")
    base = lax.psum_scatter(base, "split", scatter_dimension=0, tiled=True)
    start = lax.axis_index("split") * own
    spread = low_rank_weights(
        low,
        lax.dynamic_slice_in_dim(slot_all, start, own, 0),
        lax.dynamic_slice_in_dim(live_all, start, own, 0),
        slots,
        width,
    )
    ups = lax.all_gather(up, "split", axis=0, tiled=True).reshape(slots * width, cols)
    lora = jnp.dot(spread, ups, preferred_element_type=F32)
    return (residual.astype(F32) + base + lora).astype(BF16)


SWAP = [(0, 1), (1, 0)]
NEAR = [(0, 1), (1, 0), (2, 3), (3, 2)]
FAR = [(0, 2), (2, 0), (1, 3), (3, 1)]
VMEM = pl.BlockSpec(memory_space=pltpu.VMEM)
SMEM = pl.BlockSpec(memory_space=pltpu.SMEM)
HBM = pl.BlockSpec(memory_space=pltpu.HBM)
COST = pl.CostEstimate(flops=0, bytes_accessed=0, transcendentals=0)
PARAMS = pltpu.CompilerParams(vmem_limit_bytes=12 * 1024 * 1024)


def shape(dims, dtype):
    return jax.ShapeDtypeStruct(dims, dtype)


def column_tiles(cols):
    tile = 256 if cols % 256 == 0 else cols
    return [slice(at, at + tile) for at in range(0, cols, tile)]


def dot(a, b):
    return jnp.dot(a, b, preferred_element_type=F32)


def cut_kernel(flags_ref, rows_ref, first_ref, second_ref, half_ref, sems):
    half = half_ref.shape[0]
    step = half // 2
    start = pl.multiple_of(flags_ref[1] * half, half)
    copies = [
        pltpu.make_async_copy(rows_ref.at[pl.ds(start, step)], first_ref, sems.at[0]),
        pltpu.make_async_copy(rows_ref.at[pl.ds(start + step, step)], second_ref, sems.at[1]),
        pltpu.make_async_copy(rows_ref.at[pl.ds(start, half)], half_ref, sems.at[2]),
    ]
    for copy in copies:
        copy.start()
    for copy in copies:
        copy.wait()


def own_kernel(flags_ref, weight_ref, down_ref, rows_ref, sum_ref, low_ref, block):
    step = block.shape[0] // 4
    c = flags_ref[1]
    for i in range(4):
        half = c if i % 2 == 0 else 1 - c
        start = pl.multiple_of(half * (2 * step) + (i // 2) * step, step)
        block[i * step : (i + 1) * step] = rows_ref[pl.ds(start, step)]
    low_ref[...] = dot(block[...], down_ref[...])
    for tile in column_tiles(weight_ref.shape[1]):
        sum_ref[:, tile] = dot(block[...], weight_ref[:, tile])


def part(home, held, value, keep_ref, send_ref, rows, tile):
    @pl.when(home)
    def _():
        keep_ref[rows, tile] = held
        send_ref[rows, tile] = value.astype(BF16)

    @pl.when(jnp.logical_not(home))
    def _():
        keep_ref[rows, tile] = value
        send_ref[rows, tile] = held.astype(BF16)


def piece_kernel(flags_ref, weight_ref, down_ref, held_ref, *refs):
    *pieces, keep_ref, send_ref, low_ref, block = refs
    at = 0
    for ref in pieces:
        block[at : at + ref.shape[0]] = ref[...]
        at += ref.shape[0]
    low_ref[...] = dot(block[...], down_ref[...])
    home = flags_ref[0] == 1
    rows = slice(0, at)
    for tile in column_tiles(weight_ref.shape[1]):
        value = dot(block[...], weight_ref[:, tile])
        part(home, held_ref[rows, tile], value, keep_ref, send_ref, rows, tile)


def end_kernel(
    flags_ref, weight_ref, down_ref, held_ref, own_low, low_a, low_b, *refs
):
    *pieces, keep_ref, send_ref, low_keep_ref, low_send_ref, block = refs
    size = block.shape[0]
    at = 0
    for ref in pieces:
        block[at : at + ref.shape[0]] = ref[...]
        at += ref.shape[0]
    low_c = dot(block[...], down_ref[...])
    home = flags_ref[0] == 1
    near = pl.ds(pl.multiple_of(flags_ref[2] * (2 * size), size), 2 * size)
    far = pl.ds(pl.multiple_of((1 - flags_ref[2]) * (2 * size), size), 2 * size)

    def store(near_ref, far_ref):
        near_ref[near, :] = own_low[...]
        near_ref[far, :] = low_b[: 2 * size]
        far_ref[near, :] = jnp.concatenate([low_a[...], low_b[2 * size : 3 * size]])
        far_ref[far, :] = jnp.concatenate([low_b[3 * size :], low_c])

    @pl.when(home)
    def _():
        store(low_keep_ref, low_send_ref)

    @pl.when(jnp.logical_not(home))
    def _():
        store(low_send_ref, low_keep_ref)

    rows = slice(0, size)
    for tile in column_tiles(weight_ref.shape[1]):
        value = dot(block[...], weight_ref[:, tile])
        part(home, held_ref[rows, tile], value, keep_ref, send_ref, rows, tile)


def blocks_kernel(
    flags_ref, weight_ref, down_ref, held_ref, near_ref, near_other_ref, far_ref, far_other_ref,
    last_ref, last_other_ref, keep_ref, send_ref, hold_ref, low_ref, block,
):
    step = far_ref.shape[0]
    pieces = [
        near_ref[:step], near_other_ref[:step], near_ref[step:], near_other_ref[step:],
        far_ref[...], far_other_ref[...], last_ref[...], last_other_ref[...],
    ]
    for i, piece in enumerate(pieces):
        block[i * step : (i + 1) * step] = piece
    low_ref[...] = dot(block[...], down_ref[...])
    home = flags_ref[0] == 1
    size = 2 * step
    for tile in column_tiles(weight_ref.shape[1]):
        value = dot(block[...], weight_ref[:, tile])
        hold_ref[:, tile] = value[size : 2 * size]
        held = held_ref[size : 2 * size, tile]
        part(home, held, value[2 * size : 3 * size], keep_ref, send_ref, slice(0, size), tile)
        part(home, value[:size], value[3 * size :], keep_ref, send_ref, slice(size, 2 * size), tile)


def final_kernel(flags_ref, residual_ref, low_ref, low_got_ref, factor_ref, ups_ref, *refs):
    *parts, out_ref, lora_ref = refs
    low = low_ref[...] + low_got_ref[...]
    lora = dot((low * factor_ref[0]).astype(BF16), ups_ref[0])
    for slot in range(1, ups_ref.shape[0]):
        lora += dot((low * factor_ref[slot]).astype(BF16), ups_ref[slot])
    lora_ref[...] = lora
    step = out_ref.shape[0] // 8
    odd, c = flags_ref[2], flags_ref[1]
    at = 0
    for keep, got in zip(parts[::2], parts[1::2]):
        for begin in range(0, keep.shape[0], step):
            second, piece, other = at // 4, at // 2 % 2, at % 2
            block = (1 - odd if second else odd) * (4 * step)
            half = (1 - c if other else c) * (2 * step)
            to = pl.ds(pl.multiple_of(block + half + piece * step, step), step)
            lora = pl.ds(pl.multiple_of(block + (2 * piece + other) * step, step), step)
            here = slice(begin, begin + step)
            out_ref[to, :] = (
                residual_ref[to, :].astype(F32)
                + lora_ref[lora, :]
                + keep[here, :]
                + got[here, :].astype(F32)
            ).astype(BF16)
            at += 1


def call(kernel, outs, in_specs, operands, scratch=()):
    return pl.pallas_call(
        kernel,
        out_shape=outs,
        in_specs=in_specs,
        out_specs=jax.tree.map(lambda _: VMEM, outs),
        scratch_shapes=scratch,
        compiler_params=PARAMS,
        cost_estimate=COST,
    )(*operands)


def line(rows, residual, weight, down, up, tenant, entry, live):
    z, x, c = lax.axis_index("blk"), lax.axis_index("split"), lax.axis_index("sub")
    block_rows, feats = rows.shape
    width = down.shape[1]
    own, cols = residual.shape
    slots = entry.shape[0]
    home = (z // 2) == x
    flags = jnp.stack([home.astype(jnp.int32), c, z % 2])
    half, step = block_rows // 2, block_rows // 4
    barrier = lax.optimization_barrier

    def over_core(value):
        return lax.ppermute(value, "sub", SWAP)

    def over_x(value):
        return lax.ppermute(value, "split", SWAP)

    def along(value, pairs):
        return lax.ppermute(value, "blk", pairs)

    def rearranged(value):
        value = lax.dynamic_slice_in_dim(value, x * own, own, 0).reshape(2, 2, 2, step)
        value = jnp.where(c == 0, value, value[:, ::-1])
        return value.transpose(0, 2, 1, 3).reshape(own)

    slot_all, live_all = tables(tenant, entry, live)
    slot, rank = rearranged(slot_all), rearranged(live_all)
    kept = jnp.arange(width, dtype=jnp.int32)[None, :] < rank[:, None]
    scaling = jnp.where(kept, (width / rank.astype(F32))[:, None], jnp.zeros((), F32))
    hot = slot[None, :] == jnp.arange(slots, dtype=jnp.int32)[:, None]
    factor = jnp.where(hot[:, :, None], scaling[None], jnp.zeros((), F32))
    here = jnp.broadcast_to((slot == z)[:, None], (own, width)).astype(F32)
    down_map = down[0].T

    first, second, both = call(
        cut_kernel,
        [shape((step, feats), BF16), shape((step, feats), BF16), shape((half, feats), BF16)],
        [SMEM, HBM],
        [flags, rows],
        [pltpu.SemaphoreType.DMA((3,))],
    )
    far = [along(first, FAR), along(second, FAR)]
    near = along(both, NEAR)
    up_other = over_x(up)
    own_sum, own_low = call(
        own_kernel,
        [shape((block_rows, cols), F32), shape((block_rows, width), F32)],
        [SMEM] + [VMEM] * 3,
        [flags, weight, down_map, rows],
        [pltpu.VMEM((block_rows, feats), BF16)],
    )
    weight, own_sum = barrier((weight, own_sum))
    ups = jnp.where(x == 0, jnp.concatenate([up, up_other]), jnp.concatenate([up_other, up]))
    far[0], own_sum = barrier((far[0], own_sum))

    def in_quarters(piece):
        quarters = [piece[: step // 2], piece[step // 2 :]]
        return quarters + [over_core(quarter) for quarter in quarters]

    def parted(count):
        return [shape((count, cols), F32), shape((count, cols), BF16)]

    last = [along(far[0], NEAR)]
    keep_a, send_a, low_a = call(
        piece_kernel,
        parted(half) + [shape((half, width), F32)],
        [SMEM] + [VMEM] * 7,
        [flags, weight, down_map, own_sum] + in_quarters(far[0]),
        [pltpu.VMEM((half, feats), BF16)],
    )
    got_a = over_x(send_a)
    far[1], last[0], near, got_a, keep_a, own_sum, ups, factor, here = barrier(
        (far[1], last[0], near, got_a, keep_a, own_sum, ups, factor, here)
    )

    last.append(along(far[1], NEAR))
    keep_b, send_b, hold, low_b = call(
        blocks_kernel,
        parted(block_rows) + [shape((half, cols), F32), shape((2 * block_rows, width), F32)],
        [SMEM] + [VMEM] * 9,
        [flags, weight, down_map, own_sum, near, over_core(near), far[1], over_core(far[1])]
        + [last[0], over_core(last[0])],
        [pltpu.VMEM((2 * block_rows, feats), BF16)],
    )
    got_b = over_x(send_b)
    last[1], send_b, keep_b, hold = barrier((last[1], send_b, keep_b, hold))

    keep_c, send_c, low_keep, low_send = call(
        end_kernel,
        parted(half) + [shape((own, width), F32)] * 2,
        [SMEM] + [VMEM] * 10,
        [flags, weight, down_map, hold, own_low, low_a, low_b] + in_quarters(last[1]),
        [pltpu.VMEM((half, feats), BF16)],
    )
    got_c = over_x(send_c)
    low_send, got_b = barrier((low_send, got_b))
    low = (low_keep + over_x(low_send)) * here
    low = low + along(low, NEAR)
    low, got_c = barrier((low, got_c))
    parts = [keep_a, got_a, keep_b, got_b, keep_c, got_c]
    return call(
        final_kernel,
        shape(residual.shape, BF16),
        [SMEM] + [VMEM] * (5 + len(parts)),
        [flags, residual, low, along(low, FAR), factor, ups] + parts,
        [pltpu.VMEM(residual.shape, F32)],
    )


def shards(rows, residual, weight, down, up, tenant, entry, live):
    sizes = [lax.axis_size(name) for name in ("blk", "split", "sub")]
    plan = line if sizes == [4, 2, 2] and down.shape[0] == 1 else general
    return plan(rows, residual, weight, down, up, tenant, entry, live)


def solution(mesh):
    in_specs = (
        P(("groups", "blk"), "split"),
        P(("groups", "split"), ("blk", "sub")),
        P("split", ("blk", "sub")),
        P("blk", None, "split"),
        P("split", None, ("blk", "sub")),
        P("groups"),
        P(),
        P(),
    )
    out_specs = P(("groups", "split"), ("blk", "sub"))
    return jax.shard_map(shards, mesh=mesh, in_specs=in_specs, out_specs=out_specs, check_vma=False)
```

```python
import functools

import jax
import jax.numpy as jnp
from jax import lax
from jax.experimental import pallas as pl
from jax.experimental.pallas import tpu as pltpu
from jax.sharding import PartitionSpec as P

F32 = jnp.float32
BF16 = jnp.bfloat16


def low_rank_weights(low, slot, live, slots, rank_width):
    kept = jnp.arange(rank_width, dtype=jnp.int32)[None, :] < live[:, None]
    scaling = rank_width / live.astype(F32)
    scaled = jnp.where(kept, low * scaling[:, None], jnp.zeros((), F32)).astype(BF16)
    hot = slot[:, None] == jnp.arange(slots, dtype=jnp.int32)[None, :]
    spread = jnp.where(hot[:, :, None], scaled[:, None, :], jnp.zeros((), BF16))
    return spread.reshape(low.shape[0], slots * rank_width)


def tables(tenant, entry, live):
    ids = jnp.arange(entry.shape[0], dtype=jnp.int32)
    hot = (tenant[:, None] == ids[None, :]).astype(jnp.int32)
    return jnp.sum(hot * entry[None, :], axis=1), jnp.sum(hot * live[None, :], axis=1)


def general(rows, residual, weight, down, up, tenant, entry, live):
    own = residual.shape[0]
    cols = weight.shape[1]
    width = down.shape[1]
    slots = entry.shape[0]
    slot_all, live_all = tables(tenant, entry, live)
    part = rows.shape[0] // lax.axis_size("sub")
    mine = lax.dynamic_slice_in_dim(rows, lax.axis_index("sub") * part, part, 0)
    halves = lax.all_gather(lax.all_gather(mine, "blk", axis=0), "sub", axis=1)
    full = halves.reshape(-1, rows.shape[1])
    base = jnp.dot(full, weight, preferred_element_type=F32)
    low = lax.dot_general(
        full, down.reshape(-1, down.shape[2]), (((1,), (1,)), ((), ())), preferred_element_type=F32
    )
    held = down.shape[0]
    places = lax.axis_index("blk") * held + jnp.arange(held, dtype=jnp.int32)
    here = slot_all[:, None] == places[None, :]
    low = jnp.sum(
        jnp.where(here[:, :, None], low.reshape(-1, held, width), jnp.zeros((), F32)), axis=1
    )
    low = lax.psum(lax.psum_scatter(low, "split", scatter_dimension=0, tiled=True), "blk")
    base = lax.psum_scatter(base, "split", scatter_dimension=0, tiled=True)
    start = lax.axis_index("split") * own
    spread = low_rank_weights(
        low,
        lax.dynamic_slice_in_dim(slot_all, start, own, 0),
        lax.dynamic_slice_in_dim(live_all, start, own, 0),
        slots,
        width,
    )
    ups = lax.all_gather(up, "split", axis=0, tiled=True).reshape(slots * width, cols)
    lora = jnp.dot(spread, ups, preferred_element_type=F32)
    return (residual.astype(F32) + base + lora).astype(BF16)


SWAP = [(0, 1), (1, 0)]
NEAR = [(0, 1), (1, 0), (2, 3), (3, 2)]
FAR = [(0, 2), (2, 0), (1, 3), (3, 1)]
VMEM = pl.BlockSpec(memory_space=pltpu.VMEM)
SMEM = pl.BlockSpec(memory_space=pltpu.SMEM)
HBM = pl.BlockSpec(memory_space=pltpu.HBM)
COST = pl.CostEstimate(flops=0, bytes_accessed=0, transcendentals=0)
PARAMS = pltpu.CompilerParams(vmem_limit_bytes=20 * 1024 * 1024)


def shape(dims, dtype):
    return jax.ShapeDtypeStruct(dims, dtype)


def dot(a, b):
    return jnp.dot(a, b, preferred_element_type=F32)


def call(kernel, outs, in_specs, operands, scratch=()):
    return pl.pallas_call(
        kernel,
        out_shape=outs,
        in_specs=in_specs,
        out_specs=jax.tree.map(lambda _: VMEM, outs),
        scratch_shapes=scratch,
        compiler_params=PARAMS,
        cost_estimate=COST,
    )(*operands)


def column_tiles(cols):
    tile = 256 if cols % 256 == 0 else cols
    return [slice(at, at + tile) for at in range(0, cols, tile)]


def streamed_scratch(weight):
    return [
        pltpu.VMEM(weight.shape, weight.dtype),
        pltpu.SemaphoreType.DMA((len(column_tiles(weight.shape[1])),)),
    ]


def streamed(weight_ref, tiles_ref, sems):
    tiles = column_tiles(weight_ref.shape[1])
    copies = [
        pltpu.make_async_copy(weight_ref.at[:, tile], tiles_ref.at[:, tile], sems.at[i])
        for i, tile in enumerate(tiles)
    ]
    for copy in copies:
        copy.start()
    for copy, tile in zip(copies, tiles):
        copy.wait()
        yield tile, tiles_ref[:, tile]


def sum_kernel(weight_ref, *refs):
    *pieces, sum_ref, tiles_ref, sems = refs
    rows = jnp.concatenate([piece[...] for piece in pieces])
    for tile, weights in streamed(weight_ref, tiles_ref, sems):
        sum_ref[:, tile] = dot(rows, weights)


def part(home, held, value, keep_ref, send_ref, tile):
    keep_ref[:, tile] = jnp.where(home, held, value)
    send_ref[:, tile] = jnp.where(home, value, held).astype(BF16)


def part_kernel(begins, flags_ref, weight_ref, *refs):
    count = len(begins)
    *refs, tiles_ref, sems = refs
    pieces, helds, outs = refs[:count], refs[count : 2 * count], refs[2 * count :]
    rows = jnp.concatenate([piece[...] for piece in pieces])
    home = flags_ref[0] == 1
    size = pieces[0].shape[0]
    for tile, weights in streamed(weight_ref, tiles_ref, sems):
        value = dot(rows, weights)
        for i, begin in enumerate(begins):
            held = helds[i][begin : begin + size, tile]
            mine = value[i * size : (i + 1) * size]
            part(home, held, mine, outs[2 * i], outs[2 * i + 1], tile)


def end_kernel(flags_ref, weight_ref, piece_ref, held_ref, keep_ref, send_ref):
    size = piece_ref.shape[0]
    value = dot(piece_ref[...], weight_ref[...])
    part(flags_ref[0] == 1, held_ref[size:, :], value, keep_ref, send_ref, slice(None))


def low_kernel(maps_ref, *refs):
    *pieces, low_ref = refs
    rows = jnp.concatenate([piece[...] for piece in pieces])
    low_ref[...] = lax.dot_general(
        rows, maps_ref[...], (((1,), (1,)), ((), ())), preferred_element_type=F32
    )


def final_kernel(flags_ref, residual_ref, spread_ref, ups_ref, *refs):
    *parts, out_ref = refs
    lora = dot(spread_ref[...], ups_ref[...])
    step = out_ref.shape[0] // 4
    odd = flags_ref[1] == 1
    sums = [
        keep[...] + got[...].astype(F32) for keep, got in zip(parts[::2], parts[1::2])
    ]
    for at in range(4):
        here = slice(at * step, (at + 1) * step)
        base = jnp.where(odd, sums[(at + 2) % 4], sums[at])
        out_ref[here, :] = (residual_ref[here, :].astype(F32) + base + lora[here]).astype(BF16)


def line(rows, residual, weight, down, up, tenant, entry, live):
    z, x, c = lax.axis_index("blk"), lax.axis_index("split"), lax.axis_index("sub")
    y = lax.axis_index("groups")
    block_rows = rows.shape[0]
    width = down.shape[1]
    own, cols = residual.shape
    slots = entry.shape[0]
    home = (z // 2) == x
    odd = z % 2 == 1
    half, step = block_rows // 2, block_rows // 4
    barrier = lax.optimization_barrier

    def over_core(value):
        return lax.ppermute(value, "sub", SWAP)

    def over_x(value):
        return lax.ppermute(value, "split", SWAP)

    def along(value, pairs):
        return lax.ppermute(value, "blk", pairs)

    def by_core(mine, other):
        return jnp.where(c == 0, jnp.concatenate([mine, other]), jnp.concatenate([other, mine]))

    def whole(piece):
        return by_core(piece, over_core(piece))

    mine = [lax.dynamic_slice_in_dim(rows, p * half + c * step, step, 0) for p in range(2)]
    far = [along(mine[0], FAR)]
    near = [along(mine[0], NEAR)]
    rank_half, rank_quarter = width // 2, width // 4
    down_mine = lax.dynamic_slice_in_dim(down[0], c * rank_half, rank_half, 0)
    quarter = lax.dynamic_slice_in_dim(down_mine, y * rank_quarter, rank_quarter, 0)
    quarter = along(quarter, NEAR)
    near.append(along(mine[1], NEAR))
    far.append(along(mine[1], FAR))
    quarter_other = lax.ppermute(quarter, "groups", SWAP)
    maps = jnp.concatenate(
        [
            down_mine,
            jnp.where(
                y == 0,
                jnp.concatenate([quarter, quarter_other]),
                jnp.concatenate([quarter_other, quarter]),
            ),
        ]
    )
    up_other = over_x(up)
    ups = jnp.where(x == 0, jnp.concatenate([up, up_other]), jnp.concatenate([up_other, up]))

    slot_all, live_all = tables(tenant, entry, live)

    flags = jnp.stack([home, odd]).astype(jnp.int32)
    own_sum = call(
        sum_kernel,
        shape((block_rows, cols), F32),
        [HBM, VMEM],
        [weight, rows],
        streamed_scratch(weight),
    )
    own_low = call(low_kernel, shape((block_rows, width), F32), [VMEM] * 2, [maps, rows])

    def masked(low, place):
        slot = lax.dynamic_slice_in_dim(slot_all, place, block_rows, 0)[:, None]
        zero = jnp.zeros((), F32)
        first = jnp.where(slot == z, low[:, :rank_half], zero)
        return first + jnp.where(slot == z + 1 - 2 * (z % 2), low[:, rank_half:], zero)

    own_low = masked(own_low, z * block_rows)
    far[0], own_sum, own_low = barrier((far[0], own_sum, own_low))

    def parted(begins, pieces, helds):
        return call(
            functools.partial(part_kernel, begins),
            [shape((half, cols), F32), shape((half, cols), BF16)] * len(begins),
            [SMEM, HBM] + [VMEM] * (2 * len(begins)),
            [flags, weight] + pieces + helds,
            streamed_scratch(weight),
        )

    last = [along(far[0], NEAR)]
    far_rows = [whole(far[0])]
    kept_a, sent_a = parted([0], [far_rows[0]], [own_sum])
    near_sum = call(
        sum_kernel,
        shape((block_rows, cols), F32),
        [HBM, VMEM, VMEM],
        [weight] + [whole(piece) for piece in near],
        streamed_scratch(weight),
    )
    got_a = over_x(sent_a)
    far[1], last[0], near_sum, kept_a, ups, far_rows[0], own_low, maps = barrier(
        (far[1], last[0], near_sum, kept_a, ups, far_rows[0], own_low, maps)
    )

    last.append(along(far[1], NEAR))
    far_rows.append(whole(far[1]))
    far_low = call(low_kernel, shape((block_rows, width), F32), [VMEM] * 3, [maps] + far_rows)
    far_low = masked(far_low, (z + 2 - 4 * (z // 2)) * block_rows)
    low = jnp.where(home, own_low, far_low) + over_x(jnp.where(home, far_low, own_low))
    low = low + along(low, FAR)

    kept_b, sent_b, kept_c, sent_c = parted(
        [half, 0], [far_rows[1], whole(last[0])], [own_sum, near_sum]
    )
    got_b, got_c = over_x(sent_b), over_x(sent_c)
    last[1], got_a, kept_b, got_b, kept_c, got_c, low, near_sum = barrier(
        (last[1], got_a, kept_b, got_b, kept_c, got_c, low, near_sum)
    )

    kept_d, sent_d = call(
        end_kernel,
        [shape((half, cols), F32), shape((half, cols), BF16)],
        [SMEM] + [VMEM] * 3,
        [flags, weight, whole(last[1]), near_sum],
    )
    low_other, sent_d = barrier((along(low, NEAR), sent_d))
    got_d = over_x(sent_d)
    low = jnp.where(odd, jnp.concatenate([low_other, low]), jnp.concatenate([low, low_other]))
    low_other = over_core(low)
    low = jnp.where(
        c == 0,
        jnp.concatenate([low, low_other], axis=1),
        jnp.concatenate([low_other, low], axis=1),
    )
    start = x * own
    slot = lax.dynamic_slice_in_dim(slot_all, start, own, 0)
    rank = lax.dynamic_slice_in_dim(live_all, start, own, 0)
    spread = low_rank_weights(low, slot, rank, slots, width)
    return call(
        final_kernel,
        shape(residual.shape, BF16),
        [SMEM] + [VMEM] * 11,
        [flags, residual, spread, ups.reshape(slots * width, cols)]
        + [kept_a, got_a, kept_b, got_b, kept_c, got_c, kept_d, got_d],
    )


def shards(rows, residual, weight, down, up, tenant, entry, live):
    sizes = [lax.axis_size(name) for name in ("groups", "blk", "split", "sub")]
    plan = line if sizes == [2, 4, 2, 2] and down.shape[0] == 1 else general
    return plan(rows, residual, weight, down, up, tenant, entry, live)


def solution(mesh):
    in_specs = (
        P(("groups", "blk"), "split"),
        P(("groups", "split"), ("blk", "sub")),
        P("split", ("blk", "sub")),
        P("blk", None, "split"),
        P("split", None, ("blk", "sub")),
        P("groups"),
        P(),
        P(),
    )
    out_specs = P(("groups", "split"), ("blk", "sub"))
    return jax.shard_map(shards, mesh=mesh, in_specs=in_specs, out_specs=out_specs, check_vma=False)
```

```python
import jax
import jax.numpy as jnp
from jax import lax
from jax.sharding import PartitionSpec as P

F32 = jnp.float32
BF16 = jnp.bfloat16


def low_rank_weights(low, slot, live, slots, rank_width):
    kept = jnp.arange(rank_width, dtype=jnp.int32)[None, :] < live[:, None]
    scaling = rank_width / live.astype(F32)
    scaled = jnp.where(kept, low * scaling[:, None], jnp.zeros((), F32)).astype(BF16)
    hot = slot[:, None] == jnp.arange(slots, dtype=jnp.int32)[None, :]
    spread = jnp.where(hot[:, :, None], scaled[:, None, :], jnp.zeros((), BF16))
    return spread.reshape(low.shape[0], slots * rank_width)


def tables(tenant, entry, live):
    ids = jnp.arange(entry.shape[0], dtype=jnp.int32)
    hot = (tenant[:, None] == ids[None, :]).astype(jnp.int32)
    return jnp.sum(hot * entry[None, :], axis=1), jnp.sum(hot * live[None, :], axis=1)


def general(rows, residual, weight, down, up, tenant, entry, live):
    own = residual.shape[0]
    cols = weight.shape[1]
    width = down.shape[1]
    slots = entry.shape[0]
    slot_all, live_all = tables(tenant, entry, live)
    part = rows.shape[0] // lax.axis_size("sub")
    mine = lax.dynamic_slice_in_dim(rows, lax.axis_index("sub") * part, part, 0)
    halves = lax.all_gather(lax.all_gather(mine, "blk", axis=0), "sub", axis=1)
    full = halves.reshape(-1, rows.shape[1])
    base = jnp.dot(full, weight, preferred_element_type=F32)
    low = lax.dot_general(
        full, down.reshape(-1, down.shape[2]), (((1,), (1,)), ((), ())), preferred_element_type=F32
    )
    held = down.shape[0]
    places = lax.axis_index("blk") * held + jnp.arange(held, dtype=jnp.int32)
    here = slot_all[:, None] == places[None, :]
    low = jnp.sum(
        jnp.where(here[:, :, None], low.reshape(-1, held, width), jnp.zeros((), F32)), axis=1
    )
    low = lax.psum(lax.psum_scatter(low, "split", scatter_dimension=0, tiled=True), "blk")
    base = lax.psum_scatter(base, "split", scatter_dimension=0, tiled=True)
    start = lax.axis_index("split") * own
    spread = low_rank_weights(
        low,
        lax.dynamic_slice_in_dim(slot_all, start, own, 0),
        lax.dynamic_slice_in_dim(live_all, start, own, 0),
        slots,
        width,
    )
    ups = lax.all_gather(up, "split", axis=0, tiled=True).reshape(slots * width, cols)
    lora = jnp.dot(spread, ups, preferred_element_type=F32)
    return (residual.astype(F32) + base + lora).astype(BF16)


SWAP = [(0, 1), (1, 0)]
NEAR = [(0, 1), (1, 0), (2, 3), (3, 2)]
FAR = [(0, 2), (2, 0), (1, 3), (3, 1)]


def line(rows, residual, weight, down, up, tenant, entry, live):
    z, x, c = lax.axis_index("blk"), lax.axis_index("split"), lax.axis_index("sub")
    block_rows = rows.shape[0]
    width = down.shape[1]
    own, cols = residual.shape
    slots = entry.shape[0]
    home = (z // 2) == x
    odd = z % 2 == 1
    half, step = block_rows // 2, block_rows // 4
    barrier = lax.optimization_barrier

    def over_core(value):
        return lax.ppermute(value, "sub", SWAP)

    def over_x(value):
        return lax.ppermute(value, "split", SWAP)

    def along(value, pairs):
        return lax.ppermute(value, "blk", pairs)

    def product(block):
        return jnp.dot(block, weight, preferred_element_type=F32)

    def low_rank(block):
        return lax.dot_general(
            block, down[0], (((1,), (1,)), ((), ())), preferred_element_type=F32
        )

    def joined(piece, other):
        return jnp.where(
            c == 0, jnp.concatenate([piece, other]), jnp.concatenate([other, piece])
        )

    def whole(piece):
        return joined(piece, over_core(piece))

    def in_order(first, second):
        return jnp.where(
            odd, jnp.concatenate([second, first]), jnp.concatenate([first, second])
        )

    def exchange(near_sum, far_sum):
        got = over_x(jnp.where(home, far_sum, near_sum).astype(BF16))
        return jnp.where(home, near_sum, far_sum), got

    slot_all, live_all = tables(tenant, entry, live)
    slot = lax.dynamic_slice_in_dim(slot_all, x * own, own, 0)
    rank = lax.dynamic_slice_in_dim(live_all, x * own, own, 0)

    mine = lax.dynamic_slice_in_dim(rows, c * half, half, 0)
    near, far = along(mine, NEAR), along(mine, FAR)
    up_other = over_x(up)
    ups = jnp.where(x == 0, jnp.concatenate([up, up_other]), jnp.concatenate([up_other, up]))
    own_sum, own_low = product(rows), low_rank(rows)
    near, far, own_sum, own_low, ups = barrier((near, far, own_sum, own_low, ups))

    last = along(far, NEAR)

    def doubled(piece):
        return joined(
            piece, jnp.concatenate([over_core(piece[:step]), over_core(piece[step:])])
        )

    far = doubled(far)
    far_sum, far_low = product(far), low_rank(far)
    kept, got = exchange(own_sum, far_sum)
    first = kept + got.astype(F32)
    near = doubled(near)
    near_sum, near_low = product(near), low_rank(near)
    last, first, far_low, near_sum, near_low = barrier((last, first, far_low, near_sum, near_low))

    pieces = [whole(last[:step]), whole(last[step:])]
    last_low = low_rank(jnp.concatenate(pieces)).reshape(2, 2, step, width)
    last_low = last_low.transpose(1, 0, 2, 3).reshape(block_rows, width)
    near_low, far_low = in_order(own_low, near_low), in_order(far_low, last_low)
    low = jnp.where(home, near_low, far_low) + over_x(jnp.where(home, far_low, near_low))
    low = jnp.where((slot == z)[:, None], low, jnp.zeros((), F32))
    near_parts = near_sum.reshape(2, 2, step, cols)
    second = []
    for p, pairs in enumerate((NEAR, FAR)):
        kept, got = exchange(near_parts[:, p].reshape(half, cols), product(pieces[p]))
        low, kept, got = barrier((low, kept, got)) if p else (low, kept, got)
        low = low + along(low, pairs)
        second.append((kept + got.astype(F32)).reshape(2, step, cols))
    second = jnp.stack(second, axis=1).reshape(block_rows, cols)
    spread = low_rank_weights(low, slot, rank, slots, width)
    lora = jnp.dot(spread, ups.reshape(slots * width, cols), preferred_element_type=F32)
    return (residual.astype(F32) + in_order(first, second) + lora).astype(BF16)


def shards(rows, residual, weight, down, up, tenant, entry, live):
    sizes = [lax.axis_size(name) for name in ("blk", "split", "sub")]
    plan = line if sizes == [4, 2, 2] and down.shape[0] == 1 else general
    return plan(rows, residual, weight, down, up, tenant, entry, live)


def solution(mesh):
    in_specs = (
        P(("groups", "blk"), "split"),
        P(("groups", "split"), ("blk", "sub")),
        P("split", ("blk", "sub")),
        P("blk", None, "split"),
        P("split", None, ("blk", "sub")),
        P("groups"),
        P(),
        P(),
    )
    out_specs = P(("groups", "split"), ("blk", "sub"))
    return jax.shard_map(shards, mesh=mesh, in_specs=in_specs, out_specs=out_specs, check_vma=False)
```

```python
import jax
import jax.numpy as jnp
from jax import lax
from jax.experimental import pallas as pl
from jax.experimental.pallas import tpu as pltpu
from jax.sharding import PartitionSpec as P

F32 = jnp.float32
BF16 = jnp.bfloat16


def low_rank_weights(low, slot, live, slots, rank_width):
    kept = jnp.arange(rank_width, dtype=jnp.int32)[None, :] < live[:, None]
    scaling = rank_width / live.astype(F32)
    scaled = jnp.where(kept, low * scaling[:, None], jnp.zeros((), F32)).astype(BF16)
    hot = slot[:, None] == jnp.arange(slots, dtype=jnp.int32)[None, :]
    spread = jnp.where(hot[:, :, None], scaled[:, None, :], jnp.zeros((), BF16))
    return spread.reshape(low.shape[0], slots * rank_width)


def tables(tenant, entry, live):
    ids = jnp.arange(entry.shape[0], dtype=jnp.int32)
    hot = (tenant[:, None] == ids[None, :]).astype(jnp.int32)
    return jnp.sum(hot * entry[None, :], axis=1), jnp.sum(hot * live[None, :], axis=1)


def general(rows, residual, weight, down, up, tenant, entry, live):
    own = residual.shape[0]
    cols = weight.shape[1]
    width = down.shape[1]
    slots = entry.shape[0]
    slot_all, live_all = tables(tenant, entry, live)
    part = rows.shape[0] // lax.axis_size("sub")
    mine = lax.dynamic_slice_in_dim(rows, lax.axis_index("sub") * part, part, 0)
    halves = lax.all_gather(lax.all_gather(mine, "blk", axis=0), "sub", axis=1)
    full = halves.reshape(-1, rows.shape[1])
    base = jnp.dot(full, weight, preferred_element_type=F32)
    low = lax.dot_general(
        full, down.reshape(-1, down.shape[2]), (((1,), (1,)), ((), ())), preferred_element_type=F32
    )
    held = down.shape[0]
    places = lax.axis_index("blk") * held + jnp.arange(held, dtype=jnp.int32)
    here = slot_all[:, None] == places[None, :]
    low = jnp.sum(
        jnp.where(here[:, :, None], low.reshape(-1, held, width), jnp.zeros((), F32)), axis=1
    )
    low = lax.psum(lax.psum_scatter(low, "split", scatter_dimension=0, tiled=True), "blk")
    base = lax.psum_scatter(base, "split", scatter_dimension=0, tiled=True)
    start = lax.axis_index("split") * own
    spread = low_rank_weights(
        low,
        lax.dynamic_slice_in_dim(slot_all, start, own, 0),
        lax.dynamic_slice_in_dim(live_all, start, own, 0),
        slots,
        width,
    )
    ups = lax.all_gather(up, "split", axis=0, tiled=True).reshape(slots * width, cols)
    lora = jnp.dot(spread, ups, preferred_element_type=F32)
    return (residual.astype(F32) + base + lora).astype(BF16)


SWAP = [(0, 1), (1, 0)]
NEAR = [(0, 1), (1, 0), (2, 3), (3, 2)]
FAR = [(0, 2), (2, 0), (1, 3), (3, 1)]


def hold_kernel(array_ref, held_ref, sem):
    copy = pltpu.make_async_copy(array_ref, held_ref, sem)
    copy.start()
    copy.wait()


def hold(array):
    return pl.pallas_call(
        hold_kernel,
        out_shape=jax.ShapeDtypeStruct(array.shape, array.dtype),
        in_specs=[pl.BlockSpec(memory_space=pltpu.HBM)],
        out_specs=pl.BlockSpec(memory_space=pltpu.VMEM),
        scratch_shapes=[pltpu.SemaphoreType.DMA],
        compiler_params=pltpu.CompilerParams(vmem_limit_bytes=1024 * 1024),
    )(array)


def line(rows, residual, weight, down, up, tenant, entry, live):
    z, x, c = lax.axis_index("blk"), lax.axis_index("split"), lax.axis_index("sub")
    block_rows = rows.shape[0]
    width = down.shape[1]
    own, cols = residual.shape
    slots = entry.shape[0]
    home = (z // 2) == x
    odd = z % 2 == 1
    half, step = block_rows // 2, block_rows // 4
    barrier = lax.optimization_barrier

    def over_core(value):
        return lax.ppermute(value, "sub", SWAP)

    def over_x(value):
        return lax.ppermute(value, "split", SWAP)

    def along(value, pairs):
        return lax.ppermute(value, "blk", pairs)

    held = hold(weight)

    def product(block):
        return jnp.dot(block, held, preferred_element_type=F32)

    def low_rank(block):
        return lax.dot_general(
            block, down[0], (((1,), (1,)), ((), ())), preferred_element_type=F32
        )

    def joined(piece, other):
        return jnp.where(
            c == 0, jnp.concatenate([piece, other]), jnp.concatenate([other, piece])
        )

    def whole(piece):
        return joined(piece, over_core(piece))

    def in_order(first, second):
        return jnp.where(
            odd, jnp.concatenate([second, first]), jnp.concatenate([first, second])
        )

    def exchange(near_sum, far_sum):
        got = over_x(jnp.where(home, far_sum, near_sum).astype(BF16))
        return jnp.where(home, near_sum, far_sum), got

    slot_all, live_all = tables(tenant, entry, live)
    slot = lax.dynamic_slice_in_dim(slot_all, x * own, own, 0)
    rank = lax.dynamic_slice_in_dim(live_all, x * own, own, 0)

    mine = lax.dynamic_slice_in_dim(rows, c * half, half, 0)
    near, far = along(mine, NEAR), along(mine, FAR)
    up_other = over_x(up)
    ups = jnp.where(x == 0, jnp.concatenate([up, up_other]), jnp.concatenate([up_other, up]))
    own_sum, own_low = product(rows), low_rank(rows)
    near, far, own_sum, own_low, ups = barrier((near, far, own_sum, own_low, ups))

    last = along(far, NEAR)

    def doubled(piece):
        return joined(
            piece, jnp.concatenate([over_core(piece[:step]), over_core(piece[step:])])
        )

    far = doubled(far)
    far_sum, far_low = product(far), low_rank(far)
    kept, got = exchange(own_sum, far_sum)
    first = kept + got.astype(F32)
    near = doubled(near)
    near_sum, near_low = product(near), low_rank(near)
    last, first, far_low, near_sum, near_low = barrier((last, first, far_low, near_sum, near_low))

    pieces = [whole(last[:step]), whole(last[step:])]
    last_low = low_rank(jnp.concatenate(pieces)).reshape(2, 2, step, width)
    last_low = last_low.transpose(1, 0, 2, 3).reshape(block_rows, width)
    near_low, far_low = in_order(own_low, near_low), in_order(far_low, last_low)
    low = jnp.where(home, near_low, far_low) + over_x(jnp.where(home, far_low, near_low))
    low = jnp.where((slot == z)[:, None], low, jnp.zeros((), F32))
    near_parts = near_sum.reshape(2, 2, step, cols)
    second = []
    for p, pairs in enumerate((NEAR, FAR)):
        kept, got = exchange(near_parts[:, p].reshape(half, cols), product(pieces[p]))
        low, kept, got = barrier((low, kept, got)) if p else (low, kept, got)
        low = low + along(low, pairs)
        second.append((kept + got.astype(F32)).reshape(2, step, cols))
    second = jnp.stack(second, axis=1).reshape(block_rows, cols)
    spread = low_rank_weights(low, slot, rank, slots, width)
    lora = jnp.dot(spread, ups.reshape(slots * width, cols), preferred_element_type=F32)
    return (residual.astype(F32) + in_order(first, second) + lora).astype(BF16)


def shards(rows, residual, weight, down, up, tenant, entry, live):
    sizes = [lax.axis_size(name) for name in ("blk", "split", "sub")]
    plan = line if sizes == [4, 2, 2] and down.shape[0] == 1 else general
    return plan(rows, residual, weight, down, up, tenant, entry, live)


def solution(mesh):
    in_specs = (
        P(("groups", "blk"), "split"),
        P(("groups", "split"), ("blk", "sub")),
        P("split", ("blk", "sub")),
        P("blk", None, "split"),
        P("split", None, ("blk", "sub")),
        P("groups"),
        P(),
        P(),
    )
    out_specs = P(("groups", "split"), ("blk", "sub"))
    return jax.shard_map(shards, mesh=mesh, in_specs=in_specs, out_specs=out_specs, check_vma=False)
```

```python
import jax
import jax.numpy as jnp
from jax import lax
from jax.experimental import pallas as pl
from jax.experimental.pallas import tpu as pltpu
from jax.sharding import PartitionSpec as P

F32 = jnp.float32
BF16 = jnp.bfloat16


def low_rank_weights(low, slot, live, slots, rank_width):
    kept = jnp.arange(rank_width, dtype=jnp.int32)[None, :] < live[:, None]
    scaling = rank_width / live.astype(F32)
    scaled = jnp.where(kept, low * scaling[:, None], jnp.zeros((), F32)).astype(BF16)
    hot = slot[:, None] == jnp.arange(slots, dtype=jnp.int32)[None, :]
    spread = jnp.where(hot[:, :, None], scaled[:, None, :], jnp.zeros((), BF16))
    return spread.reshape(low.shape[0], slots * rank_width)


def tables(tenant, entry, live):
    ids = jnp.arange(entry.shape[0], dtype=jnp.int32)
    hot = (tenant[:, None] == ids[None, :]).astype(jnp.int32)
    return jnp.sum(hot * entry[None, :], axis=1), jnp.sum(hot * live[None, :], axis=1)


def general(rows, residual, weight, down, up, tenant, entry, live):
    own = residual.shape[0]
    cols = weight.shape[1]
    width = down.shape[1]
    slots = entry.shape[0]
    slot_all, live_all = tables(tenant, entry, live)
    part = rows.shape[0] // lax.axis_size("sub")
    mine = lax.dynamic_slice_in_dim(rows, lax.axis_index("sub") * part, part, 0)
    halves = lax.all_gather(lax.all_gather(mine, "blk", axis=0), "sub", axis=1)
    full = halves.reshape(-1, rows.shape[1])
    base = jnp.dot(full, weight, preferred_element_type=F32)
    low = lax.dot_general(
        full, down.reshape(-1, down.shape[2]), (((1,), (1,)), ((), ())), preferred_element_type=F32
    )
    held = down.shape[0]
    places = lax.axis_index("blk") * held + jnp.arange(held, dtype=jnp.int32)
    here = slot_all[:, None] == places[None, :]
    low = jnp.sum(
        jnp.where(here[:, :, None], low.reshape(-1, held, width), jnp.zeros((), F32)), axis=1
    )
    low = lax.psum(lax.psum_scatter(low, "split", scatter_dimension=0, tiled=True), "blk")
    base = lax.psum_scatter(base, "split", scatter_dimension=0, tiled=True)
    start = lax.axis_index("split") * own
    spread = low_rank_weights(
        low,
        lax.dynamic_slice_in_dim(slot_all, start, own, 0),
        lax.dynamic_slice_in_dim(live_all, start, own, 0),
        slots,
        width,
    )
    ups = lax.all_gather(up, "split", axis=0, tiled=True).reshape(slots * width, cols)
    lora = jnp.dot(spread, ups, preferred_element_type=F32)
    return (residual.astype(F32) + base + lora).astype(BF16)


SWAP = [(0, 1), (1, 0)]
NEAR = [(0, 1), (1, 0), (2, 3), (3, 2)]
FAR = [(0, 2), (2, 0), (1, 3), (3, 1)]
VMEM = pl.BlockSpec(memory_space=pltpu.VMEM)
SMEM = pl.BlockSpec(memory_space=pltpu.SMEM)
HBM = pl.BlockSpec(memory_space=pltpu.HBM)
COST = pl.CostEstimate(flops=0, bytes_accessed=0, transcendentals=0)
PARAMS = pltpu.CompilerParams(vmem_limit_bytes=50 * 1024 * 1024)


def shape(dims, dtype):
    return jax.ShapeDtypeStruct(dims, dtype)


def dot(a, b):
    return jnp.dot(a, b, preferred_element_type=F32)


def call(kernel, outs, in_specs, operands, scratch=()):
    return pl.pallas_call(
        kernel,
        out_shape=outs,
        in_specs=in_specs,
        out_specs=jax.tree.map(lambda _: VMEM, outs),
        scratch_shapes=scratch,
        compiler_params=PARAMS,
        cost_estimate=COST,
    )(*operands)


def column_tiles(cols):
    tile = 256 if cols % 256 == 0 else cols
    return [slice(at, at + tile) for at in range(0, cols, tile)]


def streamed_scratch(weight):
    return [
        pltpu.VMEM(weight.shape, weight.dtype),
        pltpu.SemaphoreType.DMA((len(column_tiles(weight.shape[1])),)),
    ]


def streaming(weight_ref, tiles_ref, sems):
    tiles = column_tiles(weight_ref.shape[1])
    copies = [
        pltpu.make_async_copy(weight_ref.at[:, tile], tiles_ref.at[:, tile], sems.at[i])
        for i, tile in enumerate(tiles)
    ]
    for copy in copies:
        copy.start()

    def come():
        for copy, tile in zip(copies, tiles):
            copy.wait()
            yield tile, tiles_ref[:, tile]

    return come()


def joined(flags_ref, mine, other):
    first = flags_ref[1] == 0
    return jnp.concatenate([jnp.where(first, mine, other), jnp.where(first, other, mine)])


def low_product(rows, down_ref):
    return lax.dot_general(
        rows, down_ref[...], (((1,), (1,)), ((), ())), preferred_element_type=F32
    )


def part(flags_ref, held, value, keep_ref, send_ref, tile):
    home = flags_ref[0] == 1
    keep_ref[:, tile] = jnp.where(home, held, value)
    send_ref[:, tile] = jnp.where(home, value, held).astype(BF16)


def own_kernel(weight_ref, down_ref, rows_ref, sum_ref, low_ref, tiles_ref, sems):
    stream = streaming(weight_ref, tiles_ref, sems)
    rows = rows_ref[...]
    low_ref[...] = low_product(rows, down_ref)
    for tile, weights in stream:
        sum_ref[:, tile] = dot(rows, weights)


def far_kernel(
    flags_ref, weight_ref, down_ref, held_ref, mine_ref, first_ref, second_ref,
    keep_ref, send_ref, keep_more_ref, send_more_ref, low_ref, tiles_ref, sems,
):
    stream = streaming(weight_ref, tiles_ref, sems)
    other = jnp.concatenate([first_ref[...], second_ref[...]])
    rows = joined(flags_ref, mine_ref[...], other)
    low_ref[...] = low_product(rows, down_ref)
    half = keep_ref.shape[0]
    for tile, weights in stream:
        value = dot(rows, weights)
        part(flags_ref, held_ref[:half, tile], value[:half], keep_ref, send_ref, tile)
        part(flags_ref, held_ref[half:, tile], value[half:], keep_more_ref, send_more_ref, tile)


def near_kernel(
    flags_ref, weight_ref, down_ref, mine_ref, first_ref, second_ref, last_ref, third_ref,
    fourth_ref, keep_ref, send_ref, hold_ref, low_ref, tiles_ref, sems,
):
    stream = streaming(weight_ref, tiles_ref, sems)
    other = jnp.concatenate([first_ref[...], second_ref[...]])
    near = joined(flags_ref, mine_ref[...], other)
    last = joined(flags_ref, last_ref[...], jnp.concatenate([third_ref[...], fourth_ref[...]]))
    rows = jnp.concatenate([near, last])
    low_ref[...] = low_product(rows, down_ref)
    step = last_ref.shape[0]
    for tile, weights in stream:
        value = dot(rows, weights)
        held = jnp.concatenate([value[:step], value[2 * step : 3 * step]])
        part(flags_ref, held, value[4 * step :], keep_ref, send_ref, tile)
        hold_ref[:, tile] = jnp.concatenate(
            [value[step : 2 * step], value[3 * step : 4 * step]]
        )


def last_kernel(
    flags_ref, weight_ref, down_ref, held_ref, mine_ref, first_ref, second_ref,
    keep_ref, send_ref, low_ref, tiles_ref, sems,
):
    stream = streaming(weight_ref, tiles_ref, sems)
    other = jnp.concatenate([first_ref[...], second_ref[...]])
    rows = joined(flags_ref, mine_ref[...], other)
    low_ref[...] = low_product(rows, down_ref)
    for tile, weights in stream:
        part(flags_ref, held_ref[:, tile], dot(rows, weights), keep_ref, send_ref, tile)


def final_kernel(flags_ref, residual_ref, low_ref, low_got_ref, factor_ref, ups_ref, *refs):
    *parts, out_ref = refs
    low = low_ref[...] + low_got_ref[...]
    lora = dot((low * factor_ref[0]).astype(BF16), ups_ref[0])
    for slot in range(1, ups_ref.shape[0]):
        lora += dot((low * factor_ref[slot]).astype(BF16), ups_ref[slot])
    odd = flags_ref[2] == 1
    sums = [keep[...] + got[...].astype(F32) for keep, got in zip(parts[::2], parts[1::2])]
    step = sums[2].shape[0] // 2
    first = jnp.concatenate(sums[:2])
    second = jnp.concatenate(
        [sums[2][:step], sums[3][:step], sums[2][step:], sums[3][step:]]
    )
    block = first.shape[0]
    for at, base in ((0, jnp.where(odd, second, first)), (block, jnp.where(odd, first, second))):
        here = slice(at, at + block)
        out_ref[here, :] = (residual_ref[here, :].astype(F32) + base + lora[here]).astype(BF16)


def line(rows, residual, weight, down, up, tenant, entry, live):
    z, x, c = lax.axis_index("blk"), lax.axis_index("split"), lax.axis_index("sub")
    block_rows = rows.shape[0]
    width = down.shape[1]
    own, cols = residual.shape
    slots = entry.shape[0]
    home = (z // 2) == x
    odd = z % 2 == 1
    half, step = block_rows // 2, block_rows // 4
    barrier = lax.optimization_barrier

    def over_core(value):
        return lax.ppermute(value, "sub", SWAP)

    def over_x(value):
        return lax.ppermute(value, "split", SWAP)

    def along(value, pairs):
        return lax.ppermute(value, "blk", pairs)

    def over_core_in_two(piece):
        count = piece.shape[0] // 2
        return [over_core(piece[:count]), over_core(piece[count:])]

    def in_order(first, second):
        return jnp.where(
            odd, jnp.concatenate([second, first]), jnp.concatenate([first, second])
        )

    def parted(count):
        return [shape((count, cols), F32), shape((count, cols), BF16)]

    def lows(count):
        return [shape((count, width), F32)]

    slot_all, live_all = tables(tenant, entry, live)
    slot = lax.dynamic_slice_in_dim(slot_all, x * own, own, 0)
    rank = lax.dynamic_slice_in_dim(live_all, x * own, own, 0)

    flags = jnp.stack([home, c, odd]).astype(jnp.int32)
    kept = jnp.arange(width, dtype=jnp.int32)[None, :] < rank[:, None]
    scaling = jnp.where(kept, (width / rank.astype(F32))[:, None], jnp.zeros((), F32))
    hot = slot[None, :] == jnp.arange(slots, dtype=jnp.int32)[:, None]
    factor = jnp.where(hot[:, :, None], scaling[None], jnp.zeros((), F32))

    mine = lax.dynamic_slice_in_dim(rows, c * half, half, 0)
    near, far = along(mine, NEAR), along(mine, FAR)
    up_other = over_x(up)
    ups = jnp.where(x == 0, jnp.concatenate([up, up_other]), jnp.concatenate([up_other, up]))
    own_sum, own_low = call(
        own_kernel,
        [shape((block_rows, cols), F32)] + lows(block_rows),
        [HBM, VMEM, VMEM],
        [weight, down[0], rows],
        streamed_scratch(weight),
    )
    near, far, own_sum, own_low, ups, factor = barrier((near, far, own_sum, own_low, ups, factor))

    last = [along(far[:step], NEAR), along(far[step:], NEAR)]
    kept_a, sent_a, kept_b, sent_b, far_low = call(
        far_kernel,
        parted(half) * 2 + lows(block_rows),
        [SMEM, HBM] + [VMEM] * 5,
        [flags, weight, down[0], own_sum, far] + over_core_in_two(far),
        streamed_scratch(weight),
    )
    got_a, got_b = over_x(sent_a), over_x(sent_b)
    last[0], kept_a = barrier((last[0], kept_a))

    kept_c, sent_c, hold, near_low = call(
        near_kernel,
        parted(half) + [shape((half, cols), F32)] + lows(block_rows + half),
        [SMEM, HBM] + [VMEM] * 7,
        [flags, weight, down[0], near] + over_core_in_two(near)
        + [last[0]] + over_core_in_two(last[0]),
        streamed_scratch(weight),
    )
    got_c = over_x(sent_c)
    last[1], hold, got_a, got_b, near_low = barrier((last[1], hold, got_a, got_b, near_low))

    others = over_core_in_two(last[1])
    others, got_c = barrier((others, got_c))
    kept_d, sent_d, last_low = call(
        last_kernel,
        parted(half) + lows(half),
        [SMEM, HBM] + [VMEM] * 5,
        [flags, weight, down[0], hold, last[1]] + others,
        streamed_scratch(weight),
    )
    got_d = over_x(sent_d)

    pair = [near_low[block_rows:], last_low]
    last_low = jnp.concatenate([low[at : at + step] for at in (0, step) for low in pair])
    near_low, far_low = in_order(own_low, near_low[:block_rows]), in_order(far_low, last_low)
    low = jnp.where(home, near_low, far_low) + over_x(jnp.where(home, far_low, near_low))
    low = jnp.where((slot == z)[:, None], low, jnp.zeros((), F32))
    low = low + along(low, NEAR)
    low, got_d = barrier((low, got_d))
    parts = [kept_a, got_a, kept_b, got_b, kept_c, got_c, kept_d, got_d]
    return call(
        final_kernel,
        shape(residual.shape, BF16),
        [SMEM] + [VMEM] * 13,
        [flags, residual, low, along(low, FAR), factor, ups] + parts,
    )


def shards(rows, residual, weight, down, up, tenant, entry, live):
    sizes = [lax.axis_size(name) for name in ("blk", "split", "sub")]
    plan = line if sizes == [4, 2, 2] and down.shape[0] == 1 else general
    return plan(rows, residual, weight, down, up, tenant, entry, live)


def solution(mesh):
    in_specs = (
        P(("groups", "blk"), "split"),
        P(("groups", "split"), ("blk", "sub")),
        P("split", ("blk", "sub")),
        P("blk", None, "split"),
        P("split", None, ("blk", "sub")),
        P("groups"),
        P(),
        P(),
    )
    out_specs = P(("groups", "split"), ("blk", "sub"))
    return jax.shard_map(shards, mesh=mesh, in_specs=in_specs, out_specs=out_specs, check_vma=False)
```

```python
import jax
import jax.numpy as jnp
from jax import lax
from jax.experimental import pallas as pl
from jax.experimental.pallas import tpu as pltpu
from jax.sharding import PartitionSpec as P

F32 = jnp.float32
BF16 = jnp.bfloat16


def low_rank_weights(low, slot, live, slots, rank_width):
    kept = jnp.arange(rank_width, dtype=jnp.int32)[None, :] < live[:, None]
    scaling = rank_width / live.astype(F32)
    scaled = jnp.where(kept, low * scaling[:, None], jnp.zeros((), F32)).astype(BF16)
    hot = slot[:, None] == jnp.arange(slots, dtype=jnp.int32)[None, :]
    spread = jnp.where(hot[:, :, None], scaled[:, None, :], jnp.zeros((), BF16))
    return spread.reshape(low.shape[0], slots * rank_width)


def tables(tenant, entry, live):
    ids = jnp.arange(entry.shape[0], dtype=jnp.int32)
    hot = (tenant[:, None] == ids[None, :]).astype(jnp.int32)
    return jnp.sum(hot * entry[None, :], axis=1), jnp.sum(hot * live[None, :], axis=1)


def general(rows, residual, weight, down, up, tenant, entry, live):
    own = residual.shape[0]
    cols = weight.shape[1]
    width = down.shape[1]
    slots = entry.shape[0]
    slot_all, live_all = tables(tenant, entry, live)
    part = rows.shape[0] // lax.axis_size("sub")
    mine = lax.dynamic_slice_in_dim(rows, lax.axis_index("sub") * part, part, 0)
    halves = lax.all_gather(lax.all_gather(mine, "blk", axis=0), "sub", axis=1)
    full = halves.reshape(-1, rows.shape[1])
    base = jnp.dot(full, weight, preferred_element_type=F32)
    low = lax.dot_general(
        full, down.reshape(-1, down.shape[2]), (((1,), (1,)), ((), ())), preferred_element_type=F32
    )
    held = down.shape[0]
    places = lax.axis_index("blk") * held + jnp.arange(held, dtype=jnp.int32)
    here = slot_all[:, None] == places[None, :]
    low = jnp.sum(
        jnp.where(here[:, :, None], low.reshape(-1, held, width), jnp.zeros((), F32)), axis=1
    )
    low = lax.psum(lax.psum_scatter(low, "split", scatter_dimension=0, tiled=True), "blk")
    base = lax.psum_scatter(base, "split", scatter_dimension=0, tiled=True)
    start = lax.axis_index("split") * own
    spread = low_rank_weights(
        low,
        lax.dynamic_slice_in_dim(slot_all, start, own, 0),
        lax.dynamic_slice_in_dim(live_all, start, own, 0),
        slots,
        width,
    )
    ups = lax.all_gather(up, "split", axis=0, tiled=True).reshape(slots * width, cols)
    lora = jnp.dot(spread, ups, preferred_element_type=F32)
    return (residual.astype(F32) + base + lora).astype(BF16)


SWAP = [(0, 1), (1, 0)]
NEAR = [(0, 1), (1, 0), (2, 3), (3, 2)]
FAR = [(0, 2), (2, 0), (1, 3), (3, 1)]
VMEM = pl.BlockSpec(memory_space=pltpu.VMEM)
SMEM = pl.BlockSpec(memory_space=pltpu.SMEM)
HBM = pl.BlockSpec(memory_space=pltpu.HBM)
COST = pl.CostEstimate(flops=0, bytes_accessed=0, transcendentals=0)
PARAMS = pltpu.CompilerParams(vmem_limit_bytes=16 * 1024 * 1024)
FROM_HBM = pltpu.CompilerParams(vmem_limit_bytes=40 * 1024 * 1024)


def shape(dims, dtype):
    return jax.ShapeDtypeStruct(dims, dtype)


def dot(a, b):
    return jnp.dot(a, b, preferred_element_type=F32)


def call(kernel, outs, in_specs, operands, scratch=(), params=PARAMS):
    return pl.pallas_call(
        kernel,
        out_shape=outs,
        in_specs=in_specs,
        out_specs=jax.tree.map(lambda _: VMEM, outs),
        scratch_shapes=scratch,
        compiler_params=params,
        cost_estimate=COST,
    )(*operands)


def column_tiles(cols):
    tile = 256 if cols % 256 == 0 else cols
    return [slice(at, at + tile) for at in range(0, cols, tile)]


def joined(flags_ref, mine, other):
    first = flags_ref[1] == 0
    return jnp.concatenate([jnp.where(first, mine, other), jnp.where(first, other, mine)])


def low_product(rows, down_ref):
    return lax.dot_general(
        rows, down_ref[...], (((1,), (1,)), ((), ())), preferred_element_type=F32
    )


def part(flags_ref, held, value, keep_ref, send_ref, tile):
    home = flags_ref[0] == 1
    keep_ref[:, tile] = jnp.where(home, held, value)
    send_ref[:, tile] = jnp.where(home, value, held).astype(BF16)


def own_kernel(
    weight_ref, down_ref, rows_ref, held_ref, sum_ref, low_ref, sems
):
    tiles = column_tiles(weight_ref.shape[1])
    copies = [
        pltpu.make_async_copy(weight_ref.at[:, tile], held_ref.at[:, tile], sems.at[i])
        for i, tile in enumerate(tiles)
    ]
    for copy in copies:
        copy.start()
    rows = rows_ref[...]
    low_ref[...] = low_product(rows, down_ref)
    for copy, tile in zip(copies, tiles):
        copy.wait()
        sum_ref[:, tile] = dot(rows, held_ref[:, tile])


def far_kernel(
    flags_ref, weight_ref, down_ref, held_ref, mine_ref, first_ref, second_ref,
    keep_ref, send_ref, keep_more_ref, send_more_ref, low_ref,
):
    other = jnp.concatenate([first_ref[...], second_ref[...]])
    rows = joined(flags_ref, mine_ref[...], other)
    low_ref[...] = low_product(rows, down_ref)
    half = keep_ref.shape[0]
    for tile in column_tiles(weight_ref.shape[1]):
        value = dot(rows, weight_ref[:, tile])
        part(flags_ref, held_ref[:half, tile], value[:half], keep_ref, send_ref, tile)
        part(flags_ref, held_ref[half:, tile], value[half:], keep_more_ref, send_more_ref, tile)


def near_kernel(
    flags_ref, weight_ref, down_ref, mine_ref, first_ref, second_ref, last_ref, third_ref,
    fourth_ref, keep_ref, send_ref, hold_ref, low_ref,
):
    other = jnp.concatenate([first_ref[...], second_ref[...]])
    near = joined(flags_ref, mine_ref[...], other)
    last = joined(flags_ref, last_ref[...], jnp.concatenate([third_ref[...], fourth_ref[...]]))
    rows = jnp.concatenate([near, last])
    low_ref[...] = low_product(rows, down_ref)
    step = last_ref.shape[0]
    for tile in column_tiles(weight_ref.shape[1]):
        value = dot(rows, weight_ref[:, tile])
        held = jnp.concatenate([value[:step], value[2 * step : 3 * step]])
        part(flags_ref, held, value[4 * step :], keep_ref, send_ref, tile)
        hold_ref[:, tile] = jnp.concatenate(
            [value[step : 2 * step], value[3 * step : 4 * step]]
        )


def last_kernel(
    flags_ref, weight_ref, down_ref, held_ref, own_low, far_low, near_low, mine_ref, first_ref,
    second_ref, keep_ref, send_ref, low_keep_ref, low_send_ref,
):
    other = jnp.concatenate([first_ref[...], second_ref[...]])
    rows = joined(flags_ref, mine_ref[...], other)
    low = low_product(rows, down_ref)
    block, width = own_low.shape
    step = mine_ref.shape[0]
    last_low = jnp.concatenate(
        [
            near_low[block : block + step], low[:step],
            near_low[block + step :], low[step:],
        ]
    )
    odd, home = flags_ref[2] == 1, flags_ref[0] == 1
    near = own_low[...], near_low[:block]
    far = far_low[...], last_low
    for side, here in ((0, slice(0, width)), (1, slice(width, 2 * width))):
        near_side = jnp.where(odd, near[1 - side], near[side])
        far_side = jnp.where(odd, far[1 - side], far[side])
        low_keep_ref[:, here] = jnp.where(home, near_side, far_side)
        low_send_ref[:, here] = jnp.where(home, far_side, near_side)
    for tile in column_tiles(weight_ref.shape[1]):
        value = dot(rows, weight_ref[:, tile])
        part(flags_ref, held_ref[:, tile], value, keep_ref, send_ref, tile)


def final_kernel(flags_ref, residual_ref, scaled_ref, scaled_got_ref, hot_ref, ups_ref, *refs):
    *parts, out_ref = refs
    scaled = scaled_ref[...] + scaled_got_ref[...]
    width = ups_ref.shape[1]
    scaled = jnp.concatenate([scaled[:, :width], scaled[:, width:]])
    lora = dot(scaled * hot_ref[0], ups_ref[0])
    for slot in range(1, ups_ref.shape[0]):
        lora += dot(scaled * hot_ref[slot], ups_ref[slot])
    odd = flags_ref[2] == 1
    sums = [keep[...] + got[...].astype(F32) for keep, got in zip(parts[::2], parts[1::2])]
    step = sums[2].shape[0] // 2
    first = jnp.concatenate(sums[:2])
    second = jnp.concatenate(
        [sums[2][:step], sums[3][:step], sums[2][step:], sums[3][step:]]
    )
    block = first.shape[0]
    for at, base in ((0, jnp.where(odd, second, first)), (block, jnp.where(odd, first, second))):
        here = slice(at, at + block)
        out_ref[here, :] = (residual_ref[here, :].astype(F32) + base + lora[here]).astype(BF16)


def line(rows, residual, weight, down, up, tenant, entry, live):
    z, x, c = lax.axis_index("blk"), lax.axis_index("split"), lax.axis_index("sub")
    block_rows = rows.shape[0]
    width = down.shape[1]
    own, cols = residual.shape
    slots = entry.shape[0]
    home = (z // 2) == x
    odd = z % 2 == 1
    half, step = block_rows // 2, block_rows // 4
    barrier = lax.optimization_barrier

    def over_core(value):
        return lax.ppermute(value, "sub", SWAP)

    def over_x(value):
        return lax.ppermute(value, "split", SWAP)

    def along(value, pairs):
        return lax.ppermute(value, "blk", pairs)

    def over_core_in_two(piece):
        count = piece.shape[0] // 2
        return [over_core(piece[:count]), over_core(piece[count:])]

    def parted(count):
        return [shape((count, cols), F32), shape((count, cols), BF16)]

    def lows(count):
        return [shape((count, width), F32)]

    slot_all, live_all = tables(tenant, entry, live)
    slot = lax.dynamic_slice_in_dim(slot_all, x * own, own, 0)
    rank = lax.dynamic_slice_in_dim(live_all, x * own, own, 0)

    flags = jnp.stack([home, c, odd]).astype(jnp.int32)
    kept = jnp.arange(width, dtype=jnp.int32)[None, :] < rank[:, None]
    scale = jnp.where(kept, (width / rank.astype(F32))[:, None], jnp.zeros((), F32))
    scale = jnp.where((slot == z)[:, None], scale, jnp.zeros((), F32))
    scale = jnp.concatenate([scale[:block_rows], scale[block_rows:]], axis=1)
    hot = slot[None, :] == jnp.arange(slots, dtype=jnp.int32)[:, None]
    hot = jnp.broadcast_to(hot[:, :, None], (slots, own, width)).astype(BF16)

    mine = lax.dynamic_slice_in_dim(rows, c * half, half, 0)
    near, far = along(mine, NEAR), along(mine, FAR)
    up_other = over_x(up)
    ups = jnp.where(x == 0, jnp.concatenate([up, up_other]), jnp.concatenate([up_other, up]))
    held, own_sum, own_low = call(
        own_kernel,
        [shape(weight.shape, BF16), shape((block_rows, cols), F32)] + lows(block_rows),
        [HBM, VMEM, VMEM],
        [weight, down[0], rows],
        [pltpu.SemaphoreType.DMA((len(column_tiles(cols)),))],
        FROM_HBM,
    )
    near, far, own_sum, own_low, ups, hot, scale = barrier(
        (near, far, own_sum, own_low, ups, hot, scale)
    )

    last = [along(far[:step], NEAR), along(far[step:], NEAR)]
    kept_a, sent_a, kept_b, sent_b, far_low = call(
        far_kernel,
        parted(half) * 2 + lows(block_rows),
        [SMEM] + [VMEM] * 6,
        [flags, held, down[0], own_sum, far] + over_core_in_two(far),
    )
    got_a, got_b = over_x(sent_a), over_x(sent_b)
    last[0], kept_a = barrier((last[0], kept_a))

    kept_c, sent_c, hold, near_low = call(
        near_kernel,
        parted(half) + [shape((half, cols), F32)] + lows(block_rows + half),
        [SMEM] + [VMEM] * 8,
        [flags, held, down[0], near] + over_core_in_two(near)
        + [last[0]] + over_core_in_two(last[0]),
    )
    got_c = over_x(sent_c)
    last[1], hold, got_a, got_b, near_low = barrier((last[1], hold, got_a, got_b, near_low))

    kept_d, sent_d, low, low_sent = call(
        last_kernel,
        parted(half) + [shape((block_rows, 2 * width), F32)] * 2,
        [SMEM] + [VMEM] * 9,
        [flags, held, down[0], hold, own_low, far_low, near_low, last[1]]
        + over_core_in_two(last[1]),
    )
    low_sent, got_c = barrier((low_sent, got_c))
    got_d = over_x(sent_d)

    scaled = ((low + over_x(low_sent)) * scale).astype(BF16)
    scaled = scaled + along(scaled, NEAR)
    scaled, got_d = barrier((scaled, got_d))
    parts = [kept_a, got_a, kept_b, got_b, kept_c, got_c, kept_d, got_d]
    return call(
        final_kernel,
        shape(residual.shape, BF16),
        [SMEM] + [VMEM] * 13,
        [flags, residual, scaled, along(scaled, FAR), hot, ups] + parts,
    )


def shards(rows, residual, weight, down, up, tenant, entry, live):
    sizes = [lax.axis_size(name) for name in ("blk", "split", "sub")]
    plan = line if sizes == [4, 2, 2] and down.shape[0] == 1 else general
    return plan(rows, residual, weight, down, up, tenant, entry, live)


def solution(mesh):
    in_specs = (
        P(("groups", "blk"), "split"),
        P(("groups", "split"), ("blk", "sub")),
        P("split", ("blk", "sub")),
        P("blk", None, "split"),
        P("split", None, ("blk", "sub")),
        P("groups"),
        P(),
        P(),
    )
    out_specs = P(("groups", "split"), ("blk", "sub"))
    return jax.shard_map(shards, mesh=mesh, in_specs=in_specs, out_specs=out_specs, check_vma=False)
```

```python
import jax
import jax.numpy as jnp
from jax import lax
from jax.experimental import pallas as pl
from jax.experimental.pallas import tpu as pltpu
from jax.sharding import PartitionSpec as P

F32 = jnp.float32
BF16 = jnp.bfloat16


def low_rank_weights(low, slot, live, slots, rank_width):
    kept = jnp.arange(rank_width, dtype=jnp.int32)[None, :] < live[:, None]
    scaling = rank_width / live.astype(F32)
    scaled = jnp.where(kept, low * scaling[:, None], jnp.zeros((), F32)).astype(BF16)
    hot = slot[:, None] == jnp.arange(slots, dtype=jnp.int32)[None, :]
    spread = jnp.where(hot[:, :, None], scaled[:, None, :], jnp.zeros((), BF16))
    return spread.reshape(low.shape[0], slots * rank_width)


def tables(tenant, entry, live):
    ids = jnp.arange(entry.shape[0], dtype=jnp.int32)
    hot = (tenant[:, None] == ids[None, :]).astype(jnp.int32)
    return jnp.sum(hot * entry[None, :], axis=1), jnp.sum(hot * live[None, :], axis=1)


def general(rows, residual, weight, down, up, tenant, entry, live):
    own = residual.shape[0]
    cols = weight.shape[1]
    width = down.shape[1]
    slots = entry.shape[0]
    slot_all, live_all = tables(tenant, entry, live)
    part = rows.shape[0] // lax.axis_size("sub")
    mine = lax.dynamic_slice_in_dim(rows, lax.axis_index("sub") * part, part, 0)
    halves = lax.all_gather(lax.all_gather(mine, "blk", axis=0), "sub", axis=1)
    full = halves.reshape(-1, rows.shape[1])
    base = jnp.dot(full, weight, preferred_element_type=F32)
    low = lax.dot_general(
        full, down.reshape(-1, down.shape[2]), (((1,), (1,)), ((), ())), preferred_element_type=F32
    )
    held = down.shape[0]
    places = lax.axis_index("blk") * held + jnp.arange(held, dtype=jnp.int32)
    here = slot_all[:, None] == places[None, :]
    low = jnp.sum(
        jnp.where(here[:, :, None], low.reshape(-1, held, width), jnp.zeros((), F32)), axis=1
    )
    low = lax.psum(lax.psum_scatter(low, "split", scatter_dimension=0, tiled=True), "blk")
    base = lax.psum_scatter(base, "split", scatter_dimension=0, tiled=True)
    start = lax.axis_index("split") * own
    spread = low_rank_weights(
        low,
        lax.dynamic_slice_in_dim(slot_all, start, own, 0),
        lax.dynamic_slice_in_dim(live_all, start, own, 0),
        slots,
        width,
    )
    ups = lax.all_gather(up, "split", axis=0, tiled=True).reshape(slots * width, cols)
    lora = jnp.dot(spread, ups, preferred_element_type=F32)
    return (residual.astype(F32) + base + lora).astype(BF16)


SWAP = [(0, 1), (1, 0)]
NEAR = [(0, 1), (1, 0), (2, 3), (3, 2)]
FAR = [(0, 2), (2, 0), (1, 3), (3, 1)]
VMEM = pl.BlockSpec(memory_space=pltpu.VMEM)
SMEM = pl.BlockSpec(memory_space=pltpu.SMEM)
HBM = pl.BlockSpec(memory_space=pltpu.HBM)
COST = pl.CostEstimate(flops=0, bytes_accessed=0, transcendentals=0)
PARAMS = pltpu.CompilerParams(vmem_limit_bytes=16 * 1024 * 1024)
FROM_HBM = pltpu.CompilerParams(vmem_limit_bytes=40 * 1024 * 1024)


def shape(dims, dtype):
    return jax.ShapeDtypeStruct(dims, dtype)


def dot(a, b):
    return jnp.dot(a, b, preferred_element_type=F32)


def call(kernel, outs, in_specs, operands, scratch=(), params=PARAMS):
    return pl.pallas_call(
        kernel,
        out_shape=outs,
        in_specs=in_specs,
        out_specs=jax.tree.map(lambda _: VMEM, outs),
        scratch_shapes=scratch,
        compiler_params=params,
        cost_estimate=COST,
    )(*operands)


def column_tiles(cols):
    tile = 256 if cols % 256 == 0 else cols
    return [slice(at, at + tile) for at in range(0, cols, tile)]


def joined(flags_ref, mine, other):
    first = flags_ref[1] == 0
    return jnp.concatenate([jnp.where(first, mine, other), jnp.where(first, other, mine)])


def low_product(rows, down_ref):
    return lax.dot_general(
        rows, down_ref[...], (((1,), (1,)), ((), ())), preferred_element_type=F32
    )


def part(flags_ref, held, value, keep_ref, send_ref, tile):
    home = flags_ref[0] == 1
    keep_ref[:, tile] = jnp.where(home, held, value)
    send_ref[:, tile] = jnp.where(home, value, held).astype(BF16)


def own_kernel(
    weight_ref, down_ref, rows_ref, held_ref, sum_ref, low_ref, sems
):
    tiles = column_tiles(weight_ref.shape[1])
    copies = [
        pltpu.make_async_copy(weight_ref.at[:, tile], held_ref.at[:, tile], sems.at[i])
        for i, tile in enumerate(tiles)
    ]
    for copy in copies:
        copy.start()
    rows = rows_ref[...]
    low_ref[...] = low_product(rows, down_ref)
    for copy, tile in zip(copies, tiles):
        copy.wait()
        sum_ref[:, tile] = dot(rows, held_ref[:, tile])


def far_kernel(
    flags_ref, weight_ref, down_ref, held_ref, mine_ref, first_ref, second_ref,
    keep_ref, send_ref, low_ref,
):
    other = jnp.concatenate([first_ref[...], second_ref[...]])
    rows = joined(flags_ref, mine_ref[...], other)
    low_ref[...] = low_product(rows, down_ref)
    for tile in column_tiles(weight_ref.shape[1]):
        value = dot(rows, weight_ref[:, tile])
        part(flags_ref, held_ref[:, tile], value, keep_ref, send_ref, tile)


def near_kernel(
    flags_ref, weight_ref, down_ref, mine_ref, first_ref, second_ref, last_ref, third_ref,
    fourth_ref, keep_ref, send_ref, hold_ref, low_ref,
):
    other = jnp.concatenate([first_ref[...], second_ref[...]])
    near = joined(flags_ref, mine_ref[...], other)
    last = joined(flags_ref, last_ref[...], jnp.concatenate([third_ref[...], fourth_ref[...]]))
    rows = jnp.concatenate([near, last])
    low_ref[...] = low_product(rows, down_ref)
    step = last_ref.shape[0]
    for tile in column_tiles(weight_ref.shape[1]):
        value = dot(rows, weight_ref[:, tile])
        held = jnp.concatenate([value[:step], value[2 * step : 3 * step]])
        part(flags_ref, held, value[4 * step :], keep_ref, send_ref, tile)
        hold_ref[:, tile] = jnp.concatenate(
            [value[step : 2 * step], value[3 * step : 4 * step]]
        )


def last_kernel(
    flags_ref, weight_ref, down_ref, held_ref, own_low, far_low, near_low, mine_ref, first_ref,
    second_ref, keep_ref, send_ref, low_keep_ref, low_send_ref,
):
    other = jnp.concatenate([first_ref[...], second_ref[...]])
    rows = joined(flags_ref, mine_ref[...], other)
    low = low_product(rows, down_ref)
    block, width = own_low.shape
    step = mine_ref.shape[0]
    last_low = jnp.concatenate(
        [
            near_low[block : block + step], low[:step],
            near_low[block + step :], low[step:],
        ]
    )
    odd, home = flags_ref[2] == 1, flags_ref[0] == 1
    near = own_low[...], near_low[:block]
    far = far_low[...], last_low
    for side, here in ((0, slice(0, width)), (1, slice(width, 2 * width))):
        near_side = jnp.where(odd, near[1 - side], near[side])
        far_side = jnp.where(odd, far[1 - side], far[side])
        low_keep_ref[:, here] = jnp.where(home, near_side, far_side)
        low_send_ref[:, here] = jnp.where(home, far_side, near_side)
    for tile in column_tiles(weight_ref.shape[1]):
        value = dot(rows, weight_ref[:, tile])
        part(flags_ref, held_ref[:, tile], value, keep_ref, send_ref, tile)


def base_kernel(flags_ref, residual_ref, *refs):
    *parts, out_ref = refs
    odd = flags_ref[2] == 1
    first, left, right = [
        keep[...] + got[...].astype(F32) for keep, got in zip(parts[::2], parts[1::2])
    ]
    step = left.shape[0] // 2
    second = jnp.concatenate([left[:step], right[:step], left[step:], right[step:]])
    block = first.shape[0]
    for at, base in ((0, jnp.where(odd, second, first)), (block, jnp.where(odd, first, second))):
        here = slice(at, at + block)
        out_ref[here, :] = residual_ref[here, :].astype(F32) + base


def final_kernel(base_ref, scaled_ref, scaled_got_ref, hot_ref, ups_ref, out_ref):
    scaled = scaled_ref[...] + scaled_got_ref[...]
    width = ups_ref.shape[1]
    scaled = jnp.concatenate([scaled[:, :width], scaled[:, width:]])
    lora = dot(scaled * hot_ref[0], ups_ref[0])
    for slot in range(1, ups_ref.shape[0]):
        lora += dot(scaled * hot_ref[slot], ups_ref[slot])
    out_ref[...] = (base_ref[...] + lora).astype(BF16)


def line(rows, residual, weight, down, up, tenant, entry, live):
    z, x, c = lax.axis_index("blk"), lax.axis_index("split"), lax.axis_index("sub")
    block_rows = rows.shape[0]
    width = down.shape[1]
    own, cols = residual.shape
    slots = entry.shape[0]
    home = (z // 2) == x
    odd = z % 2 == 1
    half, step = block_rows // 2, block_rows // 4
    barrier = lax.optimization_barrier

    def over_core(value):
        return lax.ppermute(value, "sub", SWAP)

    def over_x(value):
        return lax.ppermute(value, "split", SWAP)

    def along(value, pairs):
        return lax.ppermute(value, "blk", pairs)

    def over_core_in_two(piece):
        count = piece.shape[0] // 2
        return [over_core(piece[:count]), over_core(piece[count:])]

    def parted(count):
        return [shape((count, cols), F32), shape((count, cols), BF16)]

    def lows(count):
        return [shape((count, width), F32)]

    slot_all, live_all = tables(tenant, entry, live)
    slot = lax.dynamic_slice_in_dim(slot_all, x * own, own, 0)
    rank = lax.dynamic_slice_in_dim(live_all, x * own, own, 0)

    flags = jnp.stack([home, c, odd]).astype(jnp.int32)
    kept = jnp.arange(width, dtype=jnp.int32)[None, :] < rank[:, None]
    scale = jnp.where(kept, (width / rank.astype(F32))[:, None], jnp.zeros((), F32))
    scale = jnp.where((slot == z)[:, None], scale, jnp.zeros((), F32))
    scale = jnp.concatenate([scale[:block_rows], scale[block_rows:]], axis=1)
    hot = slot[None, :] == jnp.arange(slots, dtype=jnp.int32)[:, None]
    hot = jnp.broadcast_to(hot[:, :, None], (slots, own, width)).astype(BF16)

    mine = lax.dynamic_slice_in_dim(rows, c * half, half, 0)
    near, far = along(mine, NEAR), along(mine, FAR)
    up_other = over_x(up)
    ups = jnp.where(x == 0, jnp.concatenate([up, up_other]), jnp.concatenate([up_other, up]))
    held, own_sum, own_low = call(
        own_kernel,
        [shape(weight.shape, BF16), shape((block_rows, cols), F32)] + lows(block_rows),
        [HBM, VMEM, VMEM],
        [weight, down[0], rows],
        [pltpu.SemaphoreType.DMA((len(column_tiles(cols)),))],
        FROM_HBM,
    )
    near, far, own_sum, own_low, ups, hot, scale = barrier(
        (near, far, own_sum, own_low, ups, hot, scale)
    )

    last = [along(far[:step], NEAR)]
    far_others = over_core_in_two(far)
    far_second, far_others[0] = barrier((far[step:], far_others[0]))
    last.append(along(far_second, NEAR))
    kept_a, sent_a, far_low = call(
        far_kernel,
        parted(block_rows) + lows(block_rows),
        [SMEM] + [VMEM] * 6,
        [flags, held, down[0], own_sum, far] + far_others,
    )
    got_a = over_x(sent_a)
    last[0], kept_a = barrier((last[0], kept_a))

    kept_c, sent_c, hold, near_low = call(
        near_kernel,
        parted(half) + [shape((half, cols), F32)] + lows(block_rows + half),
        [SMEM] + [VMEM] * 8,
        [flags, held, down[0], near] + over_core_in_two(near)
        + [last[0]] + over_core_in_two(last[0]),
    )
    got_c = over_x(sent_c)
    last[1], hold, got_a, near_low = barrier((last[1], hold, got_a, near_low))

    kept_d, sent_d, low, low_sent = call(
        last_kernel,
        parted(half) + [shape((block_rows, 2 * width), F32)] * 2,
        [SMEM] + [VMEM] * 9,
        [flags, held, down[0], hold, own_low, far_low, near_low, last[1]]
        + over_core_in_two(last[1]),
    )
    got_d = over_x(sent_d)

    scaled = ((low + over_x(low_sent)) * scale).astype(BF16)
    scaled = scaled + along(scaled, NEAR)
    scaled, got_c, got_d = barrier((scaled, got_c, got_d))
    base = call(
        base_kernel,
        shape(residual.shape, F32),
        [SMEM] + [VMEM] * 7,
        [flags, residual, kept_a, got_a, kept_c, got_c, kept_d, got_d],
    )
    return call(
        final_kernel,
        shape(residual.shape, BF16),
        [VMEM] * 5,
        [base, scaled, along(scaled, FAR), hot, ups],
    )


def shards(rows, residual, weight, down, up, tenant, entry, live):
    sizes = [lax.axis_size(name) for name in ("blk", "split", "sub")]
    plan = line if sizes == [4, 2, 2] and down.shape[0] == 1 else general
    return plan(rows, residual, weight, down, up, tenant, entry, live)


def solution(mesh):
    in_specs = (
        P(("groups", "blk"), "split"),
        P(("groups", "split"), ("blk", "sub")),
        P("split", ("blk", "sub")),
        P("blk", None, "split"),
        P("split", None, ("blk", "sub")),
        P("groups"),
        P(),
        P(),
    )
    out_specs = P(("groups", "split"), ("blk", "sub"))
    return jax.shard_map(shards, mesh=mesh, in_specs=in_specs, out_specs=out_specs, check_vma=False)
```

```python
import jax
import jax.numpy as jnp
from jax import lax
from jax.experimental import pallas as pl
from jax.experimental.pallas import tpu as pltpu
from jax.sharding import PartitionSpec as P

F32 = jnp.float32
BF16 = jnp.bfloat16


def low_rank_weights(low, slot, live, slots, rank_width):
    kept = jnp.arange(rank_width, dtype=jnp.int32)[None, :] < live[:, None]
    scaling = rank_width / live.astype(F32)
    scaled = jnp.where(kept, low * scaling[:, None], jnp.zeros((), F32)).astype(BF16)
    hot = slot[:, None] == jnp.arange(slots, dtype=jnp.int32)[None, :]
    spread = jnp.where(hot[:, :, None], scaled[:, None, :], jnp.zeros((), BF16))
    return spread.reshape(low.shape[0], slots * rank_width)


def tables(tenant, entry, live):
    ids = jnp.arange(entry.shape[0], dtype=jnp.int32)
    hot = (tenant[:, None] == ids[None, :]).astype(jnp.int32)
    return jnp.sum(hot * entry[None, :], axis=1), jnp.sum(hot * live[None, :], axis=1)


def general(rows, residual, weight, down, up, tenant, entry, live):
    own = residual.shape[0]
    cols = weight.shape[1]
    width = down.shape[1]
    slots = entry.shape[0]
    slot_all, live_all = tables(tenant, entry, live)
    part = rows.shape[0] // lax.axis_size("sub")
    mine = lax.dynamic_slice_in_dim(rows, lax.axis_index("sub") * part, part, 0)
    halves = lax.all_gather(lax.all_gather(mine, "blk", axis=0), "sub", axis=1)
    full = halves.reshape(-1, rows.shape[1])
    base = jnp.dot(full, weight, preferred_element_type=F32)
    low = lax.dot_general(
        full, down.reshape(-1, down.shape[2]), (((1,), (1,)), ((), ())), preferred_element_type=F32
    )
    held = down.shape[0]
    places = lax.axis_index("blk") * held + jnp.arange(held, dtype=jnp.int32)
    here = slot_all[:, None] == places[None, :]
    low = jnp.sum(
        jnp.where(here[:, :, None], low.reshape(-1, held, width), jnp.zeros((), F32)), axis=1
    )
    low = lax.psum(lax.psum_scatter(low, "split", scatter_dimension=0, tiled=True), "blk")
    base = lax.psum_scatter(base, "split", scatter_dimension=0, tiled=True)
    start = lax.axis_index("split") * own
    spread = low_rank_weights(
        low,
        lax.dynamic_slice_in_dim(slot_all, start, own, 0),
        lax.dynamic_slice_in_dim(live_all, start, own, 0),
        slots,
        width,
    )
    ups = lax.all_gather(up, "split", axis=0, tiled=True).reshape(slots * width, cols)
    lora = jnp.dot(spread, ups, preferred_element_type=F32)
    return (residual.astype(F32) + base + lora).astype(BF16)


SWAP = [(0, 1), (1, 0)]
NEAR = [(0, 1), (1, 0), (2, 3), (3, 2)]
FAR = [(0, 2), (2, 0), (1, 3), (3, 1)]
VMEM = pl.BlockSpec(memory_space=pltpu.VMEM)
SMEM = pl.BlockSpec(memory_space=pltpu.SMEM)
HBM = pl.BlockSpec(memory_space=pltpu.HBM)
COST = pl.CostEstimate(flops=0, bytes_accessed=0, transcendentals=0)
PARAMS = pltpu.CompilerParams(vmem_limit_bytes=16 * 1024 * 1024)
FROM_HBM = pltpu.CompilerParams(vmem_limit_bytes=40 * 1024 * 1024)


def shape(dims, dtype):
    return jax.ShapeDtypeStruct(dims, dtype)


def dot(a, b):
    return jnp.dot(a, b, preferred_element_type=F32)


def call(kernel, outs, in_specs, operands, scratch=(), params=PARAMS):
    return pl.pallas_call(
        kernel,
        out_shape=outs,
        in_specs=in_specs,
        out_specs=jax.tree.map(lambda _: VMEM, outs),
        scratch_shapes=scratch,
        compiler_params=params,
        cost_estimate=COST,
    )(*operands)


def column_tiles(cols):
    tile = 256 if cols % 256 == 0 else cols
    return [slice(at, at + tile) for at in range(0, cols, tile)]


def joined(flags_ref, mine, other):
    first = flags_ref[1] == 0
    return jnp.concatenate([jnp.where(first, mine, other), jnp.where(first, other, mine)])


def part(flags_ref, held, value, keep_ref, send_ref, tile):
    home = flags_ref[0] == 1
    keep_ref[:, tile] = jnp.where(home, held, value)
    send_ref[:, tile] = jnp.where(home, value, held).astype(BF16)


def own_kernel(weight_ref, rows_ref, held_ref, sum_ref, sems):
    tiles = column_tiles(weight_ref.shape[1])
    copies = [
        pltpu.make_async_copy(weight_ref.at[:, tile], held_ref.at[:, tile], sems.at[i])
        for i, tile in enumerate(tiles)
    ]
    for copy in copies:
        copy.start()
    rows = rows_ref[...]
    for copy, tile in zip(copies, tiles):
        copy.wait()
        sum_ref[:, tile] = dot(rows, held_ref[:, tile])


def far_kernel(
    flags_ref, weight_ref, held_ref, mine_ref, first_ref, second_ref, keep_ref, send_ref
):
    other = jnp.concatenate([first_ref[...], second_ref[...]])
    rows = joined(flags_ref, mine_ref[...], other)
    for tile in column_tiles(weight_ref.shape[1]):
        value = dot(rows, weight_ref[:, tile])
        part(flags_ref, held_ref[:, tile], value, keep_ref, send_ref, tile)


def near_kernel(
    flags_ref, weight_ref, mine_ref, first_ref, second_ref, last_ref, third_ref, fourth_ref,
    keep_ref, send_ref, hold_ref,
):
    other = jnp.concatenate([first_ref[...], second_ref[...]])
    near = joined(flags_ref, mine_ref[: other.shape[0]], other)
    last = joined(flags_ref, last_ref[...], jnp.concatenate([third_ref[...], fourth_ref[...]]))
    rows = jnp.concatenate([near, last])
    step = last_ref.shape[0]
    for tile in column_tiles(weight_ref.shape[1]):
        value = dot(rows, weight_ref[:, tile])
        held = jnp.concatenate([value[:step], value[2 * step : 3 * step]])
        part(flags_ref, held, value[4 * step :], keep_ref, send_ref, tile)
        hold_ref[:, tile] = jnp.concatenate(
            [value[step : 2 * step], value[3 * step : 4 * step]]
        )


def low_kernel(
    flags_ref, down_ref, mine_quarter, group_quarter, core_quarter, both_quarter, rows_ref,
    mine_ref, first_ref, second_ref, own_mask_ref, far_mask_ref, keep_ref, send_ref,
):
    other = jnp.concatenate([first_ref[...], second_ref[...]])
    far = joined(flags_ref, mine_ref[...], other)

    def half(mine, other):
        first = flags_ref[3] == 0
        return jnp.concatenate([jnp.where(first, mine, other), jnp.where(first, other, mine)])

    core_half = half(mine_quarter[...], group_quarter[...])
    other_half = half(core_quarter[...], both_quarter[...])
    maps = jnp.concatenate([down_ref[...], joined(flags_ref, core_half, other_half)])
    width = down_ref.shape[0]

    def values(rows, mask_ref):
        low = lax.dot_general(
            rows, maps, (((1,), (1,)), ((), ())), preferred_element_type=F32
        ) * mask_ref[...]
        return low[:, :width] + low[:, width:]

    own, far = values(rows_ref[...], own_mask_ref), values(far, far_mask_ref)
    home = flags_ref[0] == 1
    keep_ref[...] = jnp.where(home, own, far)
    send_ref[...] = jnp.where(home, far, own)


def base_kernel(flags_ref, residual_ref, *refs):
    *parts, out_ref = refs
    odd = flags_ref[2] == 1
    first, left, right = [
        keep[...] + got[...].astype(F32) for keep, got in zip(parts[::2], parts[1::2])
    ]
    step = left.shape[0] // 2
    second = jnp.concatenate([left[:step], right[:step], left[step:], right[step:]])
    block = first.shape[0]
    for at, base in ((0, jnp.where(odd, second, first)), (block, jnp.where(odd, first, second))):
        here = slice(at, at + block)
        out_ref[here, :] = residual_ref[here, :].astype(F32) + base


def final_kernel(flags_ref, base_ref, scaled_ref, scaled_got_ref, hot_ref, ups_ref, out_ref):
    mine, got = scaled_ref[...], scaled_got_ref[...]
    odd = flags_ref[2] == 1
    scaled = jnp.concatenate([jnp.where(odd, got, mine), jnp.where(odd, mine, got)])
    lora = dot(scaled * hot_ref[0], ups_ref[0])
    for slot in range(1, ups_ref.shape[0]):
        lora += dot(scaled * hot_ref[slot], ups_ref[slot])
    out_ref[...] = (base_ref[...] + lora).astype(BF16)


def line(rows, residual, weight, down, up, tenant, entry, live):
    z, x, c = lax.axis_index("blk"), lax.axis_index("split"), lax.axis_index("sub")
    y = lax.axis_index("groups")
    block_rows = rows.shape[0]
    width = down.shape[1]
    own, cols = residual.shape
    slots = entry.shape[0]
    home = (z // 2) == x
    odd = z % 2 == 1
    half, step, quarter = block_rows // 2, block_rows // 4, width // 4
    barrier = lax.optimization_barrier

    def over_core(value):
        return lax.ppermute(value, "sub", SWAP)

    def over_x(value):
        return lax.ppermute(value, "split", SWAP)

    def along(value, pairs):
        return lax.ppermute(value, "blk", pairs)

    def over_core_in_two(piece):
        count = piece.shape[0] // 2
        return [over_core(piece[:count]), over_core(piece[count:])]

    def parted(count):
        return [shape((count, cols), F32), shape((count, cols), BF16)]

    slot_all, live_all = tables(tenant, entry, live)
    flags = jnp.stack([home, c, odd, y]).astype(jnp.int32)
    kept_place = x * own + (z % 2) * block_rows
    rank = lax.dynamic_slice_in_dim(live_all, kept_place, block_rows, 0)
    live_ranks = jnp.arange(width, dtype=jnp.int32)[None, :] < rank[:, None]
    scale = jnp.where(live_ranks, (width / rank.astype(F32))[:, None], jnp.zeros((), F32))
    slot = lax.dynamic_slice_in_dim(slot_all, x * own, own, 0)
    hot = slot[None, :] == jnp.arange(slots, dtype=jnp.int32)[:, None]
    hot = jnp.broadcast_to(hot[:, :, None], (slots, own, width)).astype(BF16)

    def tenant_mask(block):
        slot = lax.dynamic_slice_in_dim(slot_all, block * block_rows, block_rows, 0)
        entries = jnp.where(jnp.arange(2 * width) < width, z, z + 1 - 2 * (z % 2))
        return (slot[:, None] == entries[None, :]).astype(F32)

    masks = [tenant_mask(z), tenant_mask(z + 2 - 4 * (z // 2))]

    mine = lax.dynamic_slice_in_dim(rows, c * half, half, 0)
    far = along(mine, FAR)
    own_ranks = lax.dynamic_slice_in_dim(down[0], (2 * c + y) * quarter, quarter, 0)
    near = along(jnp.concatenate([mine, own_ranks]), NEAR)
    held, own_sum = call(
        own_kernel,
        [shape(weight.shape, BF16), shape((block_rows, cols), F32)],
        [HBM, VMEM],
        [weight, rows],
        [pltpu.SemaphoreType.DMA((len(column_tiles(cols)),))],
        FROM_HBM,
    )
    up, own_sum = barrier((up, own_sum))
    up_other = over_x(up)
    ups = jnp.where(x == 0, jnp.concatenate([up, up_other]), jnp.concatenate([up_other, up]))
    near, far, own_sum, ups, hot, scale, masks = barrier(
        (near, far, own_sum, ups, hot, scale, masks)
    )

    last = [along(far[:step], NEAR)]
    far_others = over_core_in_two(far)
    far_second, far_others[0] = barrier((far[step:], far_others[0]))
    last.append(along(far_second, NEAR))
    kept_a, sent_a = call(
        far_kernel,
        parted(block_rows),
        [SMEM] + [VMEM] * 5,
        [flags, held, own_sum, far] + far_others,
    )
    got_a = over_x(sent_a)

    ranks, far_others[1] = barrier((near[half:], far_others[1]))
    quarters = [
        ranks,
        lax.ppermute(ranks, "groups", SWAP),
        over_core(ranks),
        lax.ppermute(ranks, ("groups", "sub"), [(0, 3), (1, 2), (2, 1), (3, 0)]),
    ]
    low, low_sent = call(
        low_kernel,
        [shape((block_rows, width), F32)] * 2,
        [SMEM] + [VMEM] * 11,
        [flags, down[0]] + quarters + [rows, far] + far_others + masks,
    )
    low_got = over_x(low_sent)
    last[0], kept_a, low = barrier((last[0], kept_a, low))

    kept_c, sent_c, hold = call(
        near_kernel,
        parted(half) + [shape((half, cols), F32)],
        [SMEM] + [VMEM] * 7,
        [flags, held, near] + over_core_in_two(near[:half])
        + [last[0]] + over_core_in_two(last[0]),
    )
    got_c = over_x(sent_c)
    last[1], hold, got_a, low, low_got = barrier((last[1], hold, got_a, low, low_got))

    scaled = ((low + low_got) * scale).astype(BF16)
    scaled_got = along(scaled, FAR)
    kept_d, sent_d = call(
        far_kernel,
        parted(half),
        [SMEM] + [VMEM] * 5,
        [flags, held, hold, last[1]] + over_core_in_two(last[1]),
    )
    scaled_got, sent_d = barrier((scaled_got, sent_d))
    scaled = scaled + scaled_got
    got_d = over_x(sent_d)
    scaled_got = along(scaled, NEAR)
    base = call(
        base_kernel,
        shape(residual.shape, F32),
        [SMEM] + [VMEM] * 7,
        [flags, residual, kept_a, got_a, kept_c, got_c, kept_d, got_d],
    )
    return call(
        final_kernel,
        shape(residual.shape, BF16),
        [SMEM] + [VMEM] * 5,
        [flags, base, scaled, scaled_got, hot, ups],
    )


def shards(rows, residual, weight, down, up, tenant, entry, live):
    sizes = [lax.axis_size(name) for name in ("groups", "blk", "split", "sub")]
    plan = line if sizes == [2, 4, 2, 2] and down.shape[0] == 1 else general
    return plan(rows, residual, weight, down, up, tenant, entry, live)


def solution(mesh):
    in_specs = (
        P(("groups", "blk"), "split"),
        P(("groups", "split"), ("blk", "sub")),
        P("split", ("blk", "sub")),
        P("blk", None, "split"),
        P("split", None, ("blk", "sub")),
        P("groups"),
        P(),
        P(),
    )
    out_specs = P(("groups", "split"), ("blk", "sub"))
    return jax.shard_map(shards, mesh=mesh, in_specs=in_specs, out_specs=out_specs, check_vma=False)
```

```python
import jax
import jax.numpy as jnp
from jax import lax
from jax.experimental import pallas as pl
from jax.experimental.pallas import tpu as pltpu
from jax.sharding import PartitionSpec as P

F32 = jnp.float32
BF16 = jnp.bfloat16


def low_rank_weights(low, slot, live, slots, rank_width):
    kept = jnp.arange(rank_width, dtype=jnp.int32)[None, :] < live[:, None]
    scaling = rank_width / live.astype(F32)
    scaled = jnp.where(kept, low * scaling[:, None], jnp.zeros((), F32)).astype(BF16)
    hot = slot[:, None] == jnp.arange(slots, dtype=jnp.int32)[None, :]
    spread = jnp.where(hot[:, :, None], scaled[:, None, :], jnp.zeros((), BF16))
    return spread.reshape(low.shape[0], slots * rank_width)


def tables(tenant, entry, live):
    ids = jnp.arange(entry.shape[0], dtype=jnp.int32)
    hot = (tenant[:, None] == ids[None, :]).astype(jnp.int32)
    return jnp.sum(hot * entry[None, :], axis=1), jnp.sum(hot * live[None, :], axis=1)


def general(rows, residual, weight, down, up, tenant, entry, live):
    own = residual.shape[0]
    cols = weight.shape[1]
    width = down.shape[1]
    slots = entry.shape[0]
    slot_all, live_all = tables(tenant, entry, live)
    part = rows.shape[0] // lax.axis_size("sub")
    mine = lax.dynamic_slice_in_dim(rows, lax.axis_index("sub") * part, part, 0)
    halves = lax.all_gather(lax.all_gather(mine, "blk", axis=0), "sub", axis=1)
    full = halves.reshape(-1, rows.shape[1])
    base = jnp.dot(full, weight, preferred_element_type=F32)
    low = lax.dot_general(
        full, down.reshape(-1, down.shape[2]), (((1,), (1,)), ((), ())), preferred_element_type=F32
    )
    held = down.shape[0]
    places = lax.axis_index("blk") * held + jnp.arange(held, dtype=jnp.int32)
    here = slot_all[:, None] == places[None, :]
    low = jnp.sum(
        jnp.where(here[:, :, None], low.reshape(-1, held, width), jnp.zeros((), F32)), axis=1
    )
    low = lax.psum(lax.psum_scatter(low, "split", scatter_dimension=0, tiled=True), "blk")
    base = lax.psum_scatter(base, "split", scatter_dimension=0, tiled=True)
    start = lax.axis_index("split") * own
    spread = low_rank_weights(
        low,
        lax.dynamic_slice_in_dim(slot_all, start, own, 0),
        lax.dynamic_slice_in_dim(live_all, start, own, 0),
        slots,
        width,
    )
    ups = lax.all_gather(up, "split", axis=0, tiled=True).reshape(slots * width, cols)
    lora = jnp.dot(spread, ups, preferred_element_type=F32)
    return (residual.astype(F32) + base + lora).astype(BF16)


SWAP = [(0, 1), (1, 0)]
NEAR = [(0, 1), (1, 0), (2, 3), (3, 2)]
FAR = [(0, 2), (2, 0), (1, 3), (3, 1)]


def by_core(first, second):
    return [(2 * a, 2 * b) for a, b in first] + [(2 * a + 1, 2 * b + 1) for a, b in second]


VMEM = pl.BlockSpec(memory_space=pltpu.VMEM)
SMEM = pl.BlockSpec(memory_space=pltpu.SMEM)
HBM = pl.BlockSpec(memory_space=pltpu.HBM)
COST = pl.CostEstimate(flops=0, bytes_accessed=0, transcendentals=0)
PARAMS = pltpu.CompilerParams(vmem_limit_bytes=16 * 1024 * 1024)
FROM_HBM = pltpu.CompilerParams(vmem_limit_bytes=40 * 1024 * 1024)


def shape(dims, dtype):
    return jax.ShapeDtypeStruct(dims, dtype)


def dot(a, b):
    return jnp.dot(a, b, preferred_element_type=F32)


def call(kernel, outs, in_specs, operands, scratch=(), params=PARAMS):
    return pl.pallas_call(
        kernel,
        out_shape=outs,
        in_specs=in_specs,
        out_specs=jax.tree.map(lambda _: VMEM, outs),
        scratch_shapes=scratch,
        compiler_params=params,
        cost_estimate=COST,
    )(*operands)


def column_tiles(cols):
    tile = 256 if cols % 256 == 0 else cols
    return [slice(at, at + tile) for at in range(0, cols, tile)]


def joined(flags_ref, mine, other):
    first = flags_ref[1] == 0
    return jnp.concatenate([jnp.where(first, mine, other), jnp.where(first, other, mine)])


def low_product(rows, down_ref):
    return lax.dot_general(
        rows, down_ref[...], (((1,), (1,)), ((), ())), preferred_element_type=F32
    )


def part(flags_ref, held, value, keep_ref, send_ref, tile):
    home = flags_ref[0] == 1
    keep_ref[:, tile] = jnp.where(home, held, value)
    send_ref[:, tile] = jnp.where(home, value, held).astype(BF16)


def own_kernel(
    weight_ref, down_ref, rows_ref, held_ref, sum_ref, low_ref, sems
):
    tiles = column_tiles(weight_ref.shape[1])
    copies = [
        pltpu.make_async_copy(weight_ref.at[:, tile], held_ref.at[:, tile], sems.at[i])
        for i, tile in enumerate(tiles)
    ]
    for copy in copies:
        copy.start()
    rows = rows_ref[...]
    low_ref[...] = low_product(rows, down_ref)
    for copy, tile in zip(copies, tiles):
        copy.wait()
        sum_ref[:, tile] = dot(rows, held_ref[:, tile])


def blocks_kernel(
    flags_ref, weight_ref, down_ref, held_ref, mine_ref, first_ref, second_ref, third_ref,
    fourth_ref, keep_ref, send_ref, near_ref, low_ref,
):
    others = [ref[...] for ref in (first_ref, second_ref, third_ref, fourth_ref)]
    rows = jnp.concatenate([mine_ref[...]] + others)
    first = flags_ref[1] == 0
    count = mine_ref.shape[0]

    def far_and_near(value):
        one, two = value[:count], value[count:]
        return jnp.where(first, one, two), jnp.where(first, two, one)

    far_low, near_low = far_and_near(low_product(rows, down_ref))
    low_ref[:count] = far_low
    low_ref[count:] = near_low
    for tile in column_tiles(weight_ref.shape[1]):
        far, near = far_and_near(dot(rows, weight_ref[:, tile]))
        part(flags_ref, held_ref[:, tile], far, keep_ref, send_ref, tile)
        near_ref[:, tile] = near


def piece_kernel(
    flags_ref, weight_ref, down_ref, held_ref, mine_ref, first_ref, second_ref,
    keep_ref, send_ref, low_ref,
):
    other = jnp.concatenate([first_ref[...], second_ref[...]])
    rows = joined(flags_ref, mine_ref[...], other)
    low_ref[...] = low_product(rows, down_ref)
    step = mine_ref.shape[0]
    for tile in column_tiles(weight_ref.shape[1]):
        held = jnp.concatenate([held_ref[:step, tile], held_ref[2 * step : 3 * step, tile]])
        part(flags_ref, held, dot(rows, weight_ref[:, tile]), keep_ref, send_ref, tile)


def last_kernel(
    flags_ref, weight_ref, down_ref, held_ref, own_low, low_ref, piece_low, mine_ref, first_ref,
    second_ref, keep_ref, send_ref, low_keep_ref, low_send_ref,
):
    other = jnp.concatenate([first_ref[...], second_ref[...]])
    rows = joined(flags_ref, mine_ref[...], other)
    low = low_product(rows, down_ref)
    block, width = own_low.shape
    step = mine_ref.shape[0]
    last_low = jnp.concatenate(
        [
            piece_low[:step], low[:step], piece_low[step:], low[step:]
        ]
    )
    odd, home = flags_ref[2] == 1, flags_ref[0] == 1
    near = own_low[...], low_ref[block:]
    far = low_ref[:block], last_low
    for side, here in ((0, slice(0, width)), (1, slice(width, 2 * width))):
        near_side = jnp.where(odd, near[1 - side], near[side])
        far_side = jnp.where(odd, far[1 - side], far[side])
        low_keep_ref[:, here] = jnp.where(home, near_side, far_side)
        low_send_ref[:, here] = jnp.where(home, far_side, near_side)
    for tile in column_tiles(weight_ref.shape[1]):
        held = jnp.concatenate([held_ref[step : 2 * step, tile], held_ref[3 * step :, tile]])
        part(flags_ref, held, dot(rows, weight_ref[:, tile]), keep_ref, send_ref, tile)


def base_kernel(flags_ref, residual_ref, *refs):
    *parts, out_ref = refs
    odd = flags_ref[2] == 1
    first, left, right = [
        keep[...] + got[...].astype(F32) for keep, got in zip(parts[::2], parts[1::2])
    ]
    step = left.shape[0] // 2
    second = jnp.concatenate([left[:step], right[:step], left[step:], right[step:]])
    block = first.shape[0]
    for at, base in ((0, jnp.where(odd, second, first)), (block, jnp.where(odd, first, second))):
        here = slice(at, at + block)
        out_ref[here, :] = residual_ref[here, :].astype(F32) + base


def final_kernel(base_ref, scaled_ref, scaled_got_ref, hot_ref, ups_ref, out_ref):
    scaled = scaled_ref[...] + scaled_got_ref[...]
    width = ups_ref.shape[1]
    scaled = jnp.concatenate([scaled[:, :width], scaled[:, width:]])
    lora = dot(scaled * hot_ref[0], ups_ref[0])
    for slot in range(1, ups_ref.shape[0]):
        lora += dot(scaled * hot_ref[slot], ups_ref[slot])
    out_ref[...] = (base_ref[...] + lora).astype(BF16)


def line(rows, residual, weight, down, up, tenant, entry, live):
    z, x, c = lax.axis_index("blk"), lax.axis_index("split"), lax.axis_index("sub")
    block_rows = rows.shape[0]
    width = down.shape[1]
    own, cols = residual.shape
    slots = entry.shape[0]
    home = (z // 2) == x
    odd = z % 2 == 1
    half, step = block_rows // 2, block_rows // 4
    barrier = lax.optimization_barrier

    def over_core(value):
        return lax.ppermute(value, "sub", SWAP)

    def over_x(value):
        return lax.ppermute(value, "split", SWAP)

    def along(value, pairs):
        return lax.ppermute(value, "blk", pairs)

    def over_core_in_two(piece):
        count = piece.shape[0] // 2
        return [over_core(piece[:count]), over_core(piece[count:])]

    def parted(count):
        return [shape((count, cols), F32), shape((count, cols), BF16)]

    def lows(count):
        return [shape((count, width), F32)]

    slot_all, live_all = tables(tenant, entry, live)
    slot = lax.dynamic_slice_in_dim(slot_all, x * own, own, 0)
    rank = lax.dynamic_slice_in_dim(live_all, x * own, own, 0)

    flags = jnp.stack([home, c, odd]).astype(jnp.int32)
    kept = jnp.arange(width, dtype=jnp.int32)[None, :] < rank[:, None]
    scale = jnp.where(kept, (width / rank.astype(F32))[:, None], jnp.zeros((), F32))
    scale = jnp.where((slot == z)[:, None], scale, jnp.zeros((), F32))
    scale = jnp.concatenate([scale[:block_rows], scale[block_rows:]], axis=1)
    hot = slot[None, :] == jnp.arange(slots, dtype=jnp.int32)[:, None]
    hot = jnp.broadcast_to(hot[:, :, None], (slots, own, width)).astype(BF16)

    got = lax.ppermute(rows, ("blk", "sub"), by_core(FAR, NEAR))
    held, own_sum, own_low = call(
        own_kernel,
        [shape(weight.shape, BF16), shape((block_rows, cols), F32)] + lows(block_rows),
        [HBM, VMEM, VMEM],
        [weight, down[0], rows],
        [pltpu.SemaphoreType.DMA((len(column_tiles(cols)),))],
        FROM_HBM,
    )
    up, own_sum = barrier((up, own_sum))
    up_other = over_x(up)
    ups = jnp.where(x == 0, jnp.concatenate([up, up_other]), jnp.concatenate([up_other, up]))
    got, own_sum, own_low, ups, hot, scale = barrier((got, own_sum, own_low, ups, hot, scale))

    def cut(at):
        return lax.dynamic_slice_in_dim(got, c * half + at * step, step, 0)

    first_cut = cut(0)
    first_cut, got = barrier((first_cut, got))
    last = [lax.ppermute(piece, ("blk", "sub"), by_core(NEAR, FAR)) for piece in (first_cut, cut(1))]
    others = [over_core(got[at : at + step]) for at in range(0, block_rows, step)]
    kept_a, sent_a, near_sum, low_two = call(
        blocks_kernel,
        parted(block_rows) + [shape((block_rows, cols), F32)] + lows(2 * block_rows),
        [SMEM] + [VMEM] * 8,
        [flags, held, down[0], own_sum, got] + others,
    )
    got_a = over_x(sent_a)
    last[0], kept_a = barrier((last[0], kept_a))

    kept_c, sent_c, piece_low = call(
        piece_kernel,
        parted(half) + lows(half),
        [SMEM] + [VMEM] * 6,
        [flags, held, down[0], near_sum, last[0]] + over_core_in_two(last[0]),
    )
    got_c = over_x(sent_c)
    last[1], near_sum, got_a, piece_low = barrier((last[1], near_sum, got_a, piece_low))

    kept_d, sent_d, low, low_sent = call(
        last_kernel,
        parted(half) + [shape((block_rows, 2 * width), F32)] * 2,
        [SMEM] + [VMEM] * 9,
        [flags, held, down[0], near_sum, own_low, low_two, piece_low, last[1]]
        + over_core_in_two(last[1]),
    )
    got_d = over_x(sent_d)

    scaled = ((low + over_x(low_sent)) * scale).astype(BF16)
    scaled = scaled + along(scaled, NEAR)
    scaled, got_c = barrier((scaled, got_c))
    base = call(
        base_kernel,
        shape(residual.shape, F32),
        [SMEM] + [VMEM] * 7,
        [flags, residual, kept_a, got_a, kept_c, got_c, kept_d, got_d],
    )
    return call(
        final_kernel,
        shape(residual.shape, BF16),
        [VMEM] * 5,
        [base, scaled, along(scaled, FAR), hot, ups],
    )


def shards(rows, residual, weight, down, up, tenant, entry, live):
    sizes = [lax.axis_size(name) for name in ("blk", "split", "sub")]
    plan = line if sizes == [4, 2, 2] and down.shape[0] == 1 else general
    return plan(rows, residual, weight, down, up, tenant, entry, live)


def solution(mesh):
    in_specs = (
        P(("groups", "blk"), "split"),
        P(("groups", "split"), ("blk", "sub")),
        P("split", ("blk", "sub")),
        P("blk", None, "split"),
        P("split", None, ("blk", "sub")),
        P("groups"),
        P(),
        P(),
    )
    out_specs = P(("groups", "split"), ("blk", "sub"))
    return jax.shard_map(shards, mesh=mesh, in_specs=in_specs, out_specs=out_specs, check_vma=False)
```

```python
import jax
import jax.numpy as jnp
from jax import lax
from jax.experimental import pallas as pl
from jax.experimental.pallas import tpu as pltpu
from jax.sharding import PartitionSpec as P

F32 = jnp.float32
BF16 = jnp.bfloat16


def low_rank_weights(low, slot, live, slots, rank_width):
    kept = jnp.arange(rank_width, dtype=jnp.int32)[None, :] < live[:, None]
    scaling = rank_width / live.astype(F32)
    scaled = jnp.where(kept, low * scaling[:, None], jnp.zeros((), F32)).astype(BF16)
    hot = slot[:, None] == jnp.arange(slots, dtype=jnp.int32)[None, :]
    spread = jnp.where(hot[:, :, None], scaled[:, None, :], jnp.zeros((), BF16))
    return spread.reshape(low.shape[0], slots * rank_width)


def tables(tenant, entry, live):
    ids = jnp.arange(entry.shape[0], dtype=jnp.int32)
    hot = (tenant[:, None] == ids[None, :]).astype(jnp.int32)
    return jnp.sum(hot * entry[None, :], axis=1), jnp.sum(hot * live[None, :], axis=1)


def general(rows, residual, weight, down, up, tenant, entry, live):
    own = residual.shape[0]
    cols = weight.shape[1]
    width = down.shape[1]
    slots = entry.shape[0]
    slot_all, live_all = tables(tenant, entry, live)
    part = rows.shape[0] // lax.axis_size("sub")
    mine = lax.dynamic_slice_in_dim(rows, lax.axis_index("sub") * part, part, 0)
    halves = lax.all_gather(lax.all_gather(mine, "blk", axis=0), "sub", axis=1)
    full = halves.reshape(-1, rows.shape[1])
    base = jnp.dot(full, weight, preferred_element_type=F32)
    low = lax.dot_general(
        full, down.reshape(-1, down.shape[2]), (((1,), (1,)), ((), ())), preferred_element_type=F32
    )
    held = down.shape[0]
    places = lax.axis_index("blk") * held + jnp.arange(held, dtype=jnp.int32)
    here = slot_all[:, None] == places[None, :]
    low = jnp.sum(
        jnp.where(here[:, :, None], low.reshape(-1, held, width), jnp.zeros((), F32)), axis=1
    )
    low = lax.psum(lax.psum_scatter(low, "split", scatter_dimension=0, tiled=True), "blk")
    base = lax.psum_scatter(base, "split", scatter_dimension=0, tiled=True)
    start = lax.axis_index("split") * own
    spread = low_rank_weights(
        low,
        lax.dynamic_slice_in_dim(slot_all, start, own, 0),
        lax.dynamic_slice_in_dim(live_all, start, own, 0),
        slots,
        width,
    )
    ups = lax.all_gather(up, "split", axis=0, tiled=True).reshape(slots * width, cols)
    lora = jnp.dot(spread, ups, preferred_element_type=F32)
    return (residual.astype(F32) + base + lora).astype(BF16)


SWAP = [(0, 1), (1, 0)]
NEAR = [(0, 1), (1, 0), (2, 3), (3, 2)]
FAR = [(0, 2), (2, 0), (1, 3), (3, 1)]
LAST = [(0, 3), (3, 0), (1, 2), (2, 1)]


def by_core(first, second):
    return [(2 * a, 2 * b) for a, b in first] + [(2 * a + 1, 2 * b + 1) for a, b in second]


VMEM = pl.BlockSpec(memory_space=pltpu.VMEM)
SMEM = pl.BlockSpec(memory_space=pltpu.SMEM)
HBM = pl.BlockSpec(memory_space=pltpu.HBM)
COST = pl.CostEstimate(flops=0, bytes_accessed=0, transcendentals=0)
PARAMS = pltpu.CompilerParams(vmem_limit_bytes=16 * 1024 * 1024)
FROM_HBM = pltpu.CompilerParams(vmem_limit_bytes=40 * 1024 * 1024)


def shape(dims, dtype):
    return jax.ShapeDtypeStruct(dims, dtype)


def dot(a, b):
    return jnp.dot(a, b, preferred_element_type=F32)


def call(kernel, outs, in_specs, operands, scratch=(), params=PARAMS):
    return pl.pallas_call(
        kernel,
        out_shape=outs,
        in_specs=in_specs,
        out_specs=jax.tree.map(lambda _: VMEM, outs),
        scratch_shapes=scratch,
        compiler_params=params,
        cost_estimate=COST,
    )(*operands)


def column_tiles(cols):
    tile = 256 if cols % 256 == 0 else cols
    return [slice(at, at + tile) for at in range(0, cols, tile)]


def joined(flags_ref, mine, other):
    first = flags_ref[1] == 0
    return jnp.concatenate([jnp.where(first, mine, other), jnp.where(first, other, mine)])


def low_product(rows, down_ref):
    return lax.dot_general(
        rows, down_ref[...], (((1,), (1,)), ((), ())), preferred_element_type=F32
    )


def part(flags_ref, held, value, keep_ref, send_ref, tile):
    home = flags_ref[0] == 1
    keep_ref[:, tile] = jnp.where(home, held, value)
    send_ref[:, tile] = jnp.where(home, value, held).astype(BF16)


def own_kernel(
    weight_ref, down_ref, rows_ref, held_ref, sum_ref, low_ref, sems
):
    tiles = column_tiles(weight_ref.shape[1])
    copies = [
        pltpu.make_async_copy(weight_ref.at[:, tile], held_ref.at[:, tile], sems.at[i])
        for i, tile in enumerate(tiles)
    ]
    for copy in copies:
        copy.start()
    rows = rows_ref[...]
    low_ref[...] = low_product(rows, down_ref)
    for copy, tile in zip(copies, tiles):
        copy.wait()
        sum_ref[:, tile] = dot(rows, held_ref[:, tile])


def far_kernel(
    flags_ref, weight_ref, down_ref, held_ref, mine_ref, first_ref, second_ref,
    keep_ref, send_ref, low_ref,
):
    other = jnp.concatenate([first_ref[...], second_ref[...]])
    rows = joined(flags_ref, mine_ref[...], other)
    low_ref[...] = low_product(rows, down_ref)
    for tile in column_tiles(weight_ref.shape[1]):
        value = dot(rows, weight_ref[:, tile])
        part(flags_ref, held_ref[:, tile], value, keep_ref, send_ref, tile)


def near_kernel(
    flags_ref, weight_ref, down_ref, mine_ref, first_ref, second_ref, last_ref, third_ref,
    fourth_ref, keep_ref, send_ref, hold_ref, low_ref,
):
    other = jnp.concatenate([first_ref[...], second_ref[...]])
    near = joined(flags_ref, mine_ref[...], other)
    last = joined(flags_ref, last_ref[...], jnp.concatenate([third_ref[...], fourth_ref[...]]))
    rows = jnp.concatenate([near, last])
    low_ref[...] = low_product(rows, down_ref)
    step = last_ref.shape[0]
    for tile in column_tiles(weight_ref.shape[1]):
        value = dot(rows, weight_ref[:, tile])
        held = jnp.concatenate([value[:step], value[2 * step : 3 * step]])
        part(flags_ref, held, value[4 * step :], keep_ref, send_ref, tile)
        hold_ref[:, tile] = jnp.concatenate(
            [value[step : 2 * step], value[3 * step : 4 * step]]
        )


def last_kernel(
    flags_ref, weight_ref, down_ref, held_ref, own_low, far_low, near_low, mine_ref, first_ref,
    second_ref, keep_ref, send_ref, low_keep_ref, low_send_ref,
):
    other = jnp.concatenate([first_ref[...], second_ref[...]])
    rows = joined(flags_ref, mine_ref[...], other)
    low = low_product(rows, down_ref)
    block, width = own_low.shape
    step = mine_ref.shape[0]
    last_low = jnp.concatenate(
        [
            near_low[block : block + step], low[:step],
            near_low[block + step :], low[step:],
        ]
    )
    odd, home = flags_ref[2] == 1, flags_ref[0] == 1
    near = own_low[...], near_low[:block]
    far = far_low[...], last_low
    for side, here in ((0, slice(0, width)), (1, slice(width, 2 * width))):
        near_side = jnp.where(odd, near[1 - side], near[side])
        far_side = jnp.where(odd, far[1 - side], far[side])
        low_keep_ref[:, here] = jnp.where(home, near_side, far_side)
        low_send_ref[:, here] = jnp.where(home, far_side, near_side).astype(BF16)
    for tile in column_tiles(weight_ref.shape[1]):
        value = dot(rows, weight_ref[:, tile])
        part(flags_ref, held_ref[:, tile], value, keep_ref, send_ref, tile)


def base_kernel(flags_ref, residual_ref, *refs):
    *parts, out_ref = refs
    odd = flags_ref[2] == 1
    first, left, right = [
        keep[...] + got[...].astype(F32) for keep, got in zip(parts[::2], parts[1::2])
    ]
    step = left.shape[0] // 2
    second = jnp.concatenate([left[:step], right[:step], left[step:], right[step:]])
    block = first.shape[0]
    for at, base in ((0, jnp.where(odd, second, first)), (block, jnp.where(odd, first, second))):
        here = slice(at, at + block)
        out_ref[here, :] = residual_ref[here, :].astype(F32) + base


def final_kernel(base_ref, hot_ref, ups_ref, *refs):
    *parts, out_ref = refs
    scaled = sum(ref[...] for ref in parts)
    width = ups_ref.shape[1]
    scaled = jnp.concatenate([scaled[:, :width], scaled[:, width:]])
    lora = dot(scaled * hot_ref[0], ups_ref[0])
    for slot in range(1, ups_ref.shape[0]):
        lora += dot(scaled * hot_ref[slot], ups_ref[slot])
    out_ref[...] = (base_ref[...] + lora).astype(BF16)


def line(rows, residual, weight, down, up, tenant, entry, live):
    z, x, c = lax.axis_index("blk"), lax.axis_index("split"), lax.axis_index("sub")
    block_rows = rows.shape[0]
    width = down.shape[1]
    own, cols = residual.shape
    slots = entry.shape[0]
    home = (z // 2) == x
    odd = z % 2 == 1
    half, step = block_rows // 2, block_rows // 4
    barrier = lax.optimization_barrier

    def over_core(value):
        return lax.ppermute(value, "sub", SWAP)

    def over_x(value):
        return lax.ppermute(value, "split", SWAP)

    def along(value, pairs):
        return lax.ppermute(value, "blk", pairs)

    def over_core_in_two(piece):
        count = piece.shape[0] // 2
        return [over_core(piece[:count]), over_core(piece[count:])]

    def parted(count):
        return [shape((count, cols), F32), shape((count, cols), BF16)]

    def lows(count):
        return [shape((count, width), F32)]

    slot_all, live_all = tables(tenant, entry, live)
    slot = lax.dynamic_slice_in_dim(slot_all, x * own, own, 0)
    rank = lax.dynamic_slice_in_dim(live_all, x * own, own, 0)

    flags = jnp.stack([home, c, odd]).astype(jnp.int32)
    kept = jnp.arange(width, dtype=jnp.int32)[None, :] < rank[:, None]
    scale = jnp.where(kept, (width / rank.astype(F32))[:, None], jnp.zeros((), F32))
    scale = jnp.where((slot == z)[:, None], scale, jnp.zeros((), F32))
    scale = jnp.concatenate([scale[:block_rows], scale[block_rows:]], axis=1)
    hot = slot[None, :] == jnp.arange(slots, dtype=jnp.int32)[:, None]
    hot = jnp.broadcast_to(hot[:, :, None], (slots, own, width)).astype(BF16)

    mine = lax.dynamic_slice_in_dim(rows, c * half, half, 0)
    near, far = along(mine, NEAR), along(mine, FAR)
    up_other = over_x(up)
    ups = jnp.where(x == 0, jnp.concatenate([up, up_other]), jnp.concatenate([up_other, up]))
    held, own_sum, own_low = call(
        own_kernel,
        [shape(weight.shape, BF16), shape((block_rows, cols), F32)] + lows(block_rows),
        [HBM, VMEM, VMEM],
        [weight, down[0], rows],
        [pltpu.SemaphoreType.DMA((len(column_tiles(cols)),))],
        FROM_HBM,
    )
    near, far, own_sum, own_low, ups, hot, scale = barrier(
        (near, far, own_sum, own_low, ups, hot, scale)
    )

    last = [along(far[:step], NEAR)]
    far_others = over_core_in_two(far)
    far_second, far_others[0] = barrier((far[step:], far_others[0]))
    last.append(along(far_second, NEAR))
    kept_a, sent_a, far_low = call(
        far_kernel,
        parted(block_rows) + lows(block_rows),
        [SMEM] + [VMEM] * 6,
        [flags, held, down[0], own_sum, far] + far_others,
    )
    got_a = over_x(sent_a)
    last[0], kept_a = barrier((last[0], kept_a))

    kept_c, sent_c, hold, near_low = call(
        near_kernel,
        parted(half) + [shape((half, cols), F32)] + lows(block_rows + half),
        [SMEM] + [VMEM] * 8,
        [flags, held, down[0], near] + over_core_in_two(near)
        + [last[0]] + over_core_in_two(last[0]),
    )
    got_c = over_x(sent_c)
    last[1], hold, got_a, near_low = barrier((last[1], hold, got_a, near_low))

    kept_d, sent_d, low, low_sent = call(
        last_kernel,
        parted(half) + [shape((block_rows, 2 * width), dtype) for dtype in (F32, BF16)],
        [SMEM] + [VMEM] * 9,
        [flags, held, down[0], hold, own_low, far_low, near_low, last[1]]
        + over_core_in_two(last[1]),
    )
    got_d = over_x(sent_d)

    scaled = ((low + over_x(low_sent).astype(F32)) * scale).astype(BF16)
    scaled_got = [
        lax.ppermute(scaled, ("blk", "sub"), by_core(NEAR, FAR)),
        along(scaled, LAST),
    ]
    scaled_got.append(over_core(scaled_got[0]))
    base = call(
        base_kernel,
        shape(residual.shape, F32),
        [SMEM] + [VMEM] * 7,
        [flags, residual, kept_a, got_a, kept_c, got_c, kept_d, got_d],
    )
    return call(
        final_kernel,
        shape(residual.shape, BF16),
        [VMEM] * 7,
        [base, hot, ups, scaled] + scaled_got,
    )


def shards(rows, residual, weight, down, up, tenant, entry, live):
    sizes = [lax.axis_size(name) for name in ("blk", "split", "sub")]
    plan = line if sizes == [4, 2, 2] and down.shape[0] == 1 else general
    return plan(rows, residual, weight, down, up, tenant, entry, live)


def solution(mesh):
    in_specs = (
        P(("groups", "blk"), "split"),
        P(("groups", "split"), ("blk", "sub")),
        P("split", ("blk", "sub")),
        P("blk", None, "split"),
        P("split", None, ("blk", "sub")),
        P("groups"),
        P(),
        P(),
    )
    out_specs = P(("groups", "split"), ("blk", "sub"))
    return jax.shard_map(shards, mesh=mesh, in_specs=in_specs, out_specs=out_specs, check_vma=False)
```

```python
import functools

import jax
import jax.numpy as jnp
from jax import lax
from jax.experimental import pallas as pl
from jax.experimental.pallas import tpu as pltpu
from jax.sharding import PartitionSpec as P

F32 = jnp.float32
BF16 = jnp.bfloat16


def low_rank_weights(low, slot, live, slots, rank_width):
    kept = jnp.arange(rank_width, dtype=jnp.int32)[None, :] < live[:, None]
    scaling = rank_width / live.astype(F32)
    scaled = jnp.where(kept, low * scaling[:, None], jnp.zeros((), F32)).astype(BF16)
    hot = slot[:, None] == jnp.arange(slots, dtype=jnp.int32)[None, :]
    spread = jnp.where(hot[:, :, None], scaled[:, None, :], jnp.zeros((), BF16))
    return spread.reshape(low.shape[0], slots * rank_width)


def tables(tenant, entry, live):
    ids = jnp.arange(entry.shape[0], dtype=jnp.int32)
    hot = (tenant[:, None] == ids[None, :]).astype(jnp.int32)
    return jnp.sum(hot * entry[None, :], axis=1), jnp.sum(hot * live[None, :], axis=1)


def general(rows, residual, weight, down, up, tenant, entry, live):
    own = residual.shape[0]
    cols = weight.shape[1]
    width = down.shape[1]
    slots = entry.shape[0]
    slot_all, live_all = tables(tenant, entry, live)
    part = rows.shape[0] // lax.axis_size("sub")
    mine = lax.dynamic_slice_in_dim(rows, lax.axis_index("sub") * part, part, 0)
    halves = lax.all_gather(lax.all_gather(mine, "blk", axis=0), "sub", axis=1)
    full = halves.reshape(-1, rows.shape[1])
    base = jnp.dot(full, weight, preferred_element_type=F32)
    low = lax.dot_general(
        full, down.reshape(-1, down.shape[2]), (((1,), (1,)), ((), ())), preferred_element_type=F32
    )
    held = down.shape[0]
    places = lax.axis_index("blk") * held + jnp.arange(held, dtype=jnp.int32)
    here = slot_all[:, None] == places[None, :]
    low = jnp.sum(
        jnp.where(here[:, :, None], low.reshape(-1, held, width), jnp.zeros((), F32)), axis=1
    )
    low = lax.psum(lax.psum_scatter(low, "split", scatter_dimension=0, tiled=True), "blk")
    base = lax.psum_scatter(base, "split", scatter_dimension=0, tiled=True)
    start = lax.axis_index("split") * own
    spread = low_rank_weights(
        low,
        lax.dynamic_slice_in_dim(slot_all, start, own, 0),
        lax.dynamic_slice_in_dim(live_all, start, own, 0),
        slots,
        width,
    )
    ups = lax.all_gather(up, "split", axis=0, tiled=True).reshape(slots * width, cols)
    lora = jnp.dot(spread, ups, preferred_element_type=F32)
    return (residual.astype(F32) + base + lora).astype(BF16)


SWAP = [(0, 1), (1, 0)]
NEAR = [(0, 1), (1, 0), (2, 3), (3, 2)]
FAR = [(0, 2), (2, 0), (1, 3), (3, 1)]
LAST = [(0, 3), (3, 0), (1, 2), (2, 1)]


def by_core(first, second):
    return [(2 * a, 2 * b) for a, b in first] + [(2 * a + 1, 2 * b + 1) for a, b in second]


VMEM = pl.BlockSpec(memory_space=pltpu.VMEM)
SMEM = pl.BlockSpec(memory_space=pltpu.SMEM)
HBM = pl.BlockSpec(memory_space=pltpu.HBM)
COST = pl.CostEstimate(flops=0, bytes_accessed=0, transcendentals=0)
PARAMS = pltpu.CompilerParams(vmem_limit_bytes=16 * 1024 * 1024)
FROM_HBM = pltpu.CompilerParams(vmem_limit_bytes=40 * 1024 * 1024)


def shape(dims, dtype):
    return jax.ShapeDtypeStruct(dims, dtype)


def dot(a, b):
    return jnp.dot(a, b, preferred_element_type=F32)


def call(kernel, outs, in_specs, operands, scratch=(), params=PARAMS):
    return pl.pallas_call(
        kernel,
        out_shape=outs,
        in_specs=in_specs,
        out_specs=jax.tree.map(lambda _: VMEM, outs),
        scratch_shapes=scratch,
        compiler_params=params,
        cost_estimate=COST,
    )(*operands)


def column_tiles(cols):
    tile = 256 if cols % 256 == 0 else cols
    return [slice(at, at + tile) for at in range(0, cols, tile)]


def joined(flags_ref, mine, other):
    first = flags_ref[1] == 0
    return jnp.concatenate([jnp.where(first, mine, other), jnp.where(first, other, mine)])


def low_product(rows, down_ref):
    return lax.dot_general(
        rows, down_ref[...], (((1,), (1,)), ((), ())), preferred_element_type=F32
    )


def part(flags_ref, held, value, keep_ref, send_ref, tile):
    home = flags_ref[0] == 1
    keep_ref[:, tile] = jnp.where(home, held, value)
    send_ref[:, tile] = jnp.where(home, value, held).astype(BF16)


def own_kernel(
    weight_ref, down_ref, rows_ref, held_ref, sum_ref, low_ref, sems
):
    tiles = column_tiles(weight_ref.shape[1])
    copies = [
        pltpu.make_async_copy(weight_ref.at[:, tile], held_ref.at[:, tile], sems.at[i])
        for i, tile in enumerate(tiles)
    ]
    for copy in copies:
        copy.start()
    rows = rows_ref[...]
    low_ref[...] = low_product(rows, down_ref)
    for copy, tile in zip(copies, tiles):
        copy.wait()
        sum_ref[:, tile] = dot(rows, held_ref[:, tile])


def rows_of(piece, step):
    return [slice((2 * core + piece) * step, (2 * core + piece + 1) * step) for core in (0, 1)]


def in_block(first, second):
    step = first.shape[0] // 2
    return jnp.concatenate([first[:step], second[:step], first[step:], second[step:]])


def piece_kernel(
    piece, flags_ref, weight_ref, down_ref, held_ref, mine_ref, first_ref, second_ref,
    keep_ref, send_ref, low_ref,
):
    other = jnp.concatenate([first_ref[...], second_ref[...]])
    rows = joined(flags_ref, mine_ref[...], other)
    low_ref[...] = low_product(rows, down_ref)
    here = rows_of(piece, mine_ref.shape[0])
    for tile in column_tiles(weight_ref.shape[1]):
        held = jnp.concatenate([held_ref[at, tile] for at in here])
        part(flags_ref, held, dot(rows, weight_ref[:, tile]), keep_ref, send_ref, tile)


def near_kernel(
    flags_ref, weight_ref, down_ref, held_ref, mine_ref, first_ref, second_ref, near_ref,
    near_too_ref, third_ref, fourth_ref, keep_ref, send_ref, near_sum_ref, low_ref,
):
    other = jnp.concatenate([first_ref[...], second_ref[...]])
    far = joined(flags_ref, mine_ref[...], other)
    mine = jnp.concatenate([near_ref[...], near_too_ref[...]])
    other = jnp.concatenate([third_ref[...], fourth_ref[...]])
    near = joined(flags_ref, mine, other)
    rows = jnp.concatenate([near, far])
    low_ref[...] = low_product(rows, down_ref)
    here = rows_of(1, mine_ref.shape[0])
    block = near.shape[0]
    for tile in column_tiles(weight_ref.shape[1]):
        value = dot(rows, weight_ref[:, tile])
        near_sum_ref[:, tile] = value[:block]
        held = jnp.concatenate([held_ref[at, tile] for at in here])
        part(flags_ref, held, value[block:], keep_ref, send_ref, tile)


def last_kernel(
    flags_ref, weight_ref, down_ref, held_ref, own_low, low_a, low_b, low_c, mine_ref, first_ref,
    second_ref, keep_ref, send_ref, low_keep_ref, low_send_ref,
):
    other = jnp.concatenate([first_ref[...], second_ref[...]])
    rows = joined(flags_ref, mine_ref[...], other)
    low = low_product(rows, down_ref)
    block, width = own_low.shape
    odd, home = flags_ref[2] == 1, flags_ref[0] == 1
    near = own_low[...], low_b[:block]
    far = in_block(low_a[...], low_b[block:]), in_block(low_c[...], low)
    for side, here in ((0, slice(0, width)), (1, slice(width, 2 * width))):
        near_side = jnp.where(odd, near[1 - side], near[side])
        far_side = jnp.where(odd, far[1 - side], far[side])
        low_keep_ref[:, here] = jnp.where(home, near_side, far_side)
        low_send_ref[:, here] = jnp.where(home, far_side, near_side).astype(BF16)
    here = rows_of(1, mine_ref.shape[0])
    for tile in column_tiles(weight_ref.shape[1]):
        held = jnp.concatenate([held_ref[at, tile] for at in here])
        part(flags_ref, held, dot(rows, weight_ref[:, tile]), keep_ref, send_ref, tile)


def base_kernel(flags_ref, residual_ref, *refs):
    *parts, out_ref = refs
    odd = flags_ref[2] == 1
    sums = [keep[...] + got[...].astype(F32) for keep, got in zip(parts[::2], parts[1::2])]
    first, second = in_block(*sums[:2]), in_block(*sums[2:])
    block = first.shape[0]
    for at, base in ((0, jnp.where(odd, second, first)), (block, jnp.where(odd, first, second))):
        here = slice(at, at + block)
        out_ref[here, :] = residual_ref[here, :].astype(F32) + base


def final_kernel(base_ref, hot_ref, ups_ref, *refs):
    *parts, out_ref = refs
    scaled = sum(ref[...] for ref in parts)
    width = ups_ref.shape[1]
    scaled = jnp.concatenate([scaled[:, :width], scaled[:, width:]])
    lora = dot(scaled * hot_ref[0], ups_ref[0])
    for slot in range(1, ups_ref.shape[0]):
        lora += dot(scaled * hot_ref[slot], ups_ref[slot])
    out_ref[...] = (base_ref[...] + lora).astype(BF16)


def line(rows, residual, weight, down, up, tenant, entry, live):
    z, x, c = lax.axis_index("blk"), lax.axis_index("split"), lax.axis_index("sub")
    block_rows = rows.shape[0]
    width = down.shape[1]
    own, cols = residual.shape
    slots = entry.shape[0]
    home = (z // 2) == x
    odd = z % 2 == 1
    half, step = block_rows // 2, block_rows // 4
    barrier = lax.optimization_barrier

    def over_core(value):
        return lax.ppermute(value, "sub", SWAP)

    def over_x(value):
        return lax.ppermute(value, "split", SWAP)

    def along(value, pairs):
        return lax.ppermute(value, "blk", pairs)

    def over_core_in_two(piece):
        count = piece.shape[0] // 2
        return [over_core(piece[:count]), over_core(piece[count:])]

    def parted(count):
        return [shape((count, cols), F32), shape((count, cols), BF16)]

    def lows(count):
        return [shape((count, width), F32)]

    slot_all, live_all = tables(tenant, entry, live)
    slot = lax.dynamic_slice_in_dim(slot_all, x * own, own, 0)
    rank = lax.dynamic_slice_in_dim(live_all, x * own, own, 0)

    flags = jnp.stack([home, c, odd]).astype(jnp.int32)
    kept = jnp.arange(width, dtype=jnp.int32)[None, :] < rank[:, None]
    scale = jnp.where(kept, (width / rank.astype(F32))[:, None], jnp.zeros((), F32))
    scale = jnp.where((slot == z)[:, None], scale, jnp.zeros((), F32))
    scale = jnp.concatenate([scale[:block_rows], scale[block_rows:]], axis=1)
    hot = slot[None, :] == jnp.arange(slots, dtype=jnp.int32)[:, None]
    hot = jnp.broadcast_to(hot[:, :, None], (slots, own, width)).astype(BF16)

    def cut(rows, piece):
        return lax.dynamic_slice_in_dim(rows, c * half + piece * step, step, 0)

    mine = cut(rows, 0)
    far, near = [along(mine, FAR)], [along(mine, NEAR)]
    held, own_sum, own_low = call(
        own_kernel,
        [shape(weight.shape, BF16), shape((block_rows, cols), F32)] + lows(block_rows),
        [HBM, VMEM, VMEM],
        [weight, down[0], rows],
        [pltpu.SemaphoreType.DMA((len(column_tiles(cols)),))],
        FROM_HBM,
    )
    up, rows, own_sum = barrier((up, rows, own_sum))
    mine = cut(rows, 1)
    far.append(along(mine, FAR))
    near.append(along(mine, NEAR))
    up_other = over_x(up)
    ups = jnp.where(x == 0, jnp.concatenate([up, up_other]), jnp.concatenate([up_other, up]))
    far[0], own_sum, own_low = barrier((far[0], own_sum, own_low))

    def parted_piece(piece, against, value):
        return call(
            functools.partial(piece_kernel, piece),
            parted(half) + lows(half),
            [SMEM] + [VMEM] * 6,
            [flags, held, down[0], against, value] + over_core_in_two(value),
        )

    last = [along(far[0], NEAR)]
    kept_a, sent_a, low_a = parted_piece(0, own_sum, far[0])
    got_a = jnp.concatenate([over_x(sent_a[:step]), over_x(sent_a[step:])])
    near, far[1], own_sum, ups, hot, scale, got_a = barrier(
        (near, far[1], own_sum, ups, hot, scale, got_a)
    )

    last.append(along(far[1], NEAR))
    kept_b, sent_b, near_sum, low_b = call(
        near_kernel,
        parted(half) + [shape((block_rows, cols), F32)] + lows(block_rows + half),
        [SMEM] + [VMEM] * 10,
        [flags, held, down[0], own_sum, far[1]] + over_core_in_two(far[1])
        + near + [over_core(piece) for piece in near],
    )
    got_b = over_x(sent_b)
    last[0], kept_b = barrier((last[0], kept_b))

    kept_c, sent_c, low_c = parted_piece(0, near_sum, last[0])
    got_c = over_x(sent_c)
    last[1], near_sum, got_b, low_c = barrier((last[1], near_sum, got_b, low_c))

    kept_d, sent_d, low, low_sent = call(
        last_kernel,
        parted(half) + [shape((block_rows, 2 * width), dtype) for dtype in (F32, BF16)],
        [SMEM] + [VMEM] * 10,
        [flags, held, down[0], near_sum, own_low, low_a, low_b, low_c, last[1]]
        + over_core_in_two(last[1]),
    )
    got_d = over_x(sent_d)

    scaled = ((low + over_x(low_sent).astype(F32)) * scale).astype(BF16)
    scaled_got = [
        lax.ppermute(scaled, ("blk", "sub"), by_core(NEAR, FAR)),
        along(scaled, LAST),
    ]
    scaled_got.append(over_core(scaled_got[0]))
    base = call(
        base_kernel,
        shape(residual.shape, F32),
        [SMEM] + [VMEM] * 9,
        [flags, residual, kept_a, got_a, kept_b, got_b, kept_c, got_c, kept_d, got_d],
    )
    return call(
        final_kernel,
        shape(residual.shape, BF16),
        [VMEM] * 7,
        [base, hot, ups, scaled] + scaled_got,
    )


def shards(rows, residual, weight, down, up, tenant, entry, live):
    sizes = [lax.axis_size(name) for name in ("blk", "split", "sub")]
    plan = line if sizes == [4, 2, 2] and down.shape[0] == 1 else general
    return plan(rows, residual, weight, down, up, tenant, entry, live)


def solution(mesh):
    in_specs = (
        P(("groups", "blk"), "split"),
        P(("groups", "split"), ("blk", "sub")),
        P("split", ("blk", "sub")),
        P("blk", None, "split"),
        P("split", None, ("blk", "sub")),
        P("groups"),
        P(),
        P(),
    )
    out_specs = P(("groups", "split"), ("blk", "sub"))
    return jax.shard_map(shards, mesh=mesh, in_specs=in_specs, out_specs=out_specs, check_vma=False)
```

```python
import functools

import jax
import jax.numpy as jnp
from jax import lax
from jax.experimental import pallas as pl
from jax.experimental.pallas import tpu as pltpu
from jax.sharding import PartitionSpec as P

F32 = jnp.float32
BF16 = jnp.bfloat16


def low_rank_weights(low, slot, live, slots, rank_width):
    kept = jnp.arange(rank_width, dtype=jnp.int32)[None, :] < live[:, None]
    scaling = rank_width / live.astype(F32)
    scaled = jnp.where(kept, low * scaling[:, None], jnp.zeros((), F32)).astype(BF16)
    hot = slot[:, None] == jnp.arange(slots, dtype=jnp.int32)[None, :]
    spread = jnp.where(hot[:, :, None], scaled[:, None, :], jnp.zeros((), BF16))
    return spread.reshape(low.shape[0], slots * rank_width)


def tables(tenant, entry, live):
    ids = jnp.arange(entry.shape[0], dtype=jnp.int32)
    hot = (tenant[:, None] == ids[None, :]).astype(jnp.int32)
    return jnp.sum(hot * entry[None, :], axis=1), jnp.sum(hot * live[None, :], axis=1)


def general(rows, residual, weight, down, up, tenant, entry, live):
    own = residual.shape[0]
    cols = weight.shape[1]
    width = down.shape[1]
    slots = entry.shape[0]
    slot_all, live_all = tables(tenant, entry, live)
    part = rows.shape[0] // lax.axis_size("sub")
    mine = lax.dynamic_slice_in_dim(rows, lax.axis_index("sub") * part, part, 0)
    halves = lax.all_gather(lax.all_gather(mine, "blk", axis=0), "sub", axis=1)
    full = halves.reshape(-1, rows.shape[1])
    base = jnp.dot(full, weight, preferred_element_type=F32)
    low = lax.dot_general(
        full, down.reshape(-1, down.shape[2]), (((1,), (1,)), ((), ())), preferred_element_type=F32
    )
    held = down.shape[0]
    places = lax.axis_index("blk") * held + jnp.arange(held, dtype=jnp.int32)
    here = slot_all[:, None] == places[None, :]
    low = jnp.sum(
        jnp.where(here[:, :, None], low.reshape(-1, held, width), jnp.zeros((), F32)), axis=1
    )
    low = lax.psum(lax.psum_scatter(low, "split", scatter_dimension=0, tiled=True), "blk")
    base = lax.psum_scatter(base, "split", scatter_dimension=0, tiled=True)
    start = lax.axis_index("split") * own
    spread = low_rank_weights(
        low,
        lax.dynamic_slice_in_dim(slot_all, start, own, 0),
        lax.dynamic_slice_in_dim(live_all, start, own, 0),
        slots,
        width,
    )
    ups = lax.all_gather(up, "split", axis=0, tiled=True).reshape(slots * width, cols)
    lora = jnp.dot(spread, ups, preferred_element_type=F32)
    return (residual.astype(F32) + base + lora).astype(BF16)


SWAP = [(0, 1), (1, 0)]
NEAR = [(0, 1), (1, 0), (2, 3), (3, 2)]
FAR = [(0, 2), (2, 0), (1, 3), (3, 1)]
LAST = [(0, 3), (3, 0), (1, 2), (2, 1)]


def by_core(first, second):
    return [(2 * a, 2 * b) for a, b in first] + [(2 * a + 1, 2 * b + 1) for a, b in second]


VMEM = pl.BlockSpec(memory_space=pltpu.VMEM)
SMEM = pl.BlockSpec(memory_space=pltpu.SMEM)
HBM = pl.BlockSpec(memory_space=pltpu.HBM)
COST = pl.CostEstimate(flops=0, bytes_accessed=0, transcendentals=0)
PARAMS = pltpu.CompilerParams(vmem_limit_bytes=16 * 1024 * 1024)
FROM_HBM = pltpu.CompilerParams(vmem_limit_bytes=40 * 1024 * 1024)


def shape(dims, dtype):
    return jax.ShapeDtypeStruct(dims, dtype)


def dot(a, b):
    return jnp.dot(a, b, preferred_element_type=F32)


def call(kernel, outs, in_specs, operands, scratch=(), params=PARAMS):
    return pl.pallas_call(
        kernel,
        out_shape=outs,
        in_specs=in_specs,
        out_specs=jax.tree.map(lambda _: VMEM, outs),
        scratch_shapes=scratch,
        compiler_params=params,
        cost_estimate=COST,
    )(*operands)


def column_tiles(cols):
    tile = 256 if cols % 256 == 0 else cols
    return [slice(at, at + tile) for at in range(0, cols, tile)]


def joined(flags_ref, mine, other):
    first = flags_ref[1] == 0
    return jnp.concatenate([jnp.where(first, mine, other), jnp.where(first, other, mine)])


def low_product(rows, down_ref):
    return lax.dot_general(
        rows, down_ref[...], (((1,), (1,)), ((), ())), preferred_element_type=F32
    )


def part(flags_ref, held, value, keep_ref, send_ref, tile):
    home = flags_ref[0] == 1
    keep_ref[:, tile] = jnp.where(home, held, value)
    send_ref[:, tile] = jnp.where(home, value, held).astype(BF16)


def own_kernel(
    weight_ref, down_ref, rows_ref, held_ref, sum_ref, low_ref, sems
):
    tiles = column_tiles(weight_ref.shape[1])
    copies = [
        pltpu.make_async_copy(weight_ref.at[:, tile], held_ref.at[:, tile], sems.at[i])
        for i, tile in enumerate(tiles)
    ]
    for copy in copies:
        copy.start()
    rows = rows_ref[...]
    low_ref[...] = low_product(rows, down_ref)
    for copy, tile in zip(copies, tiles):
        copy.wait()
        sum_ref[:, tile] = dot(rows, held_ref[:, tile])


def rows_of(piece, step):
    return [slice((2 * core + piece) * step, (2 * core + piece + 1) * step) for core in (0, 1)]


def in_block(first, second):
    step = first.shape[0] // 2
    return jnp.concatenate([first[:step], second[:step], first[step:], second[step:]])


def piece_kernel(
    piece, flags_ref, weight_ref, down_ref, held_ref, mine_ref, first_ref, second_ref,
    keep_ref, send_ref, low_ref,
):
    other = jnp.concatenate([first_ref[...], second_ref[...]])
    rows = joined(flags_ref, mine_ref[...], other)
    low_ref[...] = low_product(rows, down_ref)
    here = rows_of(piece, mine_ref.shape[0])
    for tile in column_tiles(weight_ref.shape[1]):
        held = jnp.concatenate([held_ref[at, tile] for at in here])
        part(flags_ref, held, dot(rows, weight_ref[:, tile]), keep_ref, send_ref, tile)


def near_kernel(
    flags_ref, weight_ref, down_ref, held_ref, mine_ref, first_ref, second_ref, near_ref,
    near_too_ref, third_ref, fourth_ref, keep_ref, send_ref, near_sum_ref, low_ref,
):
    other = jnp.concatenate([first_ref[...], second_ref[...]])
    far = joined(flags_ref, mine_ref[...], other)
    mine = jnp.concatenate([near_ref[...], near_too_ref[...]])
    other = jnp.concatenate([third_ref[...], fourth_ref[...]])
    near = joined(flags_ref, mine, other)
    rows = jnp.concatenate([near, far])
    low_ref[...] = low_product(rows, down_ref)
    here = rows_of(1, mine_ref.shape[0])
    block = near.shape[0]
    for tile in column_tiles(weight_ref.shape[1]):
        value = dot(rows, weight_ref[:, tile])
        near_sum_ref[:, tile] = value[:block]
        held = jnp.concatenate([held_ref[at, tile] for at in here])
        part(flags_ref, held, value[block:], keep_ref, send_ref, tile)


def last_kernel(
    flags_ref, weight_ref, down_ref, held_ref, own_low, low_a, low_b, low_c, mine_ref, first_ref,
    second_ref, keep_ref, send_ref, low_keep_ref, low_send_ref,
):
    other = jnp.concatenate([first_ref[...], second_ref[...]])
    rows = joined(flags_ref, mine_ref[...], other)
    low = low_product(rows, down_ref)
    block, width = own_low.shape
    odd, home = flags_ref[2] == 1, flags_ref[0] == 1
    near = own_low[...], low_b[:block]
    far = in_block(low_a[...], low_b[block:]), in_block(low_c[...], low)
    for side, here in ((0, slice(0, width)), (1, slice(width, 2 * width))):
        near_side = jnp.where(odd, near[1 - side], near[side])
        far_side = jnp.where(odd, far[1 - side], far[side])
        low_keep_ref[:, here] = jnp.where(home, near_side, far_side)
        low_send_ref[:, here] = jnp.where(home, far_side, near_side).astype(BF16)
    here = rows_of(1, mine_ref.shape[0])
    for tile in column_tiles(weight_ref.shape[1]):
        held = jnp.concatenate([held_ref[at, tile] for at in here])
        part(flags_ref, held, dot(rows, weight_ref[:, tile]), keep_ref, send_ref, tile)


def base_kernel(flags_ref, residual_ref, *refs):
    *parts, out_ref = refs
    odd = flags_ref[2] == 1
    sums = [keep[...] + got[...].astype(F32) for keep, got in zip(parts[::2], parts[1::2])]
    first, second = in_block(*sums[:2]), in_block(*sums[2:])
    block = first.shape[0]
    for at, base in ((0, jnp.where(odd, second, first)), (block, jnp.where(odd, first, second))):
        here = slice(at, at + block)
        out_ref[here, :] = residual_ref[here, :].astype(F32) + base


def final_kernel(base_ref, hot_ref, ups_ref, *refs):
    *parts, out_ref = refs
    scaled = sum(ref[...] for ref in parts)
    width = ups_ref.shape[1]
    scaled = jnp.concatenate([scaled[:, :width], scaled[:, width:]])
    lora = dot(scaled * hot_ref[0], ups_ref[0])
    for slot in range(1, ups_ref.shape[0]):
        lora += dot(scaled * hot_ref[slot], ups_ref[slot])
    out_ref[...] = (base_ref[...] + lora).astype(BF16)


def line(rows, residual, weight, down, up, tenant, entry, live):
    z, x, c = lax.axis_index("blk"), lax.axis_index("split"), lax.axis_index("sub")
    block_rows = rows.shape[0]
    width = down.shape[1]
    own, cols = residual.shape
    slots = entry.shape[0]
    home = (z // 2) == x
    odd = z % 2 == 1
    half, step = block_rows // 2, block_rows // 4
    barrier = lax.optimization_barrier

    def over_core(value):
        return lax.ppermute(value, "sub", SWAP)

    def over_x(value):
        return lax.ppermute(value, "split", SWAP)

    def along(value, pairs):
        return lax.ppermute(value, "blk", pairs)

    def over_core_in_two(piece):
        count = piece.shape[0] // 2
        return [over_core(piece[:count]), over_core(piece[count:])]

    def parted(count):
        return [shape((count, cols), F32), shape((count, cols), BF16)]

    def lows(count):
        return [shape((count, width), F32)]

    slot_all, live_all = tables(tenant, entry, live)
    slot = lax.dynamic_slice_in_dim(slot_all, x * own, own, 0)
    rank = lax.dynamic_slice_in_dim(live_all, x * own, own, 0)

    flags = jnp.stack([home, c, odd]).astype(jnp.int32)
    kept = jnp.arange(width, dtype=jnp.int32)[None, :] < rank[:, None]
    scale = jnp.where(kept, (width / rank.astype(F32))[:, None], jnp.zeros((), F32))
    scale = jnp.where((slot == z)[:, None], scale, jnp.zeros((), F32))
    scale = jnp.concatenate([scale[:block_rows], scale[block_rows:]], axis=1)
    hot = slot[None, :] == jnp.arange(slots, dtype=jnp.int32)[:, None]
    hot = jnp.broadcast_to(hot[:, :, None], (slots, own, width)).astype(BF16)

    def cut(rows, piece):
        return lax.dynamic_slice_in_dim(rows, c * half + piece * step, step, 0)

    mine = cut(rows, 0)
    rows, hot, scale = barrier((rows, hot, scale))
    far, near = [along(mine, FAR)], [along(mine, NEAR)]
    held, own_sum, own_low = call(
        own_kernel,
        [shape(weight.shape, BF16), shape((block_rows, cols), F32)] + lows(block_rows),
        [HBM, VMEM, VMEM],
        [weight, down[0], rows],
        [pltpu.SemaphoreType.DMA((len(column_tiles(cols)),))],
        FROM_HBM,
    )
    up, rows, own_sum = barrier((up, rows, own_sum))
    mine = cut(rows, 1)
    far.append(along(mine, FAR))
    near.append(along(mine, NEAR))
    up_other = over_x(up)
    ups = jnp.where(x == 0, jnp.concatenate([up, up_other]), jnp.concatenate([up_other, up]))
    far[0], own_sum, own_low = barrier((far[0], own_sum, own_low))

    def parted_piece(piece, against, value):
        return call(
            functools.partial(piece_kernel, piece),
            parted(half) + lows(half),
            [SMEM] + [VMEM] * 6,
            [flags, held, down[0], against, value] + over_core_in_two(value),
        )

    last = [along(far[0], NEAR)]
    kept_a, sent_a, low_a = parted_piece(0, own_sum, far[0])
    got_a = over_x(sent_a)
    near, far[1], own_sum, ups, kept_a = barrier((near, far[1], own_sum, ups, kept_a))

    last.append(along(far[1], NEAR))
    kept_b, sent_b, near_sum, low_b = call(
        near_kernel,
        parted(half) + [shape((block_rows, cols), F32)] + lows(block_rows + half),
        [SMEM] + [VMEM] * 10,
        [flags, held, down[0], own_sum, far[1]] + over_core_in_two(far[1])
        + near + [over_core(piece) for piece in near],
    )
    sent_b, got_a = barrier((sent_b, got_a))
    got_b = over_x(sent_b)
    last[0], kept_b = barrier((last[0], kept_b))

    kept_c, sent_c, low_c = parted_piece(0, near_sum, last[0])
    got_c = over_x(sent_c)
    last[1], near_sum, got_b, low_c = barrier((last[1], near_sum, got_b, low_c))

    kept_d, sent_d, low, low_sent = call(
        last_kernel,
        parted(half) + [shape((block_rows, 2 * width), dtype) for dtype in (F32, BF16)],
        [SMEM] + [VMEM] * 10,
        [flags, held, down[0], near_sum, own_low, low_a, low_b, low_c, last[1]]
        + over_core_in_two(last[1]),
    )
    got_d = over_x(sent_d)

    scaled = ((low + over_x(low_sent).astype(F32)) * scale).astype(BF16)
    scaled_got = [
        lax.ppermute(scaled, ("blk", "sub"), by_core(NEAR, FAR)),
        along(scaled, LAST),
    ]
    scaled_got.append(over_core(scaled_got[0]))
    base = call(
        base_kernel,
        shape(residual.shape, F32),
        [SMEM] + [VMEM] * 9,
        [flags, residual, kept_a, got_a, kept_b, got_b, kept_c, got_c, kept_d, got_d],
    )
    return call(
        final_kernel,
        shape(residual.shape, BF16),
        [VMEM] * 7,
        [base, hot, ups, scaled] + scaled_got,
    )


def shards(rows, residual, weight, down, up, tenant, entry, live):
    sizes = [lax.axis_size(name) for name in ("blk", "split", "sub")]
    plan = line if sizes == [4, 2, 2] and down.shape[0] == 1 else general
    return plan(rows, residual, weight, down, up, tenant, entry, live)


def solution(mesh):
    in_specs = (
        P(("groups", "blk"), "split"),
        P(("groups", "split"), ("blk", "sub")),
        P("split", ("blk", "sub")),
        P("blk", None, "split"),
        P("split", None, ("blk", "sub")),
        P("groups"),
        P(),
        P(),
    )
    out_specs = P(("groups", "split"), ("blk", "sub"))
    return jax.shard_map(shards, mesh=mesh, in_specs=in_specs, out_specs=out_specs, check_vma=False)
```

```python
import functools

import jax
import jax.numpy as jnp
from jax import lax
from jax.experimental import pallas as pl
from jax.experimental.pallas import tpu as pltpu
from jax.sharding import PartitionSpec as P

F32 = jnp.float32
BF16 = jnp.bfloat16


def low_rank_weights(low, slot, live, slots, rank_width):
    kept = jnp.arange(rank_width, dtype=jnp.int32)[None, :] < live[:, None]
    scaling = rank_width / live.astype(F32)
    scaled = jnp.where(kept, low * scaling[:, None], jnp.zeros((), F32)).astype(BF16)
    hot = slot[:, None] == jnp.arange(slots, dtype=jnp.int32)[None, :]
    spread = jnp.where(hot[:, :, None], scaled[:, None, :], jnp.zeros((), BF16))
    return spread.reshape(low.shape[0], slots * rank_width)


def tables(tenant, entry, live):
    ids = jnp.arange(entry.shape[0], dtype=jnp.int32)
    hot = (tenant[:, None] == ids[None, :]).astype(jnp.int32)
    return jnp.sum(hot * entry[None, :], axis=1), jnp.sum(hot * live[None, :], axis=1)


def general(rows, residual, weight, down, up, tenant, entry, live):
    own = residual.shape[0]
    cols = weight.shape[1]
    width = down.shape[1]
    slots = entry.shape[0]
    slot_all, live_all = tables(tenant, entry, live)
    part = rows.shape[0] // lax.axis_size("sub")
    mine = lax.dynamic_slice_in_dim(rows, lax.axis_index("sub") * part, part, 0)
    halves = lax.all_gather(lax.all_gather(mine, "blk", axis=0), "sub", axis=1)
    full = halves.reshape(-1, rows.shape[1])
    base = jnp.dot(full, weight, preferred_element_type=F32)
    low = lax.dot_general(
        full, down.reshape(-1, down.shape[2]), (((1,), (1,)), ((), ())), preferred_element_type=F32
    )
    held = down.shape[0]
    places = lax.axis_index("blk") * held + jnp.arange(held, dtype=jnp.int32)
    here = slot_all[:, None] == places[None, :]
    low = jnp.sum(
        jnp.where(here[:, :, None], low.reshape(-1, held, width), jnp.zeros((), F32)), axis=1
    )
    low = lax.psum(lax.psum_scatter(low, "split", scatter_dimension=0, tiled=True), "blk")
    base = lax.psum_scatter(base, "split", scatter_dimension=0, tiled=True)
    start = lax.axis_index("split") * own
    spread = low_rank_weights(
        low,
        lax.dynamic_slice_in_dim(slot_all, start, own, 0),
        lax.dynamic_slice_in_dim(live_all, start, own, 0),
        slots,
        width,
    )
    ups = lax.all_gather(up, "split", axis=0, tiled=True).reshape(slots * width, cols)
    lora = jnp.dot(spread, ups, preferred_element_type=F32)
    return (residual.astype(F32) + base + lora).astype(BF16)


SWAP = [(0, 1), (1, 0)]
NEAR = [(0, 1), (1, 0), (2, 3), (3, 2)]
FAR = [(0, 2), (2, 0), (1, 3), (3, 1)]
LAST = [(0, 3), (3, 0), (1, 2), (2, 1)]


def by_core(first, second):
    return [(2 * a, 2 * b) for a, b in first] + [(2 * a + 1, 2 * b + 1) for a, b in second]


VMEM = pl.BlockSpec(memory_space=pltpu.VMEM)
SMEM = pl.BlockSpec(memory_space=pltpu.SMEM)
HBM = pl.BlockSpec(memory_space=pltpu.HBM)
COST = pl.CostEstimate(flops=0, bytes_accessed=0, transcendentals=0)
PARAMS = pltpu.CompilerParams(vmem_limit_bytes=16 * 1024 * 1024)
FROM_HBM = pltpu.CompilerParams(vmem_limit_bytes=40 * 1024 * 1024)


def shape(dims, dtype):
    return jax.ShapeDtypeStruct(dims, dtype)


def dot(a, b):
    return jnp.dot(a, b, preferred_element_type=F32)


def call(kernel, outs, in_specs, operands, scratch=(), params=PARAMS):
    return pl.pallas_call(
        kernel,
        out_shape=outs,
        in_specs=in_specs,
        out_specs=jax.tree.map(lambda _: VMEM, outs),
        scratch_shapes=scratch,
        compiler_params=params,
        cost_estimate=COST,
    )(*operands)


def column_tiles(cols):
    tile = 256 if cols % 256 == 0 else cols
    return [slice(at, at + tile) for at in range(0, cols, tile)]


def joined(flags_ref, mine, other):
    first = flags_ref[1] == 0
    return jnp.concatenate([jnp.where(first, mine, other), jnp.where(first, other, mine)])


def low_product(rows, down_ref):
    return lax.dot_general(
        rows, down_ref[...], (((1,), (1,)), ((), ())), preferred_element_type=F32
    )


def part(flags_ref, held, value, keep_ref, send_ref, tile):
    home = flags_ref[0] == 1
    keep_ref[:, tile] = jnp.where(home, held, value)
    send_ref[:, tile] = jnp.where(home, value, held).astype(BF16)


def own_kernel(
    weight_ref, down_ref, rows_ref, held_ref, sum_ref, low_ref, sems
):
    tiles = column_tiles(weight_ref.shape[1])
    copies = [
        pltpu.make_async_copy(weight_ref.at[:, tile], held_ref.at[:, tile], sems.at[i])
        for i, tile in enumerate(tiles)
    ]
    for copy in copies:
        copy.start()
    rows = rows_ref[...]
    low_ref[...] = low_product(rows, down_ref)
    for copy, tile in zip(copies, tiles):
        copy.wait()
        sum_ref[:, tile] = dot(rows, held_ref[:, tile])


def rows_of(piece, step):
    return [slice((2 * core + piece) * step, (2 * core + piece + 1) * step) for core in (0, 1)]


def in_block(first, second):
    step = first.shape[0] // 2
    return jnp.concatenate([first[:step], second[:step], first[step:], second[step:]])


def piece_kernel(
    piece, flags_ref, weight_ref, down_ref, held_ref, mine_ref, first_ref, second_ref,
    keep_ref, send_ref, low_ref,
):
    other = jnp.concatenate([first_ref[...], second_ref[...]])
    rows = joined(flags_ref, mine_ref[...], other)
    low_ref[...] = low_product(rows, down_ref)
    here = rows_of(piece, mine_ref.shape[0])
    for tile in column_tiles(weight_ref.shape[1]):
        held = jnp.concatenate([held_ref[at, tile] for at in here])
        part(flags_ref, held, dot(rows, weight_ref[:, tile]), keep_ref, send_ref, tile)


def near_kernel(
    flags_ref, weight_ref, down_ref, held_ref, mine_ref, first_ref, second_ref, near_ref,
    near_too_ref, third_ref, fourth_ref, keep_ref, send_ref, near_sum_ref, low_ref,
):
    other = jnp.concatenate([first_ref[...], second_ref[...]])
    far = joined(flags_ref, mine_ref[...], other)
    mine = jnp.concatenate([near_ref[...], near_too_ref[...]])
    other = jnp.concatenate([third_ref[...], fourth_ref[...]])
    near = joined(flags_ref, mine, other)
    rows = jnp.concatenate([near, far])
    low_ref[...] = low_product(rows, down_ref)
    here = rows_of(1, mine_ref.shape[0])
    block = near.shape[0]
    for tile in column_tiles(weight_ref.shape[1]):
        value = dot(rows, weight_ref[:, tile])
        near_sum_ref[:, tile] = value[:block]
        held = jnp.concatenate([held_ref[at, tile] for at in here])
        part(flags_ref, held, value[block:], keep_ref, send_ref, tile)


def last_kernel(
    flags_ref, weight_ref, down_ref, held_ref, own_low, low_a, low_b, low_c, mine_ref, first_ref,
    second_ref, keep_ref, send_ref, low_keep_ref, low_send_ref,
):
    other = jnp.concatenate([first_ref[...], second_ref[...]])
    rows = joined(flags_ref, mine_ref[...], other)
    low = low_product(rows, down_ref)
    block, width = own_low.shape
    odd, home = flags_ref[2] == 1, flags_ref[0] == 1
    near = own_low[...], low_b[:block]
    far = in_block(low_a[...], low_b[block:]), in_block(low_c[...], low)
    for side, here in ((0, slice(0, width)), (1, slice(width, 2 * width))):
        near_side = jnp.where(odd, near[1 - side], near[side])
        far_side = jnp.where(odd, far[1 - side], far[side])
        low_keep_ref[:, here] = jnp.where(home, near_side, far_side)
        low_send_ref[:, here] = jnp.where(home, far_side, near_side).astype(BF16)
    here = rows_of(1, mine_ref.shape[0])
    for tile in column_tiles(weight_ref.shape[1]):
        held = jnp.concatenate([held_ref[at, tile] for at in here])
        part(flags_ref, held, dot(rows, weight_ref[:, tile]), keep_ref, send_ref, tile)


def base_kernel(flags_ref, residual_ref, *refs):
    *parts, out_ref = refs
    odd = flags_ref[2] == 1
    sums = [keep[...] + got[...].astype(F32) for keep, got in zip(parts[::2], parts[1::2])]
    first, second = in_block(*sums[:2]), in_block(*sums[2:])
    block = first.shape[0]
    for at, base in ((0, jnp.where(odd, second, first)), (block, jnp.where(odd, first, second))):
        here = slice(at, at + block)
        out_ref[here, :] = residual_ref[here, :].astype(F32) + base


def final_kernel(base_ref, hot_ref, ups_ref, *refs):
    *parts, out_ref = refs
    scaled = sum(ref[...] for ref in parts)
    width = ups_ref.shape[1]
    scaled = jnp.concatenate([scaled[:, :width], scaled[:, width:]])
    lora = dot(scaled * hot_ref[0], ups_ref[0])
    for slot in range(1, ups_ref.shape[0]):
        lora += dot(scaled * hot_ref[slot], ups_ref[slot])
    out_ref[...] = (base_ref[...] + lora).astype(BF16)


def line(rows, residual, weight, down, up, tenant, entry, live):
    z, x, c = lax.axis_index("blk"), lax.axis_index("split"), lax.axis_index("sub")
    block_rows = rows.shape[0]
    width = down.shape[1]
    own, cols = residual.shape
    slots = entry.shape[0]
    home = (z // 2) == x
    odd = z % 2 == 1
    half, step = block_rows // 2, block_rows // 4
    barrier = lax.optimization_barrier

    def over_core(value):
        return lax.ppermute(value, "sub", SWAP)

    def over_x(value):
        return lax.ppermute(value, "split", SWAP)

    def along(value, pairs):
        return lax.ppermute(value, "blk", pairs)

    def over_core_in_two(piece):
        count = piece.shape[0] // 2
        return [over_core(piece[:count]), over_core(piece[count:])]

    def parted(count):
        return [shape((count, cols), F32), shape((count, cols), BF16)]

    def lows(count):
        return [shape((count, width), F32)]

    slot_all, live_all = tables(tenant, entry, live)
    slot = lax.dynamic_slice_in_dim(slot_all, x * own, own, 0)
    rank = lax.dynamic_slice_in_dim(live_all, x * own, own, 0)

    flags = jnp.stack([home, c, odd]).astype(jnp.int32)
    kept = jnp.arange(width, dtype=jnp.int32)[None, :] < rank[:, None]
    scale = jnp.where(kept, (width / rank.astype(F32))[:, None], jnp.zeros((), F32))
    scale = jnp.where((slot == z)[:, None], scale, jnp.zeros((), F32))
    scale = jnp.concatenate([scale[:block_rows], scale[block_rows:]], axis=1)
    hot = slot[None, :] == jnp.arange(slots, dtype=jnp.int32)[:, None]
    hot = jnp.broadcast_to(hot[:, :, None], (slots, own, width)).astype(BF16)

    mine = lax.dynamic_slice_in_dim(rows, c * half, step, 0)
    far, near = [along(mine, FAR)], [along(mine, NEAR)]
    offset = [(c * half + step).astype(jnp.uint32), jnp.zeros((), jnp.uint32)]
    rows, hot, scale, flags, offset, first_slots = barrier(
        (rows, hot, scale, flags, offset, x == 0)
    )
    held, own_sum, own_low = call(
        own_kernel,
        [shape(weight.shape, BF16), shape((block_rows, cols), F32)] + lows(block_rows),
        [HBM, VMEM, VMEM],
        [weight, down[0], rows],
        [pltpu.SemaphoreType.DMA((len(column_tiles(cols)),))],
        FROM_HBM,
    )
    up, rows, own_sum = barrier((up, rows, own_sum))
    mine = lax.dynamic_slice(rows, offset, (step, rows.shape[1]))
    far.append(along(mine, FAR))
    near.append(along(mine, NEAR))
    up_other = over_x(up)
    ups = jnp.where(first_slots, jnp.concatenate([up, up_other]), jnp.concatenate([up_other, up]))
    far[0], own_sum, own_low = barrier((far[0], own_sum, own_low))

    def parted_piece(piece, against, value):
        return call(
            functools.partial(piece_kernel, piece),
            parted(half) + lows(half),
            [SMEM] + [VMEM] * 6,
            [flags, held, down[0], against, value] + over_core_in_two(value),
        )

    last = [along(far[0], NEAR)]
    kept_a, sent_a, low_a = parted_piece(0, own_sum, far[0])
    got_a = over_x(sent_a)
    near, far[1], own_sum, ups, kept_a = barrier((near, far[1], own_sum, ups, kept_a))

    last.append(along(far[1], NEAR))
    kept_b, sent_b, near_sum, low_b = call(
        near_kernel,
        parted(half) + [shape((block_rows, cols), F32)] + lows(block_rows + half),
        [SMEM] + [VMEM] * 10,
        [flags, held, down[0], own_sum, far[1]] + over_core_in_two(far[1])
        + near + [over_core(piece) for piece in near],
    )
    sent_b, got_a = barrier((sent_b, got_a))
    got_b = over_x(sent_b)
    last[0], kept_b = barrier((last[0], kept_b))

    kept_c, sent_c, low_c = parted_piece(0, near_sum, last[0])
    got_c = over_x(sent_c)
    last[1], near_sum, got_b, low_c = barrier((last[1], near_sum, got_b, low_c))

    kept_d, sent_d, low, low_sent = call(
        last_kernel,
        parted(half) + [shape((block_rows, 2 * width), dtype) for dtype in (F32, BF16)],
        [SMEM] + [VMEM] * 10,
        [flags, held, down[0], near_sum, own_low, low_a, low_b, low_c, last[1]]
        + over_core_in_two(last[1]),
    )
    got_d = over_x(sent_d)

    scaled = ((low + over_x(low_sent).astype(F32)) * scale).astype(BF16)
    scaled_got = [
        lax.ppermute(scaled, ("blk", "sub"), by_core(NEAR, FAR)),
        along(scaled, LAST),
    ]
    scaled_got.append(over_core(scaled_got[0]))
    base = call(
        base_kernel,
        shape(residual.shape, F32),
        [SMEM] + [VMEM] * 9,
        [flags, residual, kept_a, got_a, kept_b, got_b, kept_c, got_c, kept_d, got_d],
    )
    return call(
        final_kernel,
        shape(residual.shape, BF16),
        [VMEM] * 7,
        [base, hot, ups, scaled] + scaled_got,
    )


def shards(rows, residual, weight, down, up, tenant, entry, live):
    sizes = [lax.axis_size(name) for name in ("blk", "split", "sub")]
    plan = line if sizes == [4, 2, 2] and down.shape[0] == 1 else general
    return plan(rows, residual, weight, down, up, tenant, entry, live)


def solution(mesh):
    in_specs = (
        P(("groups", "blk"), "split"),
        P(("groups", "split"), ("blk", "sub")),
        P("split", ("blk", "sub")),
        P("blk", None, "split"),
        P("split", None, ("blk", "sub")),
        P("groups"),
        P(),
        P(),
    )
    out_specs = P(("groups", "split"), ("blk", "sub"))
    return jax.shard_map(shards, mesh=mesh, in_specs=in_specs, out_specs=out_specs, check_vma=False)
```

```python
import functools

import jax
import jax.numpy as jnp
from jax import lax
from jax.experimental import pallas as pl
from jax.experimental.pallas import tpu as pltpu
from jax.sharding import PartitionSpec as P

F32 = jnp.float32
BF16 = jnp.bfloat16


def low_rank_weights(low, slot, live, slots, rank_width):
    kept = jnp.arange(rank_width, dtype=jnp.int32)[None, :] < live[:, None]
    scaling = rank_width / live.astype(F32)
    scaled = jnp.where(kept, low * scaling[:, None], jnp.zeros((), F32)).astype(BF16)
    hot = slot[:, None] == jnp.arange(slots, dtype=jnp.int32)[None, :]
    spread = jnp.where(hot[:, :, None], scaled[:, None, :], jnp.zeros((), BF16))
    return spread.reshape(low.shape[0], slots * rank_width)


def tables(tenant, entry, live):
    ids = jnp.arange(entry.shape[0], dtype=jnp.int32)
    hot = (tenant[:, None] == ids[None, :]).astype(jnp.int32)
    return jnp.sum(hot * entry[None, :], axis=1), jnp.sum(hot * live[None, :], axis=1)


def general(rows, residual, weight, down, up, tenant, entry, live):
    own = residual.shape[0]
    cols = weight.shape[1]
    width = down.shape[1]
    slots = entry.shape[0]
    slot_all, live_all = tables(tenant, entry, live)
    part = rows.shape[0] // lax.axis_size("sub")
    mine = lax.dynamic_slice_in_dim(rows, lax.axis_index("sub") * part, part, 0)
    halves = lax.all_gather(lax.all_gather(mine, "blk", axis=0), "sub", axis=1)
    full = halves.reshape(-1, rows.shape[1])
    base = jnp.dot(full, weight, preferred_element_type=F32)
    low = lax.dot_general(
        full, down.reshape(-1, down.shape[2]), (((1,), (1,)), ((), ())), preferred_element_type=F32
    )
    held = down.shape[0]
    places = lax.axis_index("blk") * held + jnp.arange(held, dtype=jnp.int32)
    here = slot_all[:, None] == places[None, :]
    low = jnp.sum(
        jnp.where(here[:, :, None], low.reshape(-1, held, width), jnp.zeros((), F32)), axis=1
    )
    low = lax.psum(lax.psum_scatter(low, "split", scatter_dimension=0, tiled=True), "blk")
    base = lax.psum_scatter(base, "split", scatter_dimension=0, tiled=True)
    start = lax.axis_index("split") * own
    spread = low_rank_weights(
        low,
        lax.dynamic_slice_in_dim(slot_all, start, own, 0),
        lax.dynamic_slice_in_dim(live_all, start, own, 0),
        slots,
        width,
    )
    ups = lax.all_gather(up, "split", axis=0, tiled=True).reshape(slots * width, cols)
    lora = jnp.dot(spread, ups, preferred_element_type=F32)
    return (residual.astype(F32) + base + lora).astype(BF16)


SWAP = [(0, 1), (1, 0)]
NEAR = [(0, 1), (1, 0), (2, 3), (3, 2)]
FAR = [(0, 2), (2, 0), (1, 3), (3, 1)]
LAST = [(0, 3), (3, 0), (1, 2), (2, 1)]


def by_core(first, second):
    return [(2 * a, 2 * b) for a, b in first] + [(2 * a + 1, 2 * b + 1) for a, b in second]


VMEM = pl.BlockSpec(memory_space=pltpu.VMEM)
SMEM = pl.BlockSpec(memory_space=pltpu.SMEM)
HBM = pl.BlockSpec(memory_space=pltpu.HBM)
COST = pl.CostEstimate(flops=0, bytes_accessed=0, transcendentals=0)
PARAMS = pltpu.CompilerParams(vmem_limit_bytes=16 * 1024 * 1024)
FROM_HBM = pltpu.CompilerParams(vmem_limit_bytes=40 * 1024 * 1024)


def shape(dims, dtype):
    return jax.ShapeDtypeStruct(dims, dtype)


def dot(a, b):
    return jnp.dot(a, b, preferred_element_type=F32)


def call(kernel, outs, in_specs, operands, scratch=(), params=PARAMS):
    return pl.pallas_call(
        kernel,
        out_shape=outs,
        in_specs=in_specs,
        out_specs=jax.tree.map(lambda _: VMEM, outs),
        scratch_shapes=scratch,
        compiler_params=params,
        cost_estimate=COST,
    )(*operands)


def column_tiles(cols):
    tile = 256 if cols % 256 == 0 else cols
    return [slice(at, at + tile) for at in range(0, cols, tile)]


def joined(flags_ref, mine, other):
    first = flags_ref[1] == 0
    return jnp.concatenate([jnp.where(first, mine, other), jnp.where(first, other, mine)])


def low_product(rows, down_ref):
    return lax.dot_general(
        rows, down_ref[...], (((1,), (1,)), ((), ())), preferred_element_type=F32
    )


def part(flags_ref, held, value, keep_ref, send_ref, tile):
    home = flags_ref[0] == 1
    keep_ref[:, tile] = jnp.where(home, held, value)
    send_ref[:, tile] = jnp.where(home, value, held).astype(BF16)


def own_kernel(
    weight_ref, down_ref, rows_ref, held_ref, sum_ref, low_ref, sems
):
    tiles = column_tiles(weight_ref.shape[1])
    copies = [
        pltpu.make_async_copy(weight_ref.at[:, tile], held_ref.at[:, tile], sems.at[i])
        for i, tile in enumerate(tiles)
    ]
    for copy in copies:
        copy.start()
    rows = rows_ref[...]
    low_ref[...] = low_product(rows, down_ref)
    for copy, tile in zip(copies, tiles):
        copy.wait()
        sum_ref[:, tile] = dot(rows, held_ref[:, tile])


def rows_of(piece, step):
    return [slice((2 * core + piece) * step, (2 * core + piece + 1) * step) for core in (0, 1)]


def in_block(first, second):
    step = first.shape[0] // 2
    return jnp.concatenate([first[:step], second[:step], first[step:], second[step:]])


def piece_kernel(
    piece, flags_ref, weight_ref, down_ref, held_ref, mine_ref, first_ref, second_ref,
    keep_ref, send_ref, low_ref,
):
    other = jnp.concatenate([first_ref[...], second_ref[...]])
    rows = joined(flags_ref, mine_ref[...], other)
    low_ref[...] = low_product(rows, down_ref)
    here = rows_of(piece, mine_ref.shape[0])
    for tile in column_tiles(weight_ref.shape[1]):
        held = jnp.concatenate([held_ref[at, tile] for at in here])
        part(flags_ref, held, dot(rows, weight_ref[:, tile]), keep_ref, send_ref, tile)


def near_kernel(
    flags_ref, weight_ref, down_ref, held_ref, mine_ref, first_ref, second_ref, near_ref,
    near_too_ref, third_ref, fourth_ref, keep_ref, send_ref, near_sum_ref, low_ref,
):
    other = jnp.concatenate([first_ref[...], second_ref[...]])
    far = joined(flags_ref, mine_ref[...], other)
    mine = jnp.concatenate([near_ref[...], near_too_ref[...]])
    other = jnp.concatenate([third_ref[...], fourth_ref[...]])
    near = joined(flags_ref, mine, other)
    rows = jnp.concatenate([near, far])
    low_ref[...] = low_product(rows, down_ref)
    here = rows_of(1, mine_ref.shape[0])
    block = near.shape[0]
    for tile in column_tiles(weight_ref.shape[1]):
        value = dot(rows, weight_ref[:, tile])
        near_sum_ref[:, tile] = value[:block]
        held = jnp.concatenate([held_ref[at, tile] for at in here])
        part(flags_ref, held, value[block:], keep_ref, send_ref, tile)


def last_kernel(
    flags_ref, weight_ref, down_ref, held_ref, own_low, low_a, low_b, low_c, mine_ref, first_ref,
    second_ref, keep_ref, send_ref, low_keep_ref, low_send_ref,
):
    other = jnp.concatenate([first_ref[...], second_ref[...]])
    rows = joined(flags_ref, mine_ref[...], other)
    low = low_product(rows, down_ref)
    block, width = own_low.shape
    odd, home = flags_ref[2] == 1, flags_ref[0] == 1
    near = own_low[...], low_b[:block]
    far = in_block(low_a[...], low_b[block:]), in_block(low_c[...], low)
    for side, here in ((0, slice(0, width)), (1, slice(width, 2 * width))):
        near_side = jnp.where(odd, near[1 - side], near[side])
        far_side = jnp.where(odd, far[1 - side], far[side])
        low_keep_ref[:, here] = jnp.where(home, near_side, far_side)
        low_send_ref[:, here] = jnp.where(home, far_side, near_side).astype(BF16)
    here = rows_of(1, mine_ref.shape[0])
    for tile in column_tiles(weight_ref.shape[1]):
        held = jnp.concatenate([held_ref[at, tile] for at in here])
        part(flags_ref, held, dot(rows, weight_ref[:, tile]), keep_ref, send_ref, tile)


def base_kernel(flags_ref, residual_ref, *refs):
    *parts, out_ref = refs
    odd = flags_ref[2] == 1
    sums = [keep[...] + got[...].astype(F32) for keep, got in zip(parts[::2], parts[1::2])]
    first, second = in_block(*sums[:2]), in_block(*sums[2:])
    block = first.shape[0]
    for at, base in ((0, jnp.where(odd, second, first)), (block, jnp.where(odd, first, second))):
        here = slice(at, at + block)
        out_ref[here, :] = residual_ref[here, :].astype(F32) + base


def final_kernel(base_ref, hot_ref, ups_ref, *refs):
    *parts, out_ref = refs
    scaled = sum(ref[...] for ref in parts)
    width = ups_ref.shape[1]
    scaled = jnp.concatenate([scaled[:, :width], scaled[:, width:]])
    lora = dot(scaled * hot_ref[0], ups_ref[0])
    for slot in range(1, ups_ref.shape[0]):
        lora += dot(scaled * hot_ref[slot], ups_ref[slot])
    out_ref[...] = (base_ref[...] + lora).astype(BF16)


def line(rows, residual, weight, down, up, tenant, entry, live):
    z, x, c = lax.axis_index("blk"), lax.axis_index("split"), lax.axis_index("sub")
    block_rows = rows.shape[0]
    width = down.shape[1]
    own, cols = residual.shape
    slots = entry.shape[0]
    home = (z // 2) == x
    odd = z % 2 == 1
    half, step = block_rows // 2, block_rows // 4
    barrier = lax.optimization_barrier

    def over_core(value):
        return lax.ppermute(value, "sub", SWAP)

    def over_x(value):
        return lax.ppermute(value, "split", SWAP)

    def along(value, pairs):
        return lax.ppermute(value, "blk", pairs)

    def over_core_in_two(piece):
        count = piece.shape[0] // 2
        return [over_core(piece[:count]), over_core(piece[count:])]

    def parted(count):
        return [shape((count, cols), F32), shape((count, cols), BF16)]

    def lows(count):
        return [shape((count, width), F32)]

    slot_all, live_all = tables(tenant, entry, live)
    slot = lax.dynamic_slice_in_dim(slot_all, x * own, own, 0)
    rank = lax.dynamic_slice_in_dim(live_all, x * own, own, 0)

    flags = jnp.stack([home, c, odd]).astype(jnp.int32)
    kept = jnp.arange(width, dtype=jnp.int32)[None, :] < rank[:, None]
    scale = jnp.where(kept, (width / rank.astype(F32))[:, None], jnp.zeros((), F32))
    scale = jnp.where((slot == z)[:, None], scale, jnp.zeros((), F32))
    scale = jnp.concatenate([scale[:block_rows], scale[block_rows:]], axis=1)
    hot = slot[None, :] == jnp.arange(slots, dtype=jnp.int32)[:, None]
    hot = jnp.broadcast_to(hot[:, :, None], (slots, own, width)).astype(BF16)

    mine = lax.dynamic_slice_in_dim(rows, c * half, step, 0)
    far, near = [along(mine, FAR)], [along(mine, NEAR)]
    offset = [(c * half + step).astype(jnp.uint32), jnp.zeros((), jnp.uint32)]
    rows, hot, scale, flags, offset, first_slots = barrier(
        (rows, hot, scale, flags, offset, x == 0)
    )
    held, own_sum, own_low = call(
        own_kernel,
        [shape(weight.shape, BF16), shape((block_rows, cols), F32)] + lows(block_rows),
        [HBM, VMEM, VMEM],
        [weight, down[0], rows],
        [pltpu.SemaphoreType.DMA((len(column_tiles(cols)),))],
        FROM_HBM,
    )
    up, rows, own_sum = barrier((up, rows, own_sum))
    mine = lax.dynamic_slice(rows, offset, (step, rows.shape[1]))
    far.append(along(mine, FAR))
    near.append(along(mine, NEAR))
    up_other = over_x(up)
    ups = jnp.where(first_slots, jnp.concatenate([up, up_other]), jnp.concatenate([up_other, up]))
    far[0], own_sum, own_low = barrier((far[0], own_sum, own_low))

    def parted_piece(piece, against, value):
        return call(
            functools.partial(piece_kernel, piece),
            parted(half) + lows(half),
            [SMEM] + [VMEM] * 6,
            [flags, held, down[0], against, value] + over_core_in_two(value),
        )

    last = [along(far[0], NEAR)]
    kept_a, sent_a, low_a = parted_piece(0, own_sum, far[0])
    got_a = over_x(sent_a)
    near, far[1], own_sum, ups, kept_a = barrier((near, far[1], own_sum, ups, kept_a))

    last.append(along(far[1], NEAR))
    kept_b, sent_b, near_sum, low_b = call(
        near_kernel,
        parted(half) + [shape((block_rows, cols), F32)] + lows(block_rows + half),
        [SMEM] + [VMEM] * 10,
        [flags, held, down[0], own_sum, far[1]] + over_core_in_two(far[1])
        + near + [over_core(piece) for piece in near],
    )
    last[0], kept_b = barrier((last[0], kept_b))

    kept_c, sent_c, low_c = parted_piece(0, near_sum, last[0])
    sent_b = jnp.concatenate([sent_b, sent_c])
    got_b = over_x(sent_b)
    last[1], near_sum, got_a, low_c, sent_b = barrier((last[1], near_sum, got_a, low_c, sent_b))

    kept_d, sent_d, low, low_sent = call(
        last_kernel,
        parted(half) + [shape((block_rows, 2 * width), dtype) for dtype in (F32, BF16)],
        [SMEM] + [VMEM] * 10,
        [flags, held, down[0], near_sum, own_low, low_a, low_b, low_c, last[1]]
        + over_core_in_two(last[1]),
    )
    got_d = over_x(sent_d)

    scaled = ((low + over_x(low_sent).astype(F32)) * scale).astype(BF16)
    scaled, got_b = barrier((scaled, got_b))
    got_b, got_c = got_b[:half], got_b[half:]
    scaled_got = [
        lax.ppermute(scaled, ("blk", "sub"), by_core(NEAR, FAR)),
        along(scaled, LAST),
    ]
    scaled_got.append(over_core(scaled_got[0]))
    base = call(
        base_kernel,
        shape(residual.shape, F32),
        [SMEM] + [VMEM] * 9,
        [flags, residual, kept_a, got_a, kept_b, got_b, kept_c, got_c, kept_d, got_d],
    )
    return call(
        final_kernel,
        shape(residual.shape, BF16),
        [VMEM] * 7,
        [base, hot, ups, scaled] + scaled_got,
    )


def shards(rows, residual, weight, down, up, tenant, entry, live):
    sizes = [lax.axis_size(name) for name in ("blk", "split", "sub")]
    plan = line if sizes == [4, 2, 2] and down.shape[0] == 1 else general
    return plan(rows, residual, weight, down, up, tenant, entry, live)


def solution(mesh):
    in_specs = (
        P(("groups", "blk"), "split"),
        P(("groups", "split"), ("blk", "sub")),
        P("split", ("blk", "sub")),
        P("blk", None, "split"),
        P("split", None, ("blk", "sub")),
        P("groups"),
        P(),
        P(),
    )
    out_specs = P(("groups", "split"), ("blk", "sub"))
    return jax.shard_map(shards, mesh=mesh, in_specs=in_specs, out_specs=out_specs, check_vma=False)
```
